32 devices in a mesh: ctx: 16 (over z, y, core), tp: 2 (over x).
Axes of the slice: x: 2, y: 2, z: 4, core: 2. Of those that a mesh axis runs over, the one named last changes fastest.
Arguments:
- tokens: bfloat16 [8192, 1024], P('ctx'), may hold values from -6 to 6
- cotangent: bfloat16 [8192, 1024], P('ctx'), may hold values from -6 to 6
- block_order: int32 [16], replicated, may hold values from 0 to 15, each once
- segment_ids: int32 [1, 8192], replicated, may hold values from 0 to 3, as said below
- norm_gain: bfloat16 [1024], replicated, may hold values from 0.5 to 1.5
- w_query: bfloat16 [1024, 1024], P(None, 'tp'), may hold values from -0.1875 to 0.1875
- key_weight: bfloat16 [1024, 512], P(None, 'tp'), may hold values from -0.1875 to 0.1875
- value_weight: bfloat16 [1024, 512], P(None, 'tp'), may hold values from -0.1875 to 0.1875
- query_gain: bfloat16 [64], replicated, may hold values from 0.25 to 1.75
- key_gain: bfloat16 [64], replicated, may hold values from 0.25 to 1.75
- w_out: bfloat16 [1024, 1024], P('tp'), may hold values from -3 to 3
- ffn_gain: bfloat16 [1024], replicated, may hold values from 0.5 to 1.5
- w_gate: bfloat16 [1024, 4608], P(None, 'tp'), may hold values from -0.1875 to 0.1875
- w_up: bfloat16 [1024, 4608], P(None, 'tp'), may hold values from -0.1875 to 0.1875
- w_down: bfloat16 [4608, 1024], P('tp'), may hold values from -0.09375 to 0.09375
Outputs:
- output: bfloat16 [8192, 1024], P('ctx')
- input_grad: float32 [8192, 1024], P('ctx')
- grad_norm_gain: float32 [1024], replicated
- grad_w_query: float32 [1024, 1024], P(None, 'tp')
- grad_w_key: float32 [1024, 512], P(None, 'tp')
- grad_w_value: float32 [1024, 512], P(None, 'tp')
- grad_query_gain: float32 [64], replicated
- grad_key_gain: float32 [64], replicated
- grad_w_out: float32 [1024, 1024], P('tp')
- grad_ffn_gain: float32 [1024], replicated
- grad_w_gate: float32 [1024, 4608], P(None, 'tp')
- grad_w_up: float32 [1024, 4608], P(None, 'tp')
- grad_w_down: float32 [4608, 1024], P('tp')
The draws below stay inside these ranges and needn't reach their ends.
Inputs may be any that keep to these rules, and one draw needn't show every extreme that they name: `block_order`: each index of ctx appears once. `segment_ids`: along each sequence the ids never fall; the first position has id 0 and the last id 3; document 0 covers more than the first three quarters of every sequence.
All inputs are finite; a program needn't handle non-finite values.
Results may differ from the reference program's by a relative error of at most 0.038.
Values may be sent and summed in bfloat16 or wider, within the bound.
No kernel may reach another device: no remote copies, remote signals or barrier semaphores. Data moves between devices by JAX's collectives and lax.ppermute only.
A program may use at most 576 MiB of HBM per device.

```python
import jax
import jax.numpy as jnp
from jax import lax

MODEL_WIDTH = 1024
QUERY_HEADS = 16
KEY_VALUE_HEADS = 8
HEAD_SIZE = 64
FF = 4608
TOK_DEV = 512
SEQ_LEN = 8192
SEQS = 1
BLK = 256
TOKEN_TOTAL = 8192
N_CTX = 16


def draw_segment_ids(key, part):
    key = jax.random.fold_in(key, 7)
    boundaries = jax.random.randint(key, (SEQS, 3), 3 * SEQ_LEN // 4 + 1, SEQ_LEN, dtype=jnp.int32)
    positions = jnp.arange(SEQ_LEN, dtype=jnp.int32)
    return jnp.sum((positions[None, :, None] >= boundaries[:, None, :]).astype(jnp.int32), axis=2)


def shard_levels(stream_key, shape, split, smallest, high):
    factor_of = 1.0
    for axis_at, parts in split:
        draws = jax.random.uniform(jax.random.fold_in(jax.random.fold_in(stream_key, 6), axis_at), (parts,), jnp.float32, smallest / len(split), high / len(split))
        factor_of = factor_of * jnp.repeat(jnp.exp(draws), shape[axis_at] // parts).reshape((-1,) + (1,) * (len(shape) - 1 - axis_at))
    return factor_of


def noise(rng, shape, deviation, most, pieces=(), held_as=jnp.bfloat16):
    loudness = shard_levels(rng, shape, pieces, -0.22, 0.18) if pieces else 1.0
    values = jax.random.normal(rng, shape, jnp.float32) * deviation * loudness
    return jnp.minimum(jnp.maximum(values, -most), most).astype(held_as)


def setup_inputs(seed: int = 0) -> dict:
    keys = jax.random.split(jax.random.key(seed), 16)
    tokens = noise(keys[0], (TOKEN_TOTAL, MODEL_WIDTH), 1.0, 6.0, ((0, 16),))
    cotangent = noise(keys[1], (TOKEN_TOTAL, MODEL_WIDTH), 1.0, 6.0, ((0, 16),))
    block_order = jax.random.permutation(keys[2], N_CTX).astype(jnp.int32)
    segment_ids = draw_segment_ids(jax.random.fold_in(keys[15], 71), 0)
    norm_gain = jnp.clip(1.0 + 0.1 * jax.random.normal(keys[4], (MODEL_WIDTH,), jnp.float32), 0.5, 1.5).astype(jnp.bfloat16)
    w_query = noise(keys[5], (MODEL_WIDTH, QUERY_HEADS * HEAD_SIZE), MODEL_WIDTH ** -0.5, 0.1875, ((1, 2),))
    key_weight = noise(keys[6], (MODEL_WIDTH, KEY_VALUE_HEADS * HEAD_SIZE), MODEL_WIDTH ** -0.5, 0.1875, ((1, 2),))
    value_weight = noise(keys[7], (MODEL_WIDTH, KEY_VALUE_HEADS * HEAD_SIZE), MODEL_WIDTH ** -0.5, 0.1875, ((1, 2),))
    query_gain = jnp.clip(1.0 + 0.15 * jax.random.normal(keys[8], (HEAD_SIZE,), jnp.float32), 0.25, 1.75).astype(jnp.bfloat16)
    key_gain = jnp.clip(1.0 + 0.15 * jax.random.normal(keys[9], (HEAD_SIZE,), jnp.float32), 0.25, 1.75).astype(jnp.bfloat16)
    w_out = noise(keys[10], (QUERY_HEADS * HEAD_SIZE, MODEL_WIDTH), (QUERY_HEADS * HEAD_SIZE // 256) ** -0.5, 3.0, ((0, 2),))
    ffn_gain = jnp.clip(1.0 + 0.1 * jax.random.normal(keys[11], (MODEL_WIDTH,), jnp.float32), 0.5, 1.5).astype(jnp.bfloat16)
    w_gate = noise(keys[12], (MODEL_WIDTH, FF), MODEL_WIDTH ** -0.5, 0.1875, ((1, 2),))
    w_up = noise(keys[13], (MODEL_WIDTH, FF), MODEL_WIDTH ** -0.5, 0.1875, ((1, 2),))
    w_down = noise(keys[14], (FF, MODEL_WIDTH), FF ** -0.5, 0.09375, ((0, 2),))
    return dict(tokens=tokens, cotangent=cotangent, block_order=block_order, segment_ids=segment_ids, norm_gain=norm_gain, w_query=w_query, key_weight=key_weight, value_weight=value_weight, query_gain=query_gain, key_gain=key_gain, w_out=w_out, ffn_gain=ffn_gain, w_gate=w_gate, w_up=w_up, w_down=w_down)


EPSILON = 1e-05
ROPE_BASE = 1000000.0
PRECISE = lax.Precision.HIGHEST
MASKED = -1e+30
query_block_rows = 512

@jax.custom_vjp
def low(v):
    return lax.optimization_barrier(v.astype(jnp.bfloat16)).astype(jnp.float32)

@jax.custom_vjp
def lower_precision_backward(v):
    return v

def low_keep(v):
    return (low(v), None)

def low_pass(kept, grad):
    return (grad,)

def back_keep(v):
    return (v, None)

def back_low(kept, grad):
    return (low(grad),)
low.defvjp(low_keep, low_pass)
lower_precision_backward.defvjp(back_keep, back_low)

def matrix_product(left, right):
    return jnp.dot(left, right, precision=PRECISE, preferred_element_type=jnp.float32)

def row_norm(value_rows, gain_vec):
    return value_rows * lax.rsqrt(lax.optimization_barrier(jnp.mean(value_rows * value_rows, axis=-1, keepdims=True)) + EPSILON) * gain_vec

def rotate(value_rows, cosine, sines):
    halfway = value_rows.shape[-1] // 2
    leading = value_rows[..., :halfway]
    trailing = value_rows[..., halfway:]
    return jnp.concatenate([leading * cosine - trailing * sines, trailing * cosine + leading * sines], axis=-1)

def token_places(block_order):
    row_ids = jnp.arange(TOKEN_TOTAL, dtype=jnp.int32)
    device = row_ids // TOK_DEV
    local_row = row_ids % TOK_DEV
    order_value = block_order[device]
    block_start = jnp.where(local_row // BLK % 2 == 0, order_value, 2 * N_CTX - 1 - order_value)
    return (local_row // (2 * BLK), block_start * BLK + local_row % BLK)

def by_sequence(value_rows):
    trailing = value_rows.shape[1:]
    grouped = value_rows.reshape((N_CTX, SEQS, 2 * BLK) + trailing)
    return jnp.swapaxes(grouped, 0, 1).reshape((SEQS, SEQ_LEN) + trailing)

def by_device(value_rows):
    trailing = value_rows.shape[2:]
    grouped = value_rows.reshape((SEQS, N_CTX, 2 * BLK) + trailing)
    return jnp.swapaxes(grouped, 0, 1).reshape((TOKEN_TOTAL,) + trailing)

@jax.checkpoint
def one_block(block_start, queries, key_rows_expanded, value_rows_expanded, places, segments):
    block_rows = min(query_block_rows, SEQ_LEN)
    query_block = lax.dynamic_slice_in_dim(queries, block_start, block_rows, 0)
    query_place = lax.dynamic_slice_in_dim(places, block_start, block_rows, 0)
    query_seg = lax.dynamic_slice_in_dim(segments, block_start, block_rows, 0)
    raw_scores = lower_precision_backward(jnp.einsum('qhd,khd->hqk', query_block, key_rows_expanded, precision=PRECISE) * 0.125)
    allowed = (places[None, :] <= query_place[:, None]) & (segments[None, :] == query_seg[:, None])
    scores = jnp.where(allowed[None], raw_scores, MASKED)
    peak_score = lax.optimization_barrier(jnp.max(scores, axis=-1, keepdims=True))
    weights = jnp.exp(scores - peak_score)
    probabilities = low(weights / lax.optimization_barrier(jnp.sum(weights, axis=-1, keepdims=True)))
    return jnp.einsum('hqk,khd->qhd', probabilities, value_rows_expanded, precision=PRECISE)

def attend(queries, key_rows, value_rows, places, segments):
    block_rows = min(query_block_rows, SEQ_LEN)
    key_rows_expanded = jnp.repeat(key_rows, QUERY_HEADS // KEY_VALUE_HEADS, axis=1)
    value_rows_expanded = jnp.repeat(value_rows, QUERY_HEADS // KEY_VALUE_HEADS, axis=1)
    starts = jnp.arange(SEQ_LEN // block_rows, dtype=jnp.int32) * block_rows
    blocks = lax.map(lambda block_start: one_block(block_start, queries, key_rows_expanded, value_rows_expanded, places, segments), starts)
    return blocks.reshape(SEQ_LEN, QUERY_HEADS, HEAD_SIZE)

def reference(tokens, cotangent, block_order, segment_ids, norm_gain, w_query, key_weight, value_weight, query_gain, key_gain, w_out, ffn_gain, w_gate, w_up, w_down):
    seq_ids, places = token_places(block_order)
    segments = segment_ids[seq_ids, places]
    inverse = ROPE_BASE ** (-jnp.arange(0, HEAD_SIZE, 2, dtype=jnp.float32) / HEAD_SIZE)
    angles = places.astype(jnp.float32)[:, None] * inverse[None, :]
    cosine = jnp.cos(angles)[:, None, :]
    sines = jnp.sin(angles)[:, None, :]
    place_seq = by_sequence(places)
    seg_seq = by_sequence(segments)

    def forward(inputs, first_gain, query_mat, key_matrix, value_matrix, query_gain_vec, key_gain_vec, out_mat, second_gain, gate_mat, up_mat, down_mat):
        hidden_input = low(row_norm(inputs, first_gain))
        query_raw = lower_precision_backward(matrix_product(hidden_input, query_mat)).reshape(TOKEN_TOTAL, QUERY_HEADS, HEAD_SIZE)
        key_unnormed = lower_precision_backward(matrix_product(hidden_input, key_matrix)).reshape(TOKEN_TOTAL, KEY_VALUE_HEADS, HEAD_SIZE)
        value_unnormed = lower_precision_backward(matrix_product(hidden_input, value_matrix)).reshape(TOKEN_TOTAL, KEY_VALUE_HEADS, HEAD_SIZE)
        queries = low(rotate(row_norm(query_raw, query_gain_vec), cosine, sines))
        key_rows = low(rotate(row_norm(key_unnormed, key_gain_vec), cosine, sines))
        value_rows = low(value_unnormed)
        members = (by_sequence(queries), by_sequence(key_rows), by_sequence(value_rows), place_seq, seg_seq)
        attended = lax.map(lambda member: attend(*member), members)
        attended_low = low(lower_precision_backward(by_device(attended).reshape(TOKEN_TOTAL, QUERY_HEADS * HEAD_SIZE)))
        mixed = inputs + lower_precision_backward(matrix_product(attended_low, out_mat))
        hidden_two = low(row_norm(mixed, second_gain))
        gating = lower_precision_backward(matrix_product(hidden_two, gate_mat))
        lifted = lower_precision_backward(matrix_product(hidden_two, up_mat))
        hidden_ffn = low(jax.nn.silu(gating) * lifted)
        return mixed + matrix_product(hidden_ffn, down_mat)
    floats = tuple((member.astype(jnp.float32) for member in (tokens, norm_gain, w_query, key_weight, value_weight, query_gain, key_gain, w_out, ffn_gain, w_gate, w_up, w_down)))
    result, pullback = jax.vjp(forward, *floats)
    gradients = pullback(cotangent.astype(jnp.float32))
    return (result.astype(jnp.bfloat16), gradients[0], gradients[1], gradients[2], gradients[3], gradients[4], gradients[5], gradients[6], gradients[7], gradients[8], gradients[9], gradients[10], gradients[11])
```

```python
import functools

import jax
import jax.numpy as jnp
import numpy as np
from jax import lax
from jax.experimental import pallas as pl
from jax.experimental.pallas import tpu as pltpu
from jax.sharding import PartitionSpec as P

HEAD_SIZE = 64
LANES = 2 * HEAD_SIZE
EPSILON = 1e-05
ROPE_BASE = 1000000.0
LOG2E = 1.4426950408889634
VMEM_BYTES = 56 * 2**20
f32, bf16 = jnp.float32, jnp.bfloat16
NT = (((1,), (1,)), ((), ()))


class Ring:
    def __init__(self, n_ctx):
        n = self.n = n_ctx // 2
        self.zs = 4 if n % 4 == 0 else n
        self.ys = n // self.zs
        order = [int(self.chip_at(np.int32(place))) for place in range(n)]
        self.to_right = [
            (order[i] * 2 + c, order[(i + 1) % n] * 2 + c) for i in range(n) for c in range(2)
        ]
        self.to_left = [(b, a) for a, b in self.to_right]
        self.to_sibling = [(i, i ^ 1) for i in range(n_ctx)]

    def chip_at(self, place):
        if self.ys == 1:
            return place
        where = np.where if isinstance(place, np.integer) else jnp.where
        turn = place - self.zs
        k, r = turn // (self.ys - 1), turn % (self.ys - 1)
        back = (self.zs - 1 - k) * self.ys + where(k % 2 == 0, 1 + r, self.ys - 1 - r)
        return where(place < self.zs, place * self.ys, back)

    def here(self):
        index = lax.axis_index("ctx")
        chip, core = index // 2, index % 2
        if self.ys == 1:
            return chip, core
        z, y = chip // self.ys, chip % self.ys
        k = self.zs - 1 - z
        back = self.zs + k * (self.ys - 1) + jnp.where(k % 2 == 0, y - 1, self.ys - 1 - y)
        return jnp.where(y == 0, z, back), core

    def distance(self, i):
        if isinstance(i, int):
            return -(i + 1) // 2 if i % 2 else i // 2
        return jnp.where(i % 2 == 1, -(i + 1) // 2, i // 2)

    def device_at(self, distance, other_core):
        place, core = self.here()
        return self.chip_at((place + distance + self.n) % self.n) * 2 + (core + other_core) % 2

    def right(self, x):
        return lax.ppermute(x, "ctx", self.to_right)

    def left(self, x):
        return lax.ppermute(x, "ctx", self.to_left)

    def sibling(self, x):
        return lax.ppermute(x, "ctx", self.to_sibling)


def total(*terms):
    out = terms[0].astype(f32)
    for term in terms[1:]:
        out = out + term.astype(f32)
    return out.astype(bf16)


def lower(x):
    return x[: x.shape[0] // 2]


def upper(x):
    return x[x.shape[0] // 2 :]


class RingSum:
    def __init__(self, ring):
        self.ring = ring
        self.h = ring.n // 2

    def far(self, terms):
        self.got_left = self.ring.right(total(*[lower(x) for x in terms]))
        self.got_right = self.ring.left(total(*[upper(x) for x in terms]))

    def step(self, d, terms_right, terms_left):
        if d == self.h - 1:
            a = jnp.concatenate(
                [
                    total(*[lower(x) for x in terms_right], self.got_left),
                    total(*[upper(x) for x in terms_right]),
                ]
            )
            b = jnp.concatenate(
                [
                    total(*[lower(x) for x in terms_left]),
                    total(*[upper(x) for x in terms_left], self.got_right),
                ]
            )
        else:
            a = total(*terms_right, self.got_left)
            b = total(*terms_left, self.got_right)
        self.got_left = self.ring.right(a)
        self.got_right = self.ring.left(b)
        return a, b

    def sums(self, terms):
        return total(*terms, self.got_left, self.got_right)


class RingGather:
    def __init__(self, ring, own):
        self.ring = ring
        self.parts = [own]
        self.r = self.l = own

    def step(self):
        ring = self.ring
        if len(self.parts) + 1 < ring.n:
            self.r = ring.right(self.r)
            self.l = ring.left(self.l)
            new = [self.r, self.l]
        else:
            new = [jnp.concatenate([ring.right(lower(self.r)), ring.left(upper(self.l))])]
        self.parts += new
        return new

    def all(self):
        while len(self.parts) < self.ring.n:
            self.step()
        return self.parts


def sum_over_ctx(ring, arrays):
    n = ring.n
    place, core = ring.here()
    outs = []
    for x in arrays:
        k = x.shape[0] // 2
        unit = k // n
        give = lax.dynamic_slice_in_dim(x, (1 - core) * k, k, 0)
        got = ring.sibling(give)
        keep = lax.dynamic_slice_in_dim(x, core * k, k, 0)

        def local(d):
            q = (place + d + n) % n
            return [lax.dynamic_slice_in_dim(y, q * unit, unit, 0) for y in (keep, got)]

        ring_sum = RingSum(ring)
        ring_sum.far(local(n // 2))
        for d in range(n // 2 - 1, 0, -1):
            ring_sum.step(d, local(d), local(-d))
        parts = RingGather(ring, ring_sum.sums(local(0))).all()
        out = jnp.zeros(x.shape, f32)
        for i, found in enumerate(parts):
            q = (place + ring.distance(i) + n) % n
            for c, part in ((core, found), (1 - core, ring.sibling(found))):
                out = lax.dynamic_update_slice_in_dim(
                    out, part.astype(f32), (c * n + q) * unit, 0
                )
        outs.append(out)
    return outs


def sum_over_pairs(x, axis, size):
    step = 1
    while step < size:
        x = x + lax.ppermute(x, axis, [(i, i ^ step) for i in range(size)])
        step *= 2
    return x


def sum_over_tp(x):
    size = lax.axis_size("tp")
    if size == 2:
        return x.astype(f32) + lax.ppermute(x, "tp", [(0, 1), (1, 0)]).astype(f32)
    return lax.psum(x, "tp").astype(f32)


class Tiles:
    def __init__(self, ring, first, count, seq_count, blk, order_ref, starts_ref):
        self.ring, self.first, self.slots = ring, first, 2 * count
        self.seq_count, self.blk = seq_count, blk
        self.order, self.starts = order_ref, starts_ref
        self.last = 4 * ring.n - 1
        self.rows = seq_count * (2 * self.slots + (first == 0))

    def start_of(self, seq, place):
        start = jnp.int32(0)
        for d in range(3):
            at = self.starts[seq, d]
            start = jnp.where(place >= at, at, start)
        return start

    def pair(self, row):
        seq, row = row % self.seq_count, row // self.seq_count
        slot, which = row // 2, row % 2
        if self.first == 0:
            both_high = slot == self.slots
            slot = jnp.where(both_high, 0, slot)
        mine = self.order[lax.axis_index("ctx")]
        source = self.ring.device_at(self.ring.distance(self.first + slot // 2), slot % 2)
        theirs = self.order[source]
        low = (which == 1) & (theirs <= mine)
        high = (which == 1) & (theirs > mine)
        if self.first == 0:
            low, high = low & jnp.logical_not(both_high), high | both_high
        q_place = jnp.where(low, mine, self.last - mine) * self.blk
        k_place = jnp.where(high, self.last - theirs, theirs) * self.blk
        q_tile = 2 * seq + jnp.where(low, 0, 1)
        k_tile = 2 * (self.seq_count * slot + seq) + jnp.where(high, 1, 0)
        k_end, q_end = k_place + self.blk - 1, q_place + self.blk - 1
        whole = (k_end <= q_place) & (k_place >= self.start_of(seq, q_end))
        empty = k_end < self.start_of(seq, q_place)
        kind = jnp.where(whole, 0, jnp.where(empty, 2, 1))
        return q_tile, k_tile, kind, (seq, q_place, k_place)

    def allowed(self, at, query_axis, shape):
        seq, q_place, k_place = at
        query = q_place + lax.broadcasted_iota(jnp.int32, shape, query_axis) % self.blk
        key = k_place + lax.broadcasted_iota(jnp.int32, shape, 1 - query_axis)
        return (key <= query) & (key >= self.start_of(seq, query))

    def run(self, tile):
        def body(row, carry):
            q_tile, k_tile, kind, at = self.pair(row)
            keys = pl.ds(pl.multiple_of(k_tile * self.blk, self.blk), self.blk)
            pl.when(kind == 0)(lambda: tile(q_tile, keys, None))
            pl.when(kind == 1)(lambda: tile(q_tile, keys, functools.partial(self.allowed, at)))
            return carry

        lax.fori_loop(0, self.rows, body, 0)


def forward_kernel(make, parts, heads, order_ref, starts_ref, q_ref, *refs):
    chunks, (acc_ref, out_ref, kv_ref) = refs[:parts], refs[parts:] if len(refs) == parts + 3 else (
        None,
        *refs[parts:],
    )
    tiles = make(order_ref, starts_ref)
    blk = tiles.blk
    first = lax.broadcasted_iota(jnp.int32, (blk, LANES), 1) < HEAD_SIZE
    for i, chunk in enumerate(chunks):
        kv_ref[i * chunk.shape[0] : (i + 1) * chunk.shape[0]] = chunk[...]
    out_ref[...] = jnp.zeros_like(out_ref) if acc_ref is None else acc_ref[...]

    def tile(q_tile, keys, mask):
        if mask is not None:
            allowed = mask(0, (q_ref.shape[2], blk))
        for h in range(heads):
            kv = kv_ref[keys, h * LANES : (h + 1) * LANES]
            scores = lax.dot_general(q_ref[h, q_tile], kv, NT, preferred_element_type=f32)
            weights = jnp.exp2(scores * LOG2E)
            if mask is not None:
                weights = jnp.where(allowed, weights, 0.0)
            one_v = jnp.where(first, jnp.ones_like(kv), kv)
            out_ref[h, q_tile] += jnp.dot(weights.astype(bf16), one_v, preferred_element_type=f32)

    tiles.run(tile)


def backward_kernel(
    make, parts, after, heads, order_ref, starts_ref, q_ref, do_ref, stat_ref, acc_ref, *refs
):
    chunks, refs = refs[:parts], refs[parts + after :]
    dq_ref, outs, (kv_ref, dkv_ref) = refs[0], refs[1:-2], refs[-2:]
    tiles = make(order_ref, starts_ref)
    blk = tiles.blk
    for i, chunk in enumerate(chunks):
        kv_ref[i * chunk.shape[0] : (i + 1) * chunk.shape[0]] = chunk[...]
    dq_ref[...] = acc_ref[...]
    dkv_ref[...] = jnp.zeros_like(dkv_ref)

    def tile(q_tile, keys, mask):
        if mask is not None:
            allowed = mask(1, (blk, q_ref.shape[2]))
        for h in range(heads):
            cols = slice(h * LANES, (h + 1) * LANES)
            kv = kv_ref[keys, cols]
            q = q_ref[h, q_tile]
            do = do_ref[h, q_tile]
            scores = lax.dot_general(kv, q, NT, preferred_element_type=f32)
            back_probs = lax.dot_general(kv, do, NT, preferred_element_type=f32)
            probs = jnp.exp2(scores * LOG2E - stat_ref[h, q_tile, 0:1])
            if mask is not None:
                probs = jnp.where(allowed, probs, 0.0)
            back_scores = (probs * (back_probs - stat_ref[h, q_tile, 1:2])).astype(bf16)
            both = jnp.concatenate([probs.astype(bf16), back_scores], axis=1)
            dkv_ref[keys, cols] += jnp.dot(
                both, jnp.concatenate([do, q], axis=0), preferred_element_type=f32
            )
            dq_ref[h, q_tile] += jnp.dot(kv.T[:HEAD_SIZE], back_scores, preferred_element_type=f32)

    tiles.run(tile)
    for i, out in enumerate(outs):
        out[...] = dkv_ref[i * out.shape[0] : (i + 1) * out.shape[0]].astype(out.dtype)


def in_smem():
    return pl.BlockSpec(memory_space=pltpu.SMEM)


def in_vmem():
    return pl.BlockSpec(memory_space=pltpu.VMEM)


def anywhere():
    return pl.BlockSpec(memory_space=pl.ANY)


class Attention:
    def __init__(self, ring, block_order, starts, blk):
        self.ring, self.order, self.starts = ring, block_order, starts
        self.blk, self.seq_count = blk, starts.shape[0]

    def _make(self, first, count):
        return lambda order_ref, starts_ref: Tiles(
            self.ring, first, count, self.seq_count, self.blk, order_ref, starts_ref
        )

    def _cost(self, first, count, heads, products, arrays):
        rows = self.seq_count * (4 * count + (first == 0))
        tile = 2 * self.blk * self.blk * heads * rows
        return pl.CostEstimate(
            flops=2 * tile * 256 * products,
            bytes_accessed=sum(x.size * x.dtype.itemsize for x in arrays),
            transcendentals=tile,
        )

    def forward(self, first, chunks, q, acc):
        heads, tiles, rows, _ = q.shape
        out = jax.ShapeDtypeStruct((heads, tiles, rows, LANES), f32)
        count = len(chunks) // 2
        held = [] if acc is None else [acc]
        keys, width = len(chunks) * chunks[0].shape[0], chunks[0].shape[1]
        return pl.pallas_call(
            functools.partial(forward_kernel, self._make(first, count), len(chunks), heads),
            out_shape=out,
            in_specs=[in_smem()] * 2 + [in_vmem()] * (1 + len(chunks) + len(held)),
            out_specs=in_vmem(),
            scratch_shapes=[pltpu.VMEM((keys, width), bf16)],
            compiler_params=pltpu.CompilerParams(vmem_limit_bytes=VMEM_BYTES),
            cost_estimate=self._cost(first, count, heads, 2, [q, *chunks, out, out]),
            name="attend_forward",
        )(self.order, self.starts, q, *chunks, *held)

    def backward(self, first, chunks, q, do, stats, acc, after):
        heads, tiles, rows, _ = q.shape
        count = len(chunks) // 2
        keys, width = len(chunks) * chunks[0].shape[0], chunks[0].shape[1]
        outs = [jax.ShapeDtypeStruct(acc.shape, f32)] + [
            jax.ShapeDtypeStruct(x.shape, bf16 if i % 2 else f32) for i, x in enumerate(chunks)
        ]
        dq, *grads = pl.pallas_call(
            functools.partial(
                backward_kernel, self._make(first, count), len(chunks), len(after), heads
            ),
            out_shape=outs,
            in_specs=[in_smem()] * 2
            + [in_vmem()] * (4 + len(chunks))
            + [anywhere()] * len(after),
            out_specs=[in_vmem()] * len(outs),
            scratch_shapes=[pltpu.VMEM((keys, width), bf16), pltpu.VMEM((keys, width), f32)],
            compiler_params=pltpu.CompilerParams(vmem_limit_bytes=VMEM_BYTES),
            cost_estimate=self._cost(first, count, heads, 5, [q, do, acc, *chunks, *outs]),
            name="attend_backward",
        )(self.order, self.starts, q, do, stats, acc, *chunks, *after)
        return dq, grads


def grads_kernel(ring, two_ref, gate_ref, up_ref, ffn_ref, cot_ref, keep_ref, give_ref, lhs_ref):
    _, core = ring.here()

    @pl.when(pl.program_id(0) == 0)
    def _():
        lhs_ref[...] = two_ref[...].T

    n = ring.n
    unit = lhs_ref.shape[0] // (2 * n)
    cols = gate_ref.shape[1]
    thin = cols // (2 * n)

    def store(at, value):
        rows = pl.ds(at, value.shape[1])

        @pl.when(core == 0)
        def _():
            keep_ref[:, rows] = value[:n]
            give_ref[:, rows] = value[n:]

        @pl.when(core == 1)
        def _():
            keep_ref[:, rows] = value[n:]
            give_ref[:, rows] = value[:n]

    for i, ref in enumerate((gate_ref, up_ref)):
        grad = jnp.dot(lhs_ref[...], ref[...], preferred_element_type=f32).astype(bf16)
        store(i * unit, grad.reshape(2 * n, unit, cols))
    down = jnp.dot(ffn_ref[...].T, cot_ref[...], preferred_element_type=f32).astype(bf16)
    down = down.reshape(2 * n, thin, down.shape[1])
    for q in range(down.shape[2] // cols):
        store(2 * unit + q * thin, down[:, :, q * cols : (q + 1) * cols])


def ffn_grads(ring, hidden_two, back_gate, back_up, hidden_ffn, cotangent):
    rows, width = hidden_two.shape
    units = back_gate.shape[1]
    n = ring.n
    wide = width // (2 * n) * 3
    cols = 256
    out = jax.ShapeDtypeStruct((n, wide, units), bf16)
    whole = pl.BlockSpec((rows, width), lambda j: (0, 0))
    block = pl.BlockSpec((rows, cols), lambda j: (0, j))
    cut = pl.BlockSpec((n, wide, cols), lambda j: (0, 0, j))
    return pl.pallas_call(
        functools.partial(grads_kernel, ring),
        grid=(units // cols,),
        out_shape=(out, out),
        in_specs=[whole, block, block, block, whole],
        out_specs=(cut, cut),
        scratch_shapes=[pltpu.VMEM((width, rows), bf16)],
        compiler_params=pltpu.CompilerParams(vmem_limit_bytes=VMEM_BYTES),
        cost_estimate=pl.CostEstimate(
            flops=6 * rows * width * units, bytes_accessed=20 * 2**20, transcendentals=0
        ),
        name="ffn_grads",
    )(hidden_two, back_gate, back_up, hidden_ffn, cotangent)


def place_kernel(ring, *refs):
    parts, (gate_ref, up_ref, down_ref) = refs[:-3], refs[-3:]
    place, core = ring.here()
    n = ring.n
    cols = gate_ref.shape[1]
    unit = gate_ref.shape[0] // (2 * n)
    thin = cols // (2 * n)
    for i, part in enumerate(parts):
        d = ring.distance(i // 2)
        q = (place + d + n) % n
        r = (core + i % 2) % 2 * n + q
        rows = pl.ds(pl.multiple_of(r * unit, unit), unit)
        gate_ref[rows] = part[:unit].astype(f32)
        up_ref[rows] = part[unit : 2 * unit].astype(f32)
        rows = pl.ds(pl.multiple_of(r * thin, thin), thin)
        for k in range(down_ref.shape[1] // cols):
            at = 2 * unit + k * thin
            down_ref[rows, k * cols : (k + 1) * cols] = part[at : at + thin].astype(f32)


def place_ffn(ring, parts, width):
    wide, units = parts[0].shape
    cols = 256
    return pl.pallas_call(
        functools.partial(place_kernel, ring),
        grid=(units // cols,),
        out_shape=(
            jax.ShapeDtypeStruct((width, units), f32),
            jax.ShapeDtypeStruct((width, units), f32),
            jax.ShapeDtypeStruct((units, width), f32),
        ),
        in_specs=[pl.BlockSpec((wide, cols), lambda j: (0, j))] * len(parts),
        out_specs=(
            pl.BlockSpec((width, cols), lambda j: (0, j)),
            pl.BlockSpec((width, cols), lambda j: (0, j)),
            pl.BlockSpec((cols, width), lambda j: (j, 0)),
        ),
        compiler_params=pltpu.CompilerParams(vmem_limit_bytes=VMEM_BYTES),
        cost_estimate=pl.CostEstimate(
            flops=0, bytes_accessed=18 * width * units, transcendentals=0
        ),
        name="place_ffn",
    )(*parts)


def row_norm(value_rows, gain_vec):
    factor = lax.rsqrt(jnp.mean(value_rows * value_rows, axis=-1, keepdims=True) + EPSILON)
    return (value_rows * factor * gain_vec, factor)


def norm_back(upstream, value_rows, factor, gain_vec):
    inner_grad = upstream * gain_vec
    return factor * (
        inner_grad
        - value_rows * factor * factor * jnp.mean(inner_grad * value_rows, axis=-1, keepdims=True)
    )


def rotate(value_rows, cosine, sines):
    halfway = value_rows.shape[-1] // 2
    leading = value_rows[..., :halfway]
    trailing = value_rows[..., halfway:]
    return jnp.concatenate(
        [leading * cosine - trailing * sines, trailing * cosine + leading * sines], axis=-1
    )


def rotate_back(upstream, cosine, sines):
    return rotate(upstream, cosine, -sines)


def dot(a, b, dims):
    return lax.dot_general(a, b, ((dims[:1], dims[1:]), ((), ())), preferred_element_type=f32)


def on_device(
    tokens,
    cotangent,
    block_order,
    segment_ids,
    norm_gain,
    w_query,
    key_weight,
    value_weight,
    query_gain,
    key_gain,
    w_out,
    ffn_gain,
    w_gate,
    w_up,
    w_down,
):
    devices = lax.axis_size("ctx")
    ring = Ring(devices)
    ring_place, _ = ring.here()
    rows, width = tokens.shape
    seq_count = segment_ids.shape[0]
    blk = rows // seq_count // 2
    tiles = 2 * seq_count
    kv_heads = key_weight.shape[1] // HEAD_SIZE
    query_heads = w_query.shape[1] // HEAD_SIZE
    group = query_heads // kv_heads

    order = block_order[lax.axis_index("ctx")]
    blocks = jnp.stack([order, 2 * devices - 1 - order] * seq_count)
    place = (blocks[:, None] * blk + jnp.arange(blk, dtype=jnp.int32)[None, :]).reshape(rows)
    starts = jnp.stack([jnp.sum((segment_ids < d).astype(jnp.int32), axis=1) for d in (1, 2, 3)], 1)
    inverse = ROPE_BASE ** (-jnp.arange(0, HEAD_SIZE, 2, dtype=f32) / HEAD_SIZE)
    angles = place.astype(f32)[:, None] * inverse[None, :]
    cosine = jnp.cos(angles)[:, None, :]
    sines = jnp.sin(angles)[:, None, :]

    inputs = tokens.astype(f32)
    normed, scale_one = row_norm(inputs, norm_gain)
    hidden_input = normed.astype(bf16)
    query_raw = dot(hidden_input, w_query, (1, 0)).reshape(rows, query_heads, HEAD_SIZE)
    key_raw = dot(hidden_input, key_weight, (1, 0)).reshape(rows, kv_heads, HEAD_SIZE)
    value_rows = dot(hidden_input, value_weight, (1, 0)).astype(bf16)
    query_norm, query_scale = row_norm(query_raw, query_gain)
    key_norm, key_scale = row_norm(key_raw, key_gain)
    queries = rotate(query_norm, cosine, sines).astype(bf16)
    key_rows = rotate(key_norm, cosine, sines).astype(bf16)
    own_kv = jnp.concatenate(
        [key_rows, value_rows.reshape(rows, kv_heads, HEAD_SIZE)], axis=2
    ).reshape(rows, kv_heads * LANES)

    def by_tile(x):
        x = x.reshape(tiles, blk, kv_heads, group, HEAD_SIZE)
        return x.transpose(2, 0, 3, 1, 4).reshape(kv_heads, tiles, group * blk, HEAD_SIZE)

    def by_row(x):
        x = x.reshape(kv_heads, tiles, group, blk, HEAD_SIZE)
        return x.transpose(1, 3, 0, 2, 4).reshape(rows, query_heads, HEAD_SIZE)

    q_tiles = by_tile(queries * jnp.asarray(0.125, bf16))
    q_tiles = jnp.concatenate([q_tiles, jnp.zeros_like(q_tiles)], axis=3)

    attention = Attention(ring, block_order, starts, blk)
    gather = RingGather(ring, own_kv)
    chunks = [own_kv, ring.sibling(own_kv)]
    acc = None
    first = 0
    stages = []
    while True:
        stages.append((first, chunks))
        acc = attention.forward(first, chunks, q_tiles, acc)
        first += len(chunks) // 2
        if first == ring.n:
            break
        chunks = [y for x in gather.step() for y in (x, ring.sibling(x))]
    sums = acc[..., :1]
    attended = acc[..., HEAD_SIZE:] / sums
    attended_low = by_row(attended).reshape(rows, query_heads * HEAD_SIZE).astype(bf16)

    mixed = inputs + sum_over_tp(dot(attended_low, w_out, (1, 0)).astype(bf16))
    normed_two, scale_two = row_norm(mixed, ffn_gain)
    hidden_two = normed_two.astype(bf16)

    gating = dot(hidden_two, w_gate, (1, 0))
    lifted = dot(hidden_two, w_up, (1, 0))
    logistic = jax.nn.sigmoid(gating)
    silu = gating * logistic
    hidden_ffn = (silu * lifted).astype(bf16)
    back_hidden = dot(cotangent, w_down, (1, 1))
    back_gate = (back_hidden * lifted * logistic * (1.0 + gating * (1.0 - logistic))).astype(bf16)
    back_up = (back_hidden * silu).astype(bf16)
    back_part = dot(back_gate, w_gate, (1, 1)) + dot(back_up, w_up, (1, 1))
    back_two = sum_over_tp(back_part.astype(bf16))
    output = (mixed + sum_over_tp(dot(hidden_ffn, w_down, (1, 0)).astype(bf16))).astype(bf16)
    packed = back_gate.shape[1] % 256 == 0 and width % (32 * ring.n) == 0
    if packed:
        keep, give = ffn_grads(ring, hidden_two, back_gate, back_up, hidden_ffn, cotangent)
        got = ring.sibling(give)

        def ffn_terms(d):
            q = (ring_place + d + ring.n) % ring.n
            return [lax.dynamic_index_in_dim(y, q, 0, keepdims=False) for y in (keep, got)]

        ffn_sum = RingSum(ring)
        ffn_sum.far(ffn_terms(ring.n // 2))
    else:
        grad_w_down = dot(hidden_ffn, cotangent, (0, 0)).astype(bf16)
        grad_w_gate = dot(hidden_two, back_gate, (0, 0)).astype(bf16)
        grad_w_up = dot(hidden_two, back_up, (0, 0)).astype(bf16)
        grad_w_gate, grad_w_up, grad_w_down = sum_over_ctx(
            ring, [grad_w_gate, grad_w_up, grad_w_down]
        )

    grad_ffn_gain = jnp.sum(back_two * mixed * scale_two, axis=0)
    back_mixed = cotangent.astype(f32) + norm_back(back_two, mixed, scale_two, ffn_gain)
    back_proj = back_mixed.astype(bf16)
    grad_w_out = dot(attended_low, back_proj, (0, 0)).astype(bf16)
    back_attn = dot(back_proj, w_out, (1, 1)).astype(bf16)

    do_tiles = by_tile(back_attn)
    delta = jnp.sum(do_tiles.astype(f32) * attended, axis=-1)
    do_tiles = jnp.concatenate([jnp.zeros_like(do_tiles), do_tiles], axis=3)
    stats = jnp.stack([jnp.log2(sums[..., 0]), delta], axis=2)
    dq = jnp.zeros((kv_heads, tiles, HEAD_SIZE, group * blk), f32)
    dkv_sum = RingSum(ring)
    waiting = None
    after = []
    d = ring.n // 2
    for first, chunks in reversed(stages):
        if waiting is not None:
            after = []
            if waiting[0] == ring.n // 2:
                dkv_sum.far(waiting[1][0])
            else:
                after += dkv_sum.step(waiting[0], waiting[1][1], waiting[1][0])
        if packed and 0 < d < ring.n // 2:
            after += ffn_sum.step(d, ffn_terms(d), ffn_terms(-d))
        dq, grads = attention.backward(first, chunks, q_tiles, do_tiles, stats, dq, after)
        waiting = d, [(a, ring.sibling(b)) for a, b in zip(grads[::2], grads[1::2])]
        d -= 1
    own_dkv = dkv_sum.sums(waiting[1][0])
    if packed:
        ffn_parts = RingGather(ring, ffn_sum.sums(ffn_terms(0))).all()
        ffn_parts = [y for x in ffn_parts for y in (x, ring.sibling(x))]
        grad_w_gate, grad_w_up, grad_w_down = place_ffn(ring, ffn_parts, width)

    own_dkv = own_dkv.astype(f32).reshape(rows, kv_heads, LANES)

    back_query = by_row(dq.transpose(0, 1, 3, 2)) * 0.125
    turned_query = rotate_back(back_query, cosine, sines)
    grad_query_gain = jnp.sum(turned_query * query_raw * query_scale, axis=(0, 1))
    query_delta = (
        norm_back(turned_query, query_raw, query_scale, query_gain).reshape(rows, -1).astype(bf16)
    )
    turned_key = rotate_back(own_dkv[..., :HEAD_SIZE], cosine, sines)
    grad_key_gain = jnp.sum(turned_key * key_raw * key_scale, axis=(0, 1))
    key_delta = norm_back(turned_key, key_raw, key_scale, key_gain).reshape(rows, -1).astype(bf16)
    value_delta = own_dkv[..., HEAD_SIZE:].reshape(rows, -1).astype(bf16)
    deltas = jnp.concatenate([query_delta, key_delta, value_delta], axis=1)
    weights = jnp.concatenate([w_query, key_weight, value_weight], axis=1)
    back_one = sum_over_tp(dot(deltas, weights, (1, 1)).astype(bf16))
    grad_qkv = dot(hidden_input, deltas, (0, 0)).astype(bf16)
    grad_qkv, grad_w_out = sum_over_ctx(ring, [grad_qkv, grad_w_out])
    q_cols, k_cols = w_query.shape[1], key_weight.shape[1]
    grad_w_query = grad_qkv[:, :q_cols]
    grad_w_key = grad_qkv[:, q_cols : q_cols + k_cols]
    grad_w_value = grad_qkv[:, q_cols + k_cols :]

    grad_norm_gain = jnp.sum(back_one * inputs * scale_one, axis=0)
    input_grad = back_mixed + norm_back(back_one, inputs, scale_one, norm_gain)

    head_gains = sum_over_pairs(
        jnp.concatenate([grad_query_gain, grad_key_gain]), "tp", lax.axis_size("tp")
    )
    gains = sum_over_pairs(
        jnp.concatenate([grad_norm_gain, grad_ffn_gain, head_gains]), "ctx", devices
    )
    return (
        output,
        input_grad,
        gains[:width],
        grad_w_query,
        grad_w_key,
        grad_w_value,
        gains[2 * width : 2 * width + HEAD_SIZE],
        gains[2 * width + HEAD_SIZE :],
        grad_w_out,
        gains[width : 2 * width],
        grad_w_gate,
        grad_w_up,
        grad_w_down,
    )


def solution(mesh):
    return jax.shard_map(
        on_device,
        mesh=mesh,
        in_specs=(
            P("ctx", None),
            P("ctx", None),
            P(),
            P(),
            P(),
            P(None, "tp"),
            P(None, "tp"),
            P(None, "tp"),
            P(),
            P(),
            P("tp", None),
            P(),
            P(None, "tp"),
            P(None, "tp"),
            P("tp", None),
        ),
        out_specs=(
            P("ctx", None),
            P("ctx", None),
            P(),
            P(None, "tp"),
            P(None, "tp"),
            P(None, "tp"),
            P(),
            P(),
            P("tp", None),
            P(),
            P(None, "tp"),
            P(None, "tp"),
            P("tp", None),
        ),
        check_vma=False,
    )
```

```python
import functools

import jax
import jax.numpy as jnp
import numpy as np
from jax import lax
from jax.experimental import pallas as pl
from jax.experimental.pallas import tpu as pltpu
from jax.sharding import PartitionSpec as P

HEAD_SIZE = 64
LANES = 2 * HEAD_SIZE
EPSILON = 1e-05
ROPE_BASE = 1000000.0
LOG2E = 1.4426950408889634
VMEM_BYTES = 56 * 2**20
COST_SCALE = 16
f32, bf16 = jnp.float32, jnp.bfloat16
NT = (((1,), (1,)), ((), ()))


class Ring:
    def __init__(self, n_ctx):
        n = self.n = n_ctx // 2
        self.zs = 4 if n % 4 == 0 else n
        self.ys = n // self.zs
        order = [int(self.chip_at(np.int32(place))) for place in range(n)]
        self.to_right = [
            (order[i] * 2 + c, order[(i + 1) % n] * 2 + c) for i in range(n) for c in range(2)
        ]
        self.to_left = [(b, a) for a, b in self.to_right]
        self.to_sibling = [(i, i ^ 1) for i in range(n_ctx)]

    def chip_at(self, place):
        if self.ys == 1:
            return place
        where = np.where if isinstance(place, np.integer) else jnp.where
        turn = place - self.zs
        k, r = turn // (self.ys - 1), turn % (self.ys - 1)
        back = (self.zs - 1 - k) * self.ys + where(k % 2 == 0, 1 + r, self.ys - 1 - r)
        return where(place < self.zs, place * self.ys, back)

    def here(self):
        index = lax.axis_index("ctx")
        chip, core = index // 2, index % 2
        if self.ys == 1:
            return chip, core
        z, y = chip // self.ys, chip % self.ys
        k = self.zs - 1 - z
        back = self.zs + k * (self.ys - 1) + jnp.where(k % 2 == 0, y - 1, self.ys - 1 - y)
        return jnp.where(y == 0, z, back), core

    def distances(self):
        h = self.n // 2
        return [0] + [s * d for d in range(1, h) for s in (-1, 1)] + [h]

    def device_at(self, distance, other_core):
        place, core = self.here()
        return self.chip_at((place + distance + self.n) % self.n) * 2 + (core + other_core) % 2

    def right(self, x):
        return lax.ppermute(x, "ctx", self.to_right)

    def left(self, x):
        return lax.ppermute(x, "ctx", self.to_left)

    def sibling(self, x):
        return lax.ppermute(x, "ctx", self.to_sibling)


def total(*terms):
    out = terms[0].astype(f32)
    for term in terms[1:]:
        out = out + term.astype(f32)
    return out.astype(bf16)


def lower(x):
    return x[: x.shape[0] // 2]


def upper(x):
    return x[x.shape[0] // 2 :]


class RingSum:
    def __init__(self, ring):
        self.ring = ring
        self.h = ring.n // 2

    def sends(self, d, right, left):
        if d == self.h:
            return [total(*[lower(x) for x in right]), total(*[upper(x) for x in right])]
        if d == self.h - 1:
            right_parts = [
                total(*[lower(x) for x in right], self.got[0]),
                total(*[upper(x) for x in right]),
            ]
            left_parts = [
                total(*[lower(x) for x in left]),
                total(*[upper(x) for x in left], self.got[1]),
            ]
            return [jnp.concatenate(right_parts), jnp.concatenate(left_parts)]
        return [total(*right, self.got[0]), total(*left, self.got[1])]

    def send(self, arrays):
        self.got = [self.ring.right(arrays[0]), self.ring.left(arrays[1])]

    def sums(self, terms):
        return total(*terms, *self.got)


class RingGather:
    def __init__(self, ring, own):
        self.ring = ring
        self.parts, self.siblings = [own], [ring.sibling(own)]
        self.new = [own, own]

    def sends(self):
        if len(self.parts) + 1 < self.ring.n:
            return self.new
        return [lower(self.new[0]), upper(self.new[1])]

    def send(self, arrays):
        ring = self.ring
        self.new = [ring.right(arrays[0]), ring.left(arrays[1])]
        if len(self.parts) + 1 == ring.n:
            self.new = [jnp.concatenate(self.new)]
        self.parts += self.new
        self.siblings += [ring.sibling(x) for x in self.new]

    def done(self):
        return len(self.parts) == self.ring.n

    def everything(self):
        return [y for pair in zip(self.parts, self.siblings) for y in pair]


def sum_steps(ring, terms):
    ring_sum = RingSum(ring)
    for d in range(ring.n // 2, 0, -1):
        ring_sum.send((yield ring_sum.sends(d, terms(d), terms(-d) if d < ring.n // 2 else None), []))
    gather = RingGather(ring, ring_sum.sums(terms(0)))
    before = 0
    while not gather.done():
        late = gather.siblings[:before]
        before = len(gather.siblings)
        gather.send((yield gather.sends(), late))
    return gather


class Steps:
    def __init__(self, generator):
        self.generator, self.result, self.started = generator, None, False
        self.back = None

    def sends(self):
        try:
            self.arrays, self.late = self.generator.send(self.back)
        except StopIteration as stop:
            self.arrays, self.late, self.result, self.generator = [], [], stop.value, None
        return self.arrays, self.late


def advance(steps, *others):
    steps = [x for x in steps if x is not None and x.generator is not None]
    ready = [x.sends() for x in steps]
    arrays = [y for sends, _ in ready for y in sends]
    late = [y for _, more in ready for y in more]
    tied = lax.optimization_barrier((*arrays, *late, *others))
    at = 0
    for x, (sends, _) in zip(steps, ready):
        x.back = list(tied[at : at + len(sends)])
        at += len(sends)
    return tied[at + len(late) :]


def ring_sum_parts(ring, x):
    steps = Steps(sum_steps(ring, row_terms(ring, x)))
    while steps.generator is not None:
        advance([steps])
    return steps.result.everything()


def row_terms(ring, x):
    n = ring.n
    place, core = ring.here()
    half = x.shape[0] // 2
    unit = half // n
    keep = lax.dynamic_slice_in_dim(x, core * half, half, 0)
    got = ring.sibling(lax.dynamic_slice_in_dim(x, (1 - core) * half, half, 0))

    def terms(d):
        q = (place + d + n) % n
        return [lax.dynamic_slice_in_dim(y, q * unit, unit, 0) for y in (keep, got)]

    return terms


def sum_over_ctx(ring, arrays):
    n = ring.n
    place, core = ring.here()
    outs = []
    for x in arrays:
        unit = x.shape[0] // (2 * n)
        out = jnp.zeros(x.shape, f32)
        for i, part in enumerate(ring_sum_parts(ring, x)):
            q = (place + ring.distances()[i // 2] + n) % n
            row = ((core + i % 2) % 2 * n + q) * unit
            out = lax.dynamic_update_slice_in_dim(out, part.astype(f32), row, 0)
        outs.append(out)
    return outs


def pair_steps(x, axes):
    for axis, size in axes:
        step = 1
        while step < size:
            (y,) = yield [x], []
            x = y + lax.ppermute(y, axis, [(i, i ^ step) for i in range(size)])
            step *= 2
    return x


def from_other(xs):
    return [lax.ppermute(x, "tp", [(0, 1), (1, 0)]) for x in xs]


def sum_over_tp(x):
    size = lax.axis_size("tp")
    if size == 2:
        return x.astype(f32) + lax.ppermute(x, "tp", [(0, 1), (1, 0)]).astype(f32)
    return lax.psum(x, "tp").astype(f32)


def pair_count(slots, seq_count):
    return seq_count * (2 * len(slots) + ((0, 0) in slots))


class Tiles:
    def __init__(self, ring, slots, seq_count, blk, order_ref, starts_ref):
        self.ring, self.slots = ring, slots
        self.seq_count, self.blk = seq_count, blk
        self.order, self.starts = order_ref, starts_ref
        self.last = 4 * ring.n - 1
        self.rows = pair_count(slots, seq_count)

    def start_of(self, seq, place):
        start = jnp.int32(0)
        for d in range(3):
            at = self.starts[seq, d]
            start = jnp.where(place >= at, at, start)
        return start

    def pair(self, row):
        seq, row = row % self.seq_count, row // self.seq_count
        slot, which = row // 2, row % 2
        own = self.slots.index((0, 0)) if (0, 0) in self.slots else None
        if own is not None:
            both_high = slot == len(self.slots)
            slot = jnp.where(both_high, own, slot)
        distance, other = self.slots[0]
        for i, (d, c) in enumerate(self.slots):
            distance, other = jnp.where(slot == i, d, distance), jnp.where(slot == i, c, other)
        mine = self.order[lax.axis_index("ctx")]
        theirs = self.order[self.ring.device_at(distance, other)]
        low = (which == 1) & (theirs <= mine)
        high = (which == 1) & (theirs > mine)
        if own is not None:
            low, high = low & jnp.logical_not(both_high), high | both_high
        q_place = jnp.where(low, mine, self.last - mine) * self.blk
        k_place = jnp.where(high, self.last - theirs, theirs) * self.blk
        q_tile = 2 * seq + jnp.where(low, 0, 1)
        k_tile = 2 * (self.seq_count * slot + seq) + jnp.where(high, 1, 0)
        k_end, q_end = k_place + self.blk - 1, q_place + self.blk - 1
        whole = (k_end <= q_place) & (k_place >= self.start_of(seq, q_end))
        empty = k_end < self.start_of(seq, q_place)
        kind = jnp.where(whole, 0, jnp.where(empty, 2, 1))
        return q_tile, k_tile, kind, (seq, q_place, k_place)

    def allowed(self, at, query_axis, shape):
        seq, q_place, k_place = at
        query = q_place + lax.broadcasted_iota(jnp.int32, shape, query_axis) % self.blk
        key = k_place + lax.broadcasted_iota(jnp.int32, shape, 1 - query_axis)
        return (key <= query) & (key >= self.start_of(seq, query))

    def run(self, tile):
        def body(row, carry):
            q_tile, k_tile, kind, at = self.pair(row)
            keys = pl.ds(pl.multiple_of(k_tile * self.blk, self.blk), self.blk)
            pl.when(kind == 0)(lambda: tile(q_tile, keys, None))
            pl.when(kind == 1)(lambda: tile(q_tile, keys, functools.partial(self.allowed, at)))
            return carry

        lax.fori_loop(0, self.rows, body, 0)


def forward_kernel(make, parts, heads, order_ref, starts_ref, q_ref, *refs):
    chunks, held, (out_ref, kv_ref) = refs[:parts], refs[parts:-2], refs[-2:]
    tiles = make(order_ref, starts_ref)
    blk = tiles.blk
    first = lax.broadcasted_iota(jnp.int32, (blk, LANES), 1) < HEAD_SIZE
    for i, chunk in enumerate(chunks):
        kv_ref[i * chunk.shape[0] : (i + 1) * chunk.shape[0]] = chunk[...]
    out_ref[...] = held[0][...] if held else jnp.zeros_like(out_ref)

    def tile(q_tile, keys, mask):
        if mask is not None:
            allowed = mask(0, (q_ref.shape[2], blk))
        for h in range(heads):
            kv = kv_ref[keys, h * LANES : (h + 1) * LANES]
            scores = lax.dot_general(q_ref[h, q_tile], kv, NT, preferred_element_type=f32)
            weights = jnp.exp2(scores * LOG2E)
            if mask is not None:
                weights = jnp.where(allowed, weights, 0.0)
            one_v = jnp.where(first, jnp.ones_like(kv), kv)
            out_ref[h, q_tile] += jnp.dot(weights.astype(bf16), one_v, preferred_element_type=f32)

    tiles.run(tile)


def backward_kernel(make, parts, held, heads, order_ref, starts_ref, q_ref, do_ref, stat_ref, *refs):
    chunks, held, refs = refs[:parts], refs[parts : parts + held], refs[parts + held :]
    dq_ref, outs, (kv_ref, dkv_ref) = refs[0], refs[1:-2], refs[-2:]
    tiles = make(order_ref, starts_ref)
    blk = tiles.blk
    for i, chunk in enumerate(chunks):
        kv_ref[i * chunk.shape[0] : (i + 1) * chunk.shape[0]] = chunk[...]
    dq_ref[...] = held[0][...] if held else jnp.zeros_like(dq_ref)
    dkv_ref[...] = jnp.zeros_like(dkv_ref)

    def tile(q_tile, keys, mask):
        if mask is not None:
            allowed = mask(1, (blk, q_ref.shape[2]))
        for h in range(heads):
            cols = slice(h * LANES, (h + 1) * LANES)
            kv = kv_ref[keys, cols]
            q = q_ref[h, q_tile]
            do = do_ref[h, q_tile]
            scores = lax.dot_general(kv, q, NT, preferred_element_type=f32)
            back_probs = lax.dot_general(kv, do, NT, preferred_element_type=f32)
            probs = jnp.exp2(scores * LOG2E - stat_ref[h, q_tile, 0:1])
            if mask is not None:
                probs = jnp.where(allowed, probs, 0.0)
            back_scores = (probs * (back_probs - stat_ref[h, q_tile, 1:2])).astype(bf16)
            both = jnp.concatenate([probs.astype(bf16), back_scores], axis=1)
            dkv_ref[keys, cols] += jnp.dot(
                both, jnp.concatenate([do, q], axis=0), preferred_element_type=f32
            )
            dq_ref[h, q_tile] += jnp.dot(kv.T[:HEAD_SIZE], back_scores, preferred_element_type=f32)

    tiles.run(tile)
    for i, out in enumerate(outs):
        out[...] = dkv_ref[i * out.shape[0] : (i + 1) * out.shape[0]].astype(out.dtype)


def in_smem():
    return pl.BlockSpec(memory_space=pltpu.SMEM)


def in_vmem():
    return pl.BlockSpec(memory_space=pltpu.VMEM)


class Attention:
    def __init__(self, ring, block_order, starts, blk):
        self.ring, self.order, self.starts = ring, block_order, starts
        self.blk, self.seq_count = blk, starts.shape[0]

    def _make(self, slots):
        return lambda order_ref, starts_ref: Tiles(
            self.ring, slots, self.seq_count, self.blk, order_ref, starts_ref
        )

    def _cost(self, slots, heads, products, arrays):
        tile = 2 * self.blk * self.blk * heads * pair_count(slots, self.seq_count)
        return pl.CostEstimate(
            flops=2 * tile * 256 * products // COST_SCALE,
            bytes_accessed=sum(x.size * x.dtype.itemsize for x in arrays) // COST_SCALE,
            transcendentals=tile // COST_SCALE,
        )

    def forward(self, slots, chunks, q, acc):
        heads, tiles, rows, _ = q.shape
        out = jax.ShapeDtypeStruct((heads, tiles, rows, LANES), f32)
        held = [] if acc is None else [acc]
        keys, width = len(chunks) * chunks[0].shape[0], chunks[0].shape[1]
        return pl.pallas_call(
            functools.partial(forward_kernel, self._make(slots), len(chunks), heads),
            out_shape=out,
            in_specs=[in_smem()] * 2 + [in_vmem()] * (1 + len(chunks) + len(held)),
            out_specs=in_vmem(),
            scratch_shapes=[pltpu.VMEM((keys, width), bf16)],
            compiler_params=pltpu.CompilerParams(vmem_limit_bytes=VMEM_BYTES),
            cost_estimate=self._cost(slots, heads, 2, [q, *chunks, out, out]),
            name="attend_forward",
        )(self.order, self.starts, q, *chunks, *held)

    def backward(self, slots, chunks, q, do, stats, acc):
        heads, tiles, rows, _ = q.shape
        keys, width = len(chunks) * chunks[0].shape[0], chunks[0].shape[1]
        outs = [jax.ShapeDtypeStruct((heads, tiles, HEAD_SIZE, rows), f32)] + [
            jax.ShapeDtypeStruct(x.shape, bf16 if c else f32) for x, (_, c) in zip(chunks, slots)
        ]
        held = [] if acc is None else [acc]
        dq, *grads = pl.pallas_call(
            functools.partial(
                backward_kernel, self._make(slots), len(chunks), len(held), heads
            ),
            out_shape=outs,
            in_specs=[in_smem()] * 2 + [in_vmem()] * (3 + len(chunks) + len(held)),
            out_specs=[in_vmem()] * len(outs),
            scratch_shapes=[pltpu.VMEM((keys, width), bf16), pltpu.VMEM((keys, width), f32)],
            compiler_params=pltpu.CompilerParams(vmem_limit_bytes=VMEM_BYTES),
            cost_estimate=self._cost(slots, heads, 5, [q, do, outs[0], *chunks, *outs]),
            name="attend_backward",
        )(self.order, self.starts, q, do, stats, *chunks, *held)
        return dq, grads


def grads_kernel(ring, two_ref, gate_ref, up_ref, ffn_ref, cot_ref, *refs):
    outs, (lhs_ref, all_ref) = refs[:-2], refs[-2:]
    place, core = ring.here()

    @pl.when(pl.program_id(0) == 0)
    def _():
        lhs_ref[...] = two_ref[...].T

    n = ring.n
    unit = lhs_ref.shape[0] // (2 * n)
    cols = gate_ref.shape[1]
    thin = cols // (2 * n)
    for i, ref in enumerate((gate_ref, up_ref)):
        grad = jnp.dot(lhs_ref[...], ref[...], preferred_element_type=f32).astype(bf16)
        all_ref[:, i * unit : (i + 1) * unit] = grad.reshape(2 * n, unit, cols)
    down = jnp.dot(ffn_ref[...].T, cot_ref[...], preferred_element_type=f32).astype(bf16)
    down = down.reshape(2 * n, thin, down.shape[1])
    for k in range(down.shape[2] // cols):
        at = 2 * unit + k * thin
        all_ref[:, at : at + thin] = down[:, :, k * cols : (k + 1) * cols]
    for i, d in enumerate(ring.distances()):
        q = (place + d + n) % n
        outs[i][...] = all_ref[core * n + q]
        outs[n + i][...] = all_ref[(1 - core) * n + q]


def ffn_grads(ring, hidden_two, back_gate, back_up, hidden_ffn, cotangent):
    rows, width = hidden_two.shape
    units = back_gate.shape[1]
    n = ring.n
    wide = width // (2 * n) * 3
    cols = 256
    whole = pl.BlockSpec((rows, width), lambda j: (0, 0))
    block = pl.BlockSpec((rows, cols), lambda j: (0, j))
    cut = pl.BlockSpec((wide, cols), lambda j: (0, j))
    outs = pl.pallas_call(
        functools.partial(grads_kernel, ring),
        grid=(units // cols,),
        out_shape=[jax.ShapeDtypeStruct((wide, units), bf16)] * (2 * n),
        in_specs=[whole, block, block, block, whole],
        out_specs=[cut] * (2 * n),
        scratch_shapes=[pltpu.VMEM((width, rows), bf16), pltpu.VMEM((2 * n, wide, cols), bf16)],
        compiler_params=pltpu.CompilerParams(vmem_limit_bytes=VMEM_BYTES),
        cost_estimate=pl.CostEstimate(
            flops=6 * rows * width * units // COST_SCALE, bytes_accessed=2**20, transcendentals=0
        ),
        name="ffn_grads",
    )(hidden_two, back_gate, back_up, hidden_ffn, cotangent)
    return outs[:n], outs[n:]


def place_kernel(ring, *refs):
    parts, (gate_ref, up_ref, down_ref) = refs[:-3], refs[-3:]
    place, core = ring.here()
    n = ring.n
    cols = gate_ref.shape[1]
    unit = gate_ref.shape[0] // (2 * n)
    thin = cols // (2 * n)
    for i, part in enumerate(parts):
        q = (place + ring.distances()[i // 2] + n) % n
        r = (core + i % 2) % 2 * n + q
        rows = pl.ds(pl.multiple_of(r * unit, unit), unit)
        gate_ref[rows] = part[:unit].astype(f32)
        up_ref[rows] = part[unit : 2 * unit].astype(f32)
        rows = pl.ds(pl.multiple_of(r * thin, thin), thin)
        for k in range(down_ref.shape[1] // cols):
            at = 2 * unit + k * thin
            down_ref[rows, k * cols : (k + 1) * cols] = part[at : at + thin].astype(f32)


def place_ffn(ring, parts, width):
    wide, units = parts[0].shape
    cols = 256
    return pl.pallas_call(
        functools.partial(place_kernel, ring),
        grid=(units // cols,),
        out_shape=(
            jax.ShapeDtypeStruct((width, units), f32),
            jax.ShapeDtypeStruct((width, units), f32),
            jax.ShapeDtypeStruct((units, width), f32),
        ),
        in_specs=[pl.BlockSpec((wide, cols), lambda j: (0, j))] * len(parts),
        out_specs=(
            pl.BlockSpec((width, cols), lambda j: (0, j)),
            pl.BlockSpec((width, cols), lambda j: (0, j)),
            pl.BlockSpec((cols, width), lambda j: (j, 0)),
        ),
        compiler_params=pltpu.CompilerParams(vmem_limit_bytes=VMEM_BYTES),
        cost_estimate=pl.CostEstimate(
            flops=0, bytes_accessed=18 * width * units // COST_SCALE, transcendentals=0
        ),
        name="place_ffn",
    )(*parts)


def place_qkv_kernel(ring, *refs):
    parts, (query_ref, key_ref, value_ref, out_ref) = refs[:-4], refs[-4:]
    place, core = ring.here()
    n = ring.n
    unit, thin = query_ref.shape[0] // (2 * n), out_ref.shape[0] // (2 * n)
    for i, part in enumerate(parts):
        q = (place + ring.distances()[i // 2] + n) % n
        r = (core + i % 2) % 2 * n + q
        rows = pl.ds(pl.multiple_of(r * unit, unit), unit)
        at = query_ref.shape[1]
        query_ref[rows] = part[:unit, :at].astype(f32)
        for h in range(key_ref.shape[1] // HEAD_SIZE):
            cols = slice(h * HEAD_SIZE, (h + 1) * HEAD_SIZE)
            both = part[:unit, at + h * LANES : at + (h + 1) * LANES].astype(f32)
            key_ref[rows, cols] = both[:, :HEAD_SIZE]
            value_ref[rows, cols] = both[:, HEAD_SIZE:]
        rows = pl.ds(pl.multiple_of(r * thin, thin), thin)
        out_ref[rows] = part[unit:].astype(f32)


def place_qkv(ring, parts, width, cols):
    thin = parts[0].shape[0] - width // (2 * ring.n)
    return pl.pallas_call(
        functools.partial(place_qkv_kernel, ring),
        out_shape=[jax.ShapeDtypeStruct((width, c), f32) for c in cols]
        + [jax.ShapeDtypeStruct((thin * 2 * ring.n, width), f32)],
        in_specs=[in_vmem()] * len(parts),
        out_specs=[in_vmem()] * 4,
        compiler_params=pltpu.CompilerParams(vmem_limit_bytes=VMEM_BYTES),
        cost_estimate=pl.CostEstimate(
            flops=0, bytes_accessed=9 * 2**20, transcendentals=0
        ),
        name="place_qkv",
    )(*parts)


def whole_call(kernel, name, outs, args, flops, scratch=()):
    moved = sum(x.size * x.dtype.itemsize for x in (*outs, *args))
    return pl.pallas_call(
        kernel,
        out_shape=list(outs),
        in_specs=[in_vmem()] * len(args),
        out_specs=[in_vmem()] * len(outs),
        scratch_shapes=list(scratch),
        compiler_params=pltpu.CompilerParams(vmem_limit_bytes=VMEM_BYTES),
        cost_estimate=pl.CostEstimate(
            flops=flops // COST_SCALE, bytes_accessed=moved // COST_SCALE, transcendentals=0
        ),
        name=name,
    )(*args)


def shape(*dims, dtype=f32):
    return jax.ShapeDtypeStruct(dims, dtype)


def first_lanes(rows):
    return lax.broadcasted_iota(jnp.int32, (rows, LANES), 1) < HEAD_SIZE


def head_mean(x):
    i = lax.broadcasted_iota(jnp.int32, (LANES, LANES), 0) // HEAD_SIZE
    j = lax.broadcasted_iota(jnp.int32, (LANES, LANES), 1) // HEAD_SIZE
    mean = jnp.where(i == j, 1.0 / HEAD_SIZE, 0.0)
    return jnp.dot(x, mean, precision=lax.Precision.HIGHEST, preferred_element_type=f32)


def turn(x, cosine, sines):
    lane = lax.broadcasted_iota(jnp.int32, x.shape, 1) % HEAD_SIZE
    half = HEAD_SIZE // 2
    other = jnp.where(
        lane < half, pltpu.roll(x, LANES - half, axis=1), pltpu.roll(x, half, axis=1)
    )
    return x * cosine + other * sines


def row_scale(x):
    return lax.rsqrt(jnp.mean(x * x, axis=-1, keepdims=True) + EPSILON)


def norm_back(upstream, x, scale, gain):
    inner = upstream * gain
    return scale * (inner - x * (scale * scale * jnp.mean(inner * x, axis=-1, keepdims=True)))


def head_norm_back(upstream, x, gain):
    scale = lax.rsqrt(head_mean(x * x) + EPSILON)
    inner = upstream * gain
    back = scale * (inner - x * (scale * scale * head_mean(inner * x)))
    return back, jnp.sum(upstream * x * scale, axis=0, keepdims=True)


def lanes(tile):
    return slice(tile * LANES, (tile + 1) * LANES)


def project_kernel(
    tiles,
    tokens,
    gain,
    w_query,
    w_key,
    w_value,
    query_gain,
    key_gain,
    cosine,
    sines,
    hidden,
    query_raw,
    kv_raw,
    q_tiles,
    kv,
    w_kv,
):
    x = tokens[...].astype(f32)
    hidden[...] = (x * row_scale(x) * gain[...]).astype(bf16)
    rows = x.shape[0]
    blk = rows // tiles
    first = first_lanes(rows)
    for h in range(q_tiles.shape[0]):
        raw = jnp.dot(hidden[...], w_query[:, lanes(h)], preferred_element_type=f32)
        query_raw[:, lanes(h)] = raw
        normed = raw * lax.rsqrt(head_mean(raw * raw) + EPSILON) * query_gain[...]
        turned = turn(normed, cosine[...], sines[...]).astype(bf16).astype(f32) * 0.125
        pair = [
            jnp.where(first, turned, 0.0),
            jnp.where(first, pltpu.roll(turned, HEAD_SIZE, axis=1), 0.0),
        ]
        for g, one in enumerate(pair):
            for t in range(tiles):
                q_tiles[h, t, g * blk : (g + 1) * blk] = one[t * blk : (t + 1) * blk].astype(bf16)
    for h in range(kv.shape[1] // LANES):
        cols = slice(h * HEAD_SIZE, (h + 1) * HEAD_SIZE)
        w_kv[:, lanes(h)] = jnp.concatenate([w_key[:, cols], w_value[:, cols]], axis=1)
        raw = jnp.dot(hidden[...], w_kv[:, lanes(h)], preferred_element_type=f32)
        kv_raw[:, lanes(h)] = raw
        normed = raw * lax.rsqrt(head_mean(raw * raw) + EPSILON) * key_gain[...]
        kv[:, lanes(h)] = jnp.where(first, turn(normed, cosine[...], sines[...]), raw).astype(bf16)


def mix_kernel(acc, w_out, *refs):
    attended, o, lse, halves = refs[0], refs[1], refs[2], refs[3:]
    heads, tiles, rows, _ = acc.shape
    blk = rows // 2
    first = first_lanes(rows)
    pick = jnp.where(lax.broadcasted_iota(jnp.int32, (8, LANES), 1) == 0, 1.0, 0.0)
    for h in range(heads):
        for t in range(tiles):
            x = acc[h, t]
            value = jnp.where(first, 0.0, x * pltpu.roll(1.0 / x, HEAD_SIZE, axis=1))
            o[h, t] = value
            sums = jnp.log2(jnp.where(first, x, 1.0))
            lse[h, t] = lax.dot_general(
                pick, sums, NT, precision=lax.Precision.HIGHEST, preferred_element_type=f32
            )
            low = pltpu.roll(value[:blk], HEAD_SIZE, axis=1) + value[blk:]
            attended[t * blk : (t + 1) * blk, lanes(h)] = low.astype(bf16)
    part = attended.shape[0] // len(halves)
    for i, half in enumerate(halves):
        half[...] = jnp.dot(
            attended[i * part : (i + 1) * part], w_out[...], preferred_element_type=f32
        ).astype(bf16)


def ffn_kernel(
    terms,
    tokens,
    gain,
    hidden_back,
    w_gate,
    w_up,
    *refs,
):
    mine, theirs, refs = refs[:terms], refs[terms : 2 * terms], refs[2 * terms :]
    mixed, hidden_two, hidden_ffn, back_gate, back_up, gain_grad = refs[:6]
    halves, sums = refs[6:-1], refs[-1]
    step, last = pl.program_id(0), pl.num_programs(0) - 1

    @pl.when(step == 0)
    def _():
        part = tokens.shape[0] // terms
        for i in range(terms):
            rows = slice(i * part, (i + 1) * part)
            x = tokens[rows].astype(f32) + (mine[i][...].astype(f32) + theirs[i][...].astype(f32))
            mixed[rows] = x
            hidden_two[rows] = (x * row_scale(x) * gain[...]).astype(bf16)
        sums[...] = jnp.zeros_like(sums)

    gating = jnp.dot(hidden_two[...], w_gate[...], preferred_element_type=f32)
    lifted = jnp.dot(hidden_two[...], w_up[...], preferred_element_type=f32)
    upstream = hidden_back[...]
    logistic = jax.nn.sigmoid(gating)
    silu = gating * logistic
    hidden_ffn[...] = (silu * lifted).astype(bf16)
    back_gate[...] = (
        upstream * lifted * logistic * (1.0 + gating * (1.0 - logistic))
    ).astype(bf16)
    back_up[...] = (upstream * silu).astype(bf16)
    sums[...] += lax.dot_general(
        back_gate[...], w_gate[...], NT, preferred_element_type=f32
    ) + lax.dot_general(back_up[...], w_up[...], NT, preferred_element_type=f32)

    @pl.when(step == last)
    def _():
        x = mixed[...]
        gain_grad[...] = jnp.sum(sums[...] * x * row_scale(x), axis=0, keepdims=True)
        part = sums.shape[0] // len(halves)
        for i, half in enumerate(halves):
            half[...] = sums[i * part : (i + 1) * part].astype(bf16)


def feed_forward(tokens, gain, hidden_back, w_gate, w_up, mine, theirs):
    rows, width = tokens.shape
    units = w_gate.shape[1]
    cols = 256 if units % 256 == 0 else units
    whole = pl.BlockSpec((rows, width), lambda j: (0, 0))
    line = pl.BlockSpec((1, width), lambda j: (0, 0))
    block = pl.BlockSpec((rows, cols), lambda j: (0, j))
    weight = pl.BlockSpec((width, cols), lambda j: (0, j))
    part = pl.BlockSpec((rows // len(mine), width), lambda j: (0, 0))
    half = pl.BlockSpec((rows // 2, width), lambda j: (0, 0))
    low = shape(rows, units, dtype=bf16)
    return pl.pallas_call(
        functools.partial(ffn_kernel, len(mine)),
        grid=(units // cols,),
        out_shape=[shape(rows, width), shape(rows, width, dtype=bf16), low, low, low]
        + [shape(1, width)]
        + [shape(rows // 2, width, dtype=bf16)] * 2,
        in_specs=[whole, line, block, weight, weight] + [part] * (2 * len(mine)),
        out_specs=[whole, whole, block, block, block, line, half, half],
        scratch_shapes=[pltpu.VMEM((rows, width), f32)],
        compiler_params=pltpu.CompilerParams(vmem_limit_bytes=VMEM_BYTES),
        cost_estimate=pl.CostEstimate(
            flops=8 * rows * width * units // COST_SCALE, bytes_accessed=2**20, transcendentals=0
        ),
        name="feed_forward",
    )(tokens, gain, hidden_back, w_gate, w_up, *mine, *theirs)


def back_kernel(terms, cotangent, mixed, gain, w_out, o, lse, *refs):
    mine, theirs, (back_mixed, back_proj, do_tiles, stats) = (
        refs[:terms],
        refs[terms : 2 * terms],
        refs[2 * terms :],
    )
    part = cotangent.shape[0] // terms
    for i in range(terms):
        rows = slice(i * part, (i + 1) * part)
        x = mixed[rows]
        upstream = mine[i][...].astype(f32) + theirs[i][...].astype(f32)
        back = cotangent[rows].astype(f32) + norm_back(upstream, x, row_scale(x), gain[...])
        back_mixed[rows] = back
        back_proj[rows] = back.astype(bf16)
    heads, tiles, rows, _ = o.shape
    blk = rows // 2
    first = first_lanes(blk)
    ones = jnp.ones((8, LANES), f32)
    row = lax.broadcasted_iota(jnp.int32, (8, rows), 0)
    for h in range(heads):
        attn = lax.dot_general(back_proj[...], w_out[lanes(h)], NT, preferred_element_type=f32)
        for t in range(tiles):
            here = attn[t * blk : (t + 1) * blk]
            do = jnp.concatenate(
                [
                    jnp.where(first, 0.0, pltpu.roll(here, HEAD_SIZE, axis=1)),
                    jnp.where(first, 0.0, here),
                ],
                axis=0,
            ).astype(bf16)
            do_tiles[h, t] = do
            delta = lax.dot_general(
                ones,
                do.astype(f32) * o[h, t],
                NT,
                precision=lax.Precision.HIGHEST,
                preferred_element_type=f32,
            )
            stats[h, t] = jnp.where(row == 0, lse[h, t], delta)


def back_query_kernel(dq, query_raw, query_gain, cosine, sines, query_delta, gain_grad):
    heads, tiles, _, rows = dq.shape
    blk = rows // 2
    gain_grad[...] = jnp.zeros_like(gain_grad)
    for t in range(tiles):
        at = slice(t * blk, (t + 1) * blk)
        for h in range(heads):
            both = jnp.concatenate([dq[h, t, :, :blk], dq[h, t, :, blk:]], axis=0) * 0.125
            turned = turn(both.T, cosine[at], -sines[at])
            back, gain_terms = head_norm_back(turned, query_raw[at, lanes(h)], query_gain[...])
            query_delta[at, lanes(h)] = back.astype(bf16)
            gain_grad[...] += gain_terms


def back_project_kernel(
    ring,
    tokens,
    hidden,
    query_delta,
    own_dkv,
    kv_raw,
    key_gain,
    cosine,
    sines,
    w_query,
    w_kv,
    attended,
    back_proj,
    *refs,
):
    low, norm_grad, gain_grad, kv_delta = refs[:4]
    outs, all_ref = refs[4:-1], refs[-1]
    rows, width = tokens.shape
    first = first_lanes(rows)
    gain_grad[...] = jnp.zeros_like(gain_grad)
    for h in range(own_dkv.shape[1] // LANES):
        dkv = own_dkv[:, lanes(h)].astype(f32)
        turned = turn(dkv, cosine[...], -sines[...])
        back, gain_terms = head_norm_back(turned, kv_raw[:, lanes(h)], key_gain[...])
        kv_delta[:, lanes(h)] = jnp.where(first, back, dkv).astype(bf16)
        gain_grad[...] += gain_terms
    part = lax.dot_general(
        query_delta[...], w_query[...], NT, preferred_element_type=f32
    ) + lax.dot_general(kv_delta[...], w_kv[...], NT, preferred_element_type=f32)
    low[...] = part.astype(bf16)
    x = tokens[...].astype(f32)
    norm_grad[...] = jnp.sum(part * x * row_scale(x), axis=0, keepdims=True)
    if not outs:
        return
    lhs = hidden[...].T
    place, core = ring.here()
    n = ring.n
    unit = width // (2 * n)
    q_cols = query_delta.shape[1]
    for cols, right in (
        (slice(0, q_cols), query_delta),
        (slice(q_cols, q_cols + kv_delta.shape[1]), kv_delta),
    ):
        grad = jnp.dot(lhs, right[...], preferred_element_type=f32).astype(bf16)
        all_ref[:, :unit, cols] = grad.reshape(2 * n, unit, grad.shape[1])
    grad = jnp.dot(attended[...].T, back_proj[...], preferred_element_type=f32).astype(bf16)
    all_ref[:, unit:] = grad.reshape(2 * n, -1, width)
    for i, d in enumerate(ring.distances()):
        q = (place + d + n) % n
        outs[i][...] = all_ref[core * n + q]
        outs[n + i][...] = all_ref[(1 - core) * n + q]


def dot(a, b, dims):
    return lax.dot_general(a, b, ((dims[:1], dims[1:]), ((), ())), preferred_element_type=f32)


def on_device(
    tokens,
    cotangent,
    block_order,
    segment_ids,
    norm_gain,
    w_query,
    key_weight,
    value_weight,
    query_gain,
    key_gain,
    w_out,
    ffn_gain,
    w_gate,
    w_up,
    w_down,
):
    devices = lax.axis_size("ctx")
    ring = Ring(devices)
    far = ring.n // 2
    rows, width = tokens.shape
    seq_count = segment_ids.shape[0]
    blk = rows // seq_count // 2
    tiles = 2 * seq_count
    kv_heads = key_weight.shape[1] // HEAD_SIZE
    q_cols, k_cols = w_query.shape[1], key_weight.shape[1]
    units = w_gate.shape[1]
    packed = units % 256 == 0 and width % (32 * ring.n) == 0 and w_out.shape[0] % (32 * ring.n) == 0
    pair = lax.axis_size("tp") == 2

    def shared(halves):
        if pair:
            return from_other(halves), list(halves)
        return [lax.psum(x, "tp") for x in halves], [jnp.zeros_like(x) for x in halves]

    order = block_order[lax.axis_index("ctx")]
    blocks = jnp.stack([order, 2 * devices - 1 - order] * seq_count)
    place = (blocks[:, None] * blk + jnp.arange(blk, dtype=jnp.int32)[None, :]).reshape(rows)
    starts = jnp.stack([jnp.sum((segment_ids < d).astype(jnp.int32), axis=1) for d in (1, 2, 3)], 1)
    lane = np.arange(LANES) % HEAD_SIZE
    half = HEAD_SIZE // 2
    inverse = ROPE_BASE ** (-jnp.arange(0, HEAD_SIZE, 2, dtype=f32) / HEAD_SIZE)
    angles = place.astype(f32)[:, None] * jnp.tile(inverse, LANES // half)[None, :]
    cosine = jnp.cos(angles)
    sines = jnp.sin(angles) * np.where(lane < half, -1.0, 1.0).astype(np.float32)[None, :]

    def line(x):
        return x.astype(f32).reshape(1, -1)

    def head_line(x):
        return jnp.tile(line(x), (1, 2))

    hidden_input, query_raw, kv_raw, q_tiles, own_kv, w_kv = whole_call(
        functools.partial(project_kernel, tiles),
        "project",
        [
            shape(rows, width, dtype=bf16),
            shape(rows, q_cols),
            shape(rows, 2 * k_cols),
            shape(kv_heads, tiles, 2 * blk, LANES, dtype=bf16),
            shape(rows, 2 * k_cols, dtype=bf16),
            shape(width, 2 * k_cols, dtype=bf16),
        ],
        [
            tokens,
            line(norm_gain),
            w_query,
            key_weight,
            value_weight,
            head_line(query_gain),
            head_line(key_gain),
            cosine,
            sines,
        ],
        2 * rows * width * (q_cols + 2 * k_cols),
    )

    attention = Attention(ring, block_order, starts, blk)
    gather = RingGather(ring, own_kv)
    found = {(0, 0): own_kv, (0, 1): gather.siblings[0]}
    gather.send(gather.sends())
    acc = attention.forward([(0, 0)], [own_kv], q_tiles, None)
    late = [(0, 1)]
    for d in range(1, far + 1):
        now = [(-d, 0), (d, 0)] if d < far else [(d, 0)]
        k = len(now)
        *gather.new, acc = lax.optimization_barrier((*gather.new, acc))
        gather.parts[-k:] = gather.new
        gather.siblings[-k:] = [ring.sibling(x) for x in gather.new]
        for i, (x, _) in enumerate(now):
            found[x, 0], found[x, 1] = gather.parts[i - k], gather.siblings[i - k]
        if d < far:
            gather.send(gather.sends())
        slots = late + now if d < far else late
        acc = attention.forward(slots, [found[x] for x in slots], q_tiles, acc)
        late = [(x, 1) for x, _ in now]
    slots = now + late
    acc = attention.forward(slots, [found[x] for x in slots], q_tiles, acc)
    attended, o, lse, *mix_halves = whole_call(
        mix_kernel,
        "mix",
        [
            shape(rows, q_cols, dtype=bf16),
            shape(*acc.shape),
            shape(kv_heads, tiles, 8, 2 * blk),
            shape(rows // 2, width, dtype=bf16),
            shape(rows // 2, width, dtype=bf16),
        ],
        [acc, w_out],
        2 * rows * width * q_cols,
    )
    theirs, mine = shared(mix_halves)
    back_hidden = dot(cotangent, w_down, (1, 1))
    back_hidden, *theirs = lax.optimization_barrier((back_hidden, *theirs))

    mixed, hidden_two, hidden_ffn, back_gate, back_up, grad_ffn_gain, *halves = feed_forward(
        tokens, line(ffn_gain), back_hidden, w_gate, w_up, mine, theirs
    )
    if packed:
        first, mine_first = shared(halves[:1])
        keep, give = ffn_grads(ring, hidden_two, back_gate, back_up, hidden_ffn, cotangent)
        at = {d: i for i, d in enumerate(ring.distances())}
        second, first[0], *give = lax.optimization_barrier((halves[1], first[0], *give))
        second, mine_second = shared([second])
        got = [ring.sibling(x) for x in give]
        ffn_sum = Steps(sum_steps(ring, lambda d: [keep[at[d]], got[at[d]]]))
        advance([ffn_sum])
        theirs = advance([ffn_sum], first[0], second[0])
        mine = mine_first + mine_second
    else:
        theirs, mine = shared(halves)
        grad_w_down = dot(hidden_ffn, cotangent, (0, 0)).astype(bf16)
        grad_w_gate = dot(hidden_two, back_gate, (0, 0)).astype(bf16)
        grad_w_up = dot(hidden_two, back_up, (0, 0)).astype(bf16)
        grad_w_gate, grad_w_up, grad_w_down = sum_over_ctx(
            ring, [grad_w_gate, grad_w_up, grad_w_down]
        )
        ffn_sum = None
    hidden_ffn, *theirs = lax.optimization_barrier((hidden_ffn, *theirs))
    output_part = dot(hidden_ffn, w_down, (1, 0)).astype(bf16)
    output = (mixed + sum_over_tp(output_part)).astype(bf16)

    back_mixed, back_proj, do_tiles, stats = whole_call(
        functools.partial(back_kernel, 2),
        "back",
        [
            shape(rows, width),
            shape(rows, width, dtype=bf16),
            shape(*q_tiles.shape, dtype=bf16),
            shape(*lse.shape),
        ],
        [cotangent, mixed, line(ffn_gain), w_out, o, lse, *mine, *theirs],
        2 * rows * width * q_cols,
    )
    dq = None
    terms = {}

    def dkv_steps():
        ring_sum = RingSum(ring)
        for d in range(far, 0, -1):
            ring_sum.send((yield ring_sum.sends(d, terms[d], terms.get(-d)), []))
        return ring_sum

    dkv_sum = Steps(dkv_steps())
    for d in range(far, -1, -1):
        slots = [(x, c) for x in ([-d, d] if 0 < d < far else [d]) for c in (0, 1)]
        if d < far:
            (do_tiles,) = advance([ffn_sum, dkv_sum if d < far - 1 else None], do_tiles)
        dq, grads = attention.backward(
            slots, [found[x] for x in slots], q_tiles, do_tiles, stats, dq
        )
        for i in range(0, len(slots), 2):
            terms[slots[i][0]] = [grads[i], ring.sibling(grads[i + 1])]
    (dq,) = advance([ffn_sum, dkv_sum], dq)
    query_delta, grad_query_gain = whole_call(
        back_query_kernel,
        "back_query",
        [shape(rows, q_cols, dtype=bf16), shape(1, LANES)],
        [dq, query_raw, head_line(query_gain), cosine, sines],
        2 * rows * width,
    )
    advance([dkv_sum])
    own_dkv = dkv_sum.result.sums(terms[0])
    wide = width // (2 * ring.n) + w_out.shape[0] // (2 * ring.n)
    one_low, grad_norm_gain, grad_key_gain, kv_delta, *cuts = whole_call(
        functools.partial(back_project_kernel, ring),
        "back_project",
        [
            shape(rows, width, dtype=bf16),
            shape(1, width),
            shape(1, LANES),
            shape(rows, 2 * k_cols, dtype=bf16),
        ]
        + ([shape(wide, width, dtype=bf16)] * (2 * ring.n) if packed else []),
        [
            tokens,
            hidden_input,
            query_delta,
            own_dkv,
            kv_raw,
            head_line(key_gain),
            cosine,
            sines,
            w_query,
            w_kv,
            attended,
            back_proj,
        ],
        4 * rows * width * (q_cols + 2 * k_cols),
        [pltpu.VMEM((2 * ring.n, wide, width), bf16)],
    )

    gains = jnp.concatenate(
        [
            grad_norm_gain[0],
            grad_ffn_gain[0],
            grad_query_gain[0, :HEAD_SIZE] + grad_query_gain[0, HEAD_SIZE:],
            grad_key_gain[0, :HEAD_SIZE],
        ]
    )
    gain_sum = Steps(pair_steps(gains, [("tp", lax.axis_size("tp")), ("ctx", devices)]))
    theirs, mine = shared([one_low])
    if packed:
        keep_qkv, give_qkv = cuts[: ring.n], cuts[ring.n :]
        got_qkv = [ring.sibling(x) for x in give_qkv]
        qkv_sum = Steps(sum_steps(ring, lambda d: [keep_qkv[at[d]], got_qkv[at[d]]]))
        placed, waiting = None, []
        while qkv_sum.generator is not None:
            waiting = advance([ffn_sum, qkv_sum, gain_sum], *waiting)
            if placed is None and ffn_sum.result is not None:
                placed = waiting = place_ffn(ring, ffn_sum.result.everything(), width)
            elif len(waiting) == 3:
                placed, waiting = waiting, theirs
            elif len(waiting) == 1:
                theirs, waiting = waiting, []
        grad_w_gate, grad_w_up, grad_w_down = placed
        grad_w_query, grad_w_key, grad_w_value, grad_w_out = place_qkv(
            ring, qkv_sum.result.everything(), width, (q_cols, k_cols, k_cols)
        )
    else:
        while gain_sum.generator is not None:
            advance([gain_sum])
        grad_w_query, grad_kv, grad_w_out = sum_over_ctx(
            ring,
            [
                dot(hidden_input, query_delta, (0, 0)).astype(bf16),
                dot(hidden_input, kv_delta, (0, 0)).astype(bf16),
                dot(attended, back_proj, (0, 0)).astype(bf16),
            ],
        )
        grad_kv = grad_kv.reshape(width, kv_heads, 2, HEAD_SIZE)
        grad_w_key = grad_kv[:, :, 0].reshape(width, k_cols)
        grad_w_value = grad_kv[:, :, 1].reshape(width, k_cols)
    gains = gain_sum.result
    back_one = mine[0].astype(f32) + theirs[0].astype(f32)
    inputs = tokens.astype(f32)
    input_grad = back_mixed + norm_back(back_one, inputs, row_scale(inputs), norm_gain)

    return (
        output,
        input_grad,
        gains[:width],
        grad_w_query,
        grad_w_key,
        grad_w_value,
        gains[2 * width : 2 * width + HEAD_SIZE],
        gains[2 * width + HEAD_SIZE :],
        grad_w_out,
        gains[width : 2 * width],
        grad_w_gate,
        grad_w_up,
        grad_w_down,
    )


def solution(mesh):
    return jax.shard_map(
        on_device,
        mesh=mesh,
        in_specs=(
            P("ctx", None),
            P("ctx", None),
            P(),
            P(),
            P(),
            P(None, "tp"),
            P(None, "tp"),
            P(None, "tp"),
            P(),
            P(),
            P("tp", None),
            P(),
            P(None, "tp"),
            P(None, "tp"),
            P("tp", None),
        ),
        out_specs=(
            P("ctx", None),
            P("ctx", None),
            P(),
            P(None, "tp"),
            P(None, "tp"),
            P(None, "tp"),
            P(),
            P(),
            P("tp", None),
            P(),
            P(None, "tp"),
            P(None, "tp"),
            P("tp", None),
        ),
        check_vma=False,
    )
```

```python
import functools

import jax
import jax.numpy as jnp
import numpy as np
from jax import lax
from jax.experimental import pallas as pl
from jax.experimental.pallas import tpu as pltpu
from jax.sharding import PartitionSpec as P

HEAD_SIZE = 64
LANES = 2 * HEAD_SIZE
EPSILON = 1e-05
ROPE_BASE = 1000000.0
LOG2E = 1.4426950408889634
VMEM_BYTES = 24 * 2**20
COST_SCALE = 1
FFN_COLS = 768
LATE = True
f32, bf16 = jnp.float32, jnp.bfloat16
NT = (((1,), (1,)), ((), ()))


class Ring:
    def __init__(self, n_ctx):
        n = self.n = n_ctx // 2
        self.zs = 4 if n % 4 == 0 else n
        self.ys = n // self.zs
        order = [int(self.chip_at(np.int32(place))) for place in range(n)]

        def steps(flip, turned):
            return [
                (order[i] * 2 + c, order[(i + (1 - 2 * (c ^ turned))) % n] * 2 + (c ^ flip))
                for i in range(n)
                for c in (0, 1)
            ]

        self.onward, self.across, self.spread = steps(0, 0), steps(1, 0), steps(1, 1)
        self.to_sibling = [(i, i ^ 1) for i in range(n_ctx)]

    def chip_at(self, place):
        if self.ys == 1:
            return place
        where = np.where if isinstance(place, np.integer) else jnp.where
        turn = place - self.zs
        k, r = turn // (self.ys - 1), turn % (self.ys - 1)
        back = (self.zs - 1 - k) * self.ys + where(k % 2 == 0, 1 + r, self.ys - 1 - r)
        return where(place < self.zs, place * self.ys, back)

    def here(self):
        index = lax.axis_index("ctx")
        chip, core = index // 2, index % 2
        if self.ys == 1:
            return chip, core
        z, y = chip // self.ys, chip % self.ys
        k = self.zs - 1 - z
        back = self.zs + k * (self.ys - 1) + jnp.where(k % 2 == 0, y - 1, self.ys - 1 - y)
        return jnp.where(y == 0, z, back), core

    def at(self, slot):
        place, core = self.here()
        distance, other = slot
        return (place + (1 - 2 * core) * distance + self.n) % self.n, (core + other) % 2

    def device_at(self, slot):
        place, core = self.at(slot)
        return self.chip_at(place) * 2 + core

    def hop(self, x):
        return lax.ppermute(x, "ctx", self.onward)

    def sibling(self, x):
        return lax.ppermute(x, "ctx", self.to_sibling)


def total(*terms):
    out = terms[0].astype(f32)
    for term in terms[1:]:
        out = out + term.astype(f32)
    return out.astype(bf16)


class RingGather:
    def __init__(self, ring, own):
        self.ring, self.far = ring, ring.n // 2
        self.pieces = [([(0, 0)], own), ([(0, 1)], ring.sibling(own))]
        self.step = 0

    def sends(self):
        last = self.pieces[-2][1]
        if self.step == 0:
            return [self.pieces[0][1]]
        return [last[0]] if self.step + 1 == self.far else [last]

    def send(self, arrays):
        (x,) = arrays
        self.step += 1
        new = [self.ring.hop(x)]
        if self.step == 1:
            new.append(lax.ppermute(x, "ctx", self.ring.spread))
        return new

    def arrive(self, arrays):
        d = self.step
        if d == 1:
            new = [([(-1, c)], x) for c, x in enumerate(arrays)]
            pair = jnp.stack(arrays)
            self.pieces += [([(-1, 0), (-1, 1)], pair), ([(1, 1), (1, 0)], self.ring.sibling(pair))]
            return new
        (x,) = arrays
        if d == self.far:
            new = [([(d, 0)], x), ([(d, 1)], self.ring.sibling(x))]
        else:
            new = [([(-d, 0), (-d, 1)], x), ([(d, 1), (d, 0)], self.ring.sibling(x))]
        self.pieces += new
        return new[:1]

    def done(self):
        return self.step == self.far


def sum_steps(ring, terms, box=None):
    _, core = ring.here()
    far = ring.n // 2
    (x,) = yield [total(*terms(far))]
    (got,) = yield [ring.hop(x)]
    for d in range(far - 1, 1, -1):
        here = terms(d)
        if d == far - 1:
            x = jnp.stack([total(*[y[0] for y in here], got), total(*[y[1] for y in here])])
        else:
            x = total(*here, got)
        (x,) = yield [x]
        (got,) = yield [ring.hop(x)]
    here = terms(1)
    x = yield [total(*[y[c] for y in here], got[c]) for c in (0, 1)]
    got = yield [ring.hop(x[0]), lax.ppermute(x[1], "ctx", ring.across)]
    own = total(*terms(0), *got)
    if box is None:
        return own
    gather = RingGather(ring, own)
    box.append(gather)
    while not gather.done():
        late = [x for _, x in gather.pieces[-1:]]
        new = gather.send((yield gather.sends()))
        came = yield new + late
        gather.arrive(came[: len(new)])
    return gather


class Steps:
    def __init__(self, generator):
        self.generator, self.result = generator, None
        self.sent = self.came = None

    def arrivals(self):
        return self.generator.send(self.sent) if self.sent is not None else []

    def sends(self):
        try:
            return self.generator.send(self.came or None)
        except StopIteration as stop:
            self.result, self.generator = stop.value, None
            return []


def tied(lists, others):
    flat = lax.optimization_barrier((*[x for xs in lists for x in xs], *others))
    out = []
    for xs in lists:
        out.append(list(flat[: len(xs)]))
        flat = flat[len(xs) :]
    return out, flat


def advance(steps, *others):
    steps = [x for x in steps if x is not None and x.generator is not None]
    came, others = tied([x.arrivals() for x in steps], others)
    for x, arrays in zip(steps, came):
        x.came = arrays
    sends, others = tied([x.sends() for x in steps], others)
    for x, arrays in zip(steps, sends):
        x.sent = arrays
    return others


def sum_over_ctx(ring, arrays):
    n = ring.n
    far = n // 2
    outs = []
    for x in arrays:
        unit = x.shape[0] // (2 * n)
        cut = x.reshape(2, n, unit, x.shape[1])

        def piece(distance, other):
            place, core = ring.at((distance, other))
            return cut[core, place]

        def terms(d):
            if d in (0, far):
                return [piece(d, 0), ring.sibling(piece(d, 1))]
            keep = jnp.stack([piece(d, 0), piece(d, 1)])
            return [keep, ring.sibling(jnp.stack([piece(-d, 1), piece(-d, 0)]))]

        box = []
        steps = Steps(sum_steps(ring, terms, box))
        while steps.generator is not None:
            advance([steps])
        out = jnp.zeros(x.shape, f32)
        for slots, part in box[0].pieces:
            for i, slot in enumerate(slots):
                place, core = ring.at(slot)
                one = part if len(slots) == 1 else part[i]
                out = lax.dynamic_update_slice_in_dim(
                    out, one.astype(f32), (core * n + place) * unit, 0
                )
        outs.append(out)
    return outs


def exchange_steps(x):
    (x,) = yield [x]
    (theirs,) = yield [lax.ppermute(x, "tp", [(0, 1), (1, 0)])]
    return theirs


def pair_steps(x, axes):
    for axis, size in axes:
        step = 1
        while step < size:
            (mine,) = yield [x]
            (theirs,) = yield [lax.ppermute(mine, axis, [(i, i ^ step) for i in range(size)])]
            x = mine + theirs
            step *= 2
    return x


def from_other(xs):
    return [lax.ppermute(x, "tp", [(0, 1), (1, 0)]) for x in xs]


def sum_over_tp(x):
    size = lax.axis_size("tp")
    if size == 2:
        return x.astype(f32) + lax.ppermute(x, "tp", [(0, 1), (1, 0)]).astype(f32)
    return lax.psum(x, "tp").astype(f32)


def pair_count(slots, seq_count):
    return seq_count * (2 * len(slots) + ((0, 0) in slots))


class Tiles:
    def __init__(self, ring, slots, seq_count, blk, order_ref, starts_ref):
        self.ring, self.slots = ring, slots
        self.seq_count, self.blk = seq_count, blk
        self.order, self.starts = order_ref, starts_ref
        self.last = 4 * ring.n - 1
        self.rows = pair_count(slots, seq_count)

    def start_of(self, seq, place):
        start = jnp.int32(0)
        for d in range(3):
            at = self.starts[seq, d]
            start = jnp.where(place >= at, at, start)
        return start

    def pair(self, row):
        seq, row = row % self.seq_count, row // self.seq_count
        slot, which = row // 2, row % 2
        own = self.slots.index((0, 0)) if (0, 0) in self.slots else None
        if own is not None:
            both_high = slot == len(self.slots)
            slot = jnp.where(both_high, own, slot)
        distance, other = self.slots[0]
        for i, (d, c) in enumerate(self.slots):
            distance, other = jnp.where(slot == i, d, distance), jnp.where(slot == i, c, other)
        mine = self.order[lax.axis_index("ctx")]
        theirs = self.order[self.ring.device_at((distance, other))]
        low = (which == 1) & (theirs <= mine)
        high = (which == 1) & (theirs > mine)
        if own is not None:
            low, high = low & jnp.logical_not(both_high), high | both_high
        q_place = jnp.where(low, mine, self.last - mine) * self.blk
        k_place = jnp.where(high, self.last - theirs, theirs) * self.blk
        q_tile = 2 * seq + jnp.where(low, 0, 1)
        k_tile = 2 * (self.seq_count * slot + seq) + jnp.where(high, 1, 0)
        k_end, q_end = k_place + self.blk - 1, q_place + self.blk - 1
        whole = (k_end <= q_place) & (k_place >= self.start_of(seq, q_end))
        empty = k_end < self.start_of(seq, q_place)
        kind = jnp.where(whole, 0, jnp.where(empty, 2, 1))
        return q_tile, k_tile, kind, (seq, q_place, k_place)

    def allowed(self, at, query_axis, shape):
        seq, q_place, k_place = at
        query = q_place + lax.broadcasted_iota(jnp.int32, shape, query_axis) % self.blk
        key = k_place + lax.broadcasted_iota(jnp.int32, shape, 1 - query_axis)
        return (key <= query) & (key >= self.start_of(seq, query))

    def run(self, tile):
        def body(row, carry):
            q_tile, k_tile, kind, at = self.pair(row)
            keys = pl.ds(pl.multiple_of(k_tile * self.blk, self.blk), self.blk)
            pl.when(kind == 0)(lambda: tile(q_tile, keys, None))
            pl.when(kind == 1)(lambda: tile(q_tile, keys, functools.partial(self.allowed, at)))
            return carry

        lax.fori_loop(0, self.rows, body, 0)


def load_chunks(chunks, kv_ref):
    at = 0
    for chunk in chunks:
        for part in [chunk] if len(chunk.shape) == 2 else [chunk.at[0], chunk.at[1]]:
            kv_ref[at : at + part.shape[0]] = part[...]
            at += part.shape[0]


def forward_kernel(make, parts, heads, order_ref, starts_ref, q_ref, *refs):
    chunks, held, (out_ref, kv_ref) = refs[:parts], refs[parts:-2], refs[-2:]
    tiles = make(order_ref, starts_ref)
    blk = tiles.blk
    first = lax.broadcasted_iota(jnp.int32, (blk, LANES), 1) < HEAD_SIZE
    load_chunks(chunks, kv_ref)
    out_ref[...] = held[0][...] if held else jnp.zeros_like(out_ref)

    def tile(q_tile, keys, mask):
        if mask is not None:
            allowed = mask(0, (q_ref.shape[2], blk))
        for h in range(heads):
            kv = kv_ref[keys, h * LANES : (h + 1) * LANES]
            scores = lax.dot_general(q_ref[h, q_tile], kv, NT, preferred_element_type=f32)
            weights = jnp.exp2(scores * LOG2E)
            if mask is not None:
                weights = jnp.where(allowed, weights, 0.0)
            one_v = jnp.where(first, jnp.ones_like(kv), kv)
            out_ref[h, q_tile] += jnp.dot(weights.astype(bf16), one_v, preferred_element_type=f32)

    tiles.run(tile)


def backward_kernel(make, parts, held, heads, order_ref, starts_ref, q_ref, do_ref, stat_ref, *refs):
    chunks, held, refs = refs[:parts], refs[parts : parts + held], refs[parts + held :]
    dq_ref, keep_ref, give_ref, kv_ref, dkv_ref = refs
    tiles = make(order_ref, starts_ref)
    blk = tiles.blk
    load_chunks(chunks, kv_ref)
    dq_ref[...] = held[0][...] if held else jnp.zeros_like(dq_ref)
    dkv_ref[...] = jnp.zeros_like(dkv_ref)

    def tile(q_tile, keys, mask):
        if mask is not None:
            allowed = mask(1, (blk, q_ref.shape[2]))
        for h in range(heads):
            cols = slice(h * LANES, (h + 1) * LANES)
            kv = kv_ref[keys, cols]
            q = q_ref[h, q_tile]
            do = do_ref[h, q_tile]
            scores = lax.dot_general(kv, q, NT, preferred_element_type=f32)
            back_probs = lax.dot_general(kv, do, NT, preferred_element_type=f32)
            probs = jnp.exp2(scores * LOG2E - stat_ref[h, q_tile, 0:1])
            if mask is not None:
                probs = jnp.where(allowed, probs, 0.0)
            back_scores = (probs * (back_probs - stat_ref[h, q_tile, 1:2])).astype(bf16)
            both = jnp.concatenate([probs.astype(bf16), back_scores], axis=1)
            dkv_ref[keys, cols] += jnp.dot(
                both, jnp.concatenate([do, q], axis=0), preferred_element_type=f32
            )
            dq_ref[h, q_tile] += jnp.dot(kv.T[:HEAD_SIZE], back_scores, preferred_element_type=f32)

    tiles.run(tile)
    rows = keep_ref.shape[-2]
    if len(keep_ref.shape) == 2:
        keep_ref[...] = dkv_ref[:rows]
        give_ref[...] = dkv_ref[rows:].astype(bf16)
        return
    for c in (0, 1):
        keep_ref[c] = dkv_ref[(3 - c) * rows : (4 - c) * rows]
        give_ref[c] = dkv_ref[(1 - c) * rows : (2 - c) * rows].astype(bf16)


def in_smem():
    return pl.BlockSpec(memory_space=pltpu.SMEM)


def in_vmem():
    return pl.BlockSpec(memory_space=pltpu.VMEM)


class Attention:
    def __init__(self, ring, block_order, starts, blk):
        self.ring, self.order, self.starts = ring, block_order, starts
        self.blk, self.seq_count = blk, starts.shape[0]

    def _make(self, slots):
        return lambda order_ref, starts_ref: Tiles(
            self.ring, slots, self.seq_count, self.blk, order_ref, starts_ref
        )

    def _cost(self, slots, heads, products, arrays):
        tile = 2 * self.blk * self.blk * heads * pair_count(slots, self.seq_count)
        return pl.CostEstimate(
            flops=2 * tile * 256 * products // COST_SCALE,
            bytes_accessed=sum(x.size * x.dtype.itemsize for x in arrays) // COST_SCALE,
            transcendentals=tile // COST_SCALE,
        )

    def forward(self, pieces, q, acc):
        heads, tiles, rows, _ = q.shape
        out = jax.ShapeDtypeStruct((heads, tiles, rows, LANES), f32)
        held = [] if acc is None else [acc]
        slots, chunks = [x for xs, _ in pieces for x in xs], [x for _, x in pieces]
        keys, width = len(slots) * chunks[0].shape[-2], chunks[0].shape[-1]
        return pl.pallas_call(
            functools.partial(forward_kernel, self._make(slots), len(chunks), heads),
            out_shape=out,
            in_specs=[in_smem()] * 2 + [in_vmem()] * (1 + len(chunks) + len(held)),
            out_specs=in_vmem(),
            scratch_shapes=[pltpu.VMEM((keys, width), bf16)],
            compiler_params=pltpu.CompilerParams(vmem_limit_bytes=VMEM_BYTES),
            cost_estimate=self._cost(slots, heads, 2, [q, *chunks, out, out]),
            name="attend_forward",
        )(self.order, self.starts, q, *chunks, *held)

    def backward(self, pieces, q, do, stats, acc):
        heads, tiles, rows, _ = q.shape
        slots, chunks = [x for xs, _ in pieces for x in xs], [x for _, x in pieces]
        keys, width = len(slots) * chunks[0].shape[-2], chunks[0].shape[-1]
        outs = [
            jax.ShapeDtypeStruct((heads, tiles, HEAD_SIZE, rows), f32),
            jax.ShapeDtypeStruct(chunks[0].shape, f32),
            jax.ShapeDtypeStruct(chunks[0].shape, bf16),
        ]
        held = [] if acc is None else [acc]
        return pl.pallas_call(
            functools.partial(
                backward_kernel, self._make(slots), len(chunks), len(held), heads
            ),
            out_shape=outs,
            in_specs=[in_smem()] * 2 + [in_vmem()] * (3 + len(chunks) + len(held)),
            out_specs=[in_vmem()] * len(outs),
            scratch_shapes=[pltpu.VMEM((keys, width), bf16), pltpu.VMEM((keys, width), f32)],
            compiler_params=pltpu.CompilerParams(vmem_limit_bytes=VMEM_BYTES),
            cost_estimate=self._cost(slots, heads, 5, [q, do, outs[0], *chunks, *outs]),
            name="attend_backward",
        )(self.order, self.starts, q, do, stats, *chunks, *held)


def grads_kernel(ring, two_ref, gate_ref, up_ref, ffn_ref, cot_ref, *refs):
    outs, (lhs_ref, all_ref) = refs[:-2], refs[-2:]

    @pl.when(pl.program_id(0) == 0)
    def _():
        lhs_ref[...] = two_ref[...].T

    n = ring.n
    unit = lhs_ref.shape[0] // (2 * n)
    cols = gate_ref.shape[1]
    thin = cols // (2 * n)
    for i, ref in enumerate((gate_ref, up_ref)):
        grad = jnp.dot(lhs_ref[...], ref[...], preferred_element_type=f32).astype(bf16)
        all_ref[:, i * unit : (i + 1) * unit] = grad.reshape(2 * n, unit, cols)
    down = jnp.dot(ffn_ref[...].T, cot_ref[...], preferred_element_type=f32).astype(bf16)
    down = down.reshape(2 * n, thin, down.shape[1])
    for k in range(down.shape[2] // cols):
        at = 2 * unit + k * thin
        all_ref[:, at : at + thin] = down[:, :, k * cols : (k + 1) * cols]
    deal(ring, lambda at: all_ref[at], lambda ref, x: ref.at[0].__setitem__(..., x), outs)


def deal(ring, read, write, outs):
    far = ring.n // 2

    def part(distance, other):
        place, core = ring.at((distance, other))
        return read(core * ring.n + place)

    keep_far, give_far, *keep, give = outs
    write(keep_far, part(far, 0))
    write(give_far, part(far, 1))
    write(keep[0], part(0, 0))
    write(give.at[0], part(0, 1))
    for d in range(1, far):
        for c in (0, 1):
            write(keep[d].at[c], part(d, c))
            write(give.at[2 * d - 1 + c], part(-d, 1 - c))


def dealt(ring, cut):
    far = ring.n // 2
    heads = [(), (), ()] + [(2,)] * (far - 1) + [(2 * far - 1,)]
    return [jax.ShapeDtypeStruct((*head, *cut.shape), cut.dtype) for head in heads]


def dealt_terms(ring, outs):
    far = ring.n // 2
    keep_far, give_far, *keep, give = outs
    got_far = ring.sibling(give_far)
    give, got_far = lax.optimization_barrier((give, got_far))
    got = ring.sibling(give)

    def terms(d):
        if d == far:
            return [keep_far, got_far]
        if d == 0:
            return [keep[0], got[0]]
        return [keep[d], got[2 * d - 1 : 2 * d + 1]]

    return terms


def ffn_grads(ring, hidden_two, back_gate, back_up, hidden_ffn, cotangent):
    rows, width = hidden_two.shape
    units = back_gate.shape[1]
    n = ring.n
    wide = width // (2 * n) * 3
    cols = 256
    whole = pl.BlockSpec((rows, width), lambda j: (0, 0))
    block = pl.BlockSpec((rows, cols), lambda j: (0, j))
    outs = dealt(ring, shape(units // cols, wide, cols, dtype=bf16))
    cuts = [
        pl.BlockSpec(
            (*x.shape[:-3], 1, wide, cols), lambda j, k=len(x.shape): (0,) * (k - 3) + (j, 0, 0)
        )
        for x in outs
    ]
    return pl.pallas_call(
        functools.partial(grads_kernel, ring),
        grid=(units // cols,),
        out_shape=outs,
        in_specs=[whole, block, block, block, whole],
        out_specs=cuts,
        scratch_shapes=[pltpu.VMEM((width, rows), bf16), pltpu.VMEM((2 * n, wide, cols), bf16)],
        compiler_params=pltpu.CompilerParams(vmem_limit_bytes=VMEM_BYTES),
        cost_estimate=pl.CostEstimate(
            flops=6 * rows * width * units // COST_SCALE, bytes_accessed=2**20, transcendentals=0
        ),
        name="ffn_grads",
    )(hidden_two, back_gate, back_up, hidden_ffn, cotangent)


def place_kernel(ring, slots, count, *refs):
    arrays, outs, (wide_ref, down_ref, sem) = refs[:count], refs[-6:-3], refs[-3:]
    parts = [y for x in arrays for y in ([x] if len(x.shape) == 3 else [x.at[0], x.at[1]])]
    n = ring.n
    blocks, _, cols = parts[0].shape
    unit = outs[0].shape[0] // (2 * n)
    thin = cols // (2 * n)
    copies = []
    for i, slot in enumerate(slots):
        part = parts[i]
        place, core = ring.at(slot)
        r = core * n + place
        for w in range(2):
            for j in range(blocks):
                wide_ref[i, w, :, j * cols : (j + 1) * cols] = part[
                    j, w * unit : (w + 1) * unit
                ].astype(f32)
            rows = pl.ds(pl.multiple_of(r * unit, unit), unit)
            copies.append((wide_ref.at[i, w], outs[w].at[rows]))
        for j in range(blocks):
            for k in range(outs[2].shape[1] // cols):
                at = 2 * unit + k * thin
                down_ref[i, j, :, k * cols : (k + 1) * cols] = part[j, at : at + thin].astype(f32)
            rows = pl.ds(pl.multiple_of(j * cols + r * thin, thin), thin)
            copies.append((down_ref.at[i, j], outs[2].at[rows]))
        for k in range(i * (2 + blocks), (i + 1) * (2 + blocks)):
            pltpu.make_async_copy(*copies[k], sem.at[k]).start()
    for k, pair in enumerate(copies):
        pltpu.make_async_copy(*pair, sem.at[k]).wait()


def place_ffn(ring, pieces, width, held):
    slots, parts = [x for xs, _ in pieces for x in xs], [x for _, x in pieces]
    blocks, wide, cols = parts[0].shape[-3:]
    units = blocks * cols
    count = len(slots)
    thin = cols // (2 * ring.n)
    anywhere = pl.BlockSpec(memory_space=pl.ANY)
    return pl.pallas_call(
        functools.partial(place_kernel, ring, slots, len(parts)),
        out_shape=[shape(width, units), shape(width, units), shape(units, width)],
        in_specs=[in_vmem()] * len(parts) + [anywhere] * len(held),
        out_specs=[anywhere] * 3,
        input_output_aliases={len(parts) + i: i for i in range(len(held))},
        scratch_shapes=[
            pltpu.VMEM((count, 2, width // (2 * ring.n), units), f32),
            pltpu.VMEM((count, blocks, thin, width), f32),
            pltpu.SemaphoreType.DMA((count * (2 + blocks),)),
        ],
        compiler_params=pltpu.CompilerParams(vmem_limit_bytes=VMEM_BYTES),
        cost_estimate=pl.CostEstimate(
            flops=0, bytes_accessed=8 * count * wide * units, transcendentals=0
        ),
        name="place_ffn",
    )(*parts, *held)


def place_qkv_kernel(ring, slots, *refs):
    arrays, (query_ref, key_ref, value_ref, out_ref) = refs[:-4], refs[-4:]
    parts = [y for x in arrays for y in ([x] if len(x.shape) == 2 else [x.at[0], x.at[1]])]
    n = ring.n
    unit, thin = query_ref.shape[0] // (2 * n), out_ref.shape[0] // (2 * n)
    for slot, part in zip(slots, parts):
        place, core = ring.at(slot)
        r = core * n + place
        rows = pl.ds(pl.multiple_of(r * unit, unit), unit)
        at = query_ref.shape[1]
        query_ref[rows] = part[:unit, :at].astype(f32)
        for h in range(key_ref.shape[1] // HEAD_SIZE):
            cols = slice(h * HEAD_SIZE, (h + 1) * HEAD_SIZE)
            both = part[:unit, at + h * LANES : at + (h + 1) * LANES].astype(f32)
            key_ref[rows, cols] = both[:, :HEAD_SIZE]
            value_ref[rows, cols] = both[:, HEAD_SIZE:]
        rows = pl.ds(pl.multiple_of(r * thin, thin), thin)
        out_ref[rows] = part[unit:].astype(f32)


def place_qkv(ring, pieces, width, cols):
    slots, parts = [x for xs, _ in pieces for x in xs], [x for _, x in pieces]
    thin = parts[0].shape[-2] - width // (2 * ring.n)
    return whole_call(
        functools.partial(place_qkv_kernel, ring, slots),
        "place_qkv",
        [shape(width, c) for c in cols] + [shape(thin * 2 * ring.n, width)],
        parts,
        0,
    )


def whole_call(kernel, name, outs, args, flops, scratch=(), scalars=(0, 0)):
    moved = sum(x.size * x.dtype.itemsize for x in (*outs, *args))
    return pl.pallas_call(
        kernel,
        out_shape=list(outs),
        in_specs=[in_smem()] * scalars[0] + [in_vmem()] * (len(args) - scalars[0]),
        out_specs=[in_smem()] * scalars[1] + [in_vmem()] * (len(outs) - scalars[1]),
        scratch_shapes=list(scratch),
        compiler_params=pltpu.CompilerParams(vmem_limit_bytes=VMEM_BYTES),
        cost_estimate=pl.CostEstimate(
            flops=flops // COST_SCALE, bytes_accessed=moved // COST_SCALE, transcendentals=0
        ),
        name=name,
    )(*args)


def shape(*dims, dtype=f32):
    return jax.ShapeDtypeStruct(dims, dtype)


def first_lanes(rows):
    return lax.broadcasted_iota(jnp.int32, (rows, LANES), 1) < HEAD_SIZE


def head_mean(x):
    i = lax.broadcasted_iota(jnp.int32, (LANES, LANES), 0) // HEAD_SIZE
    j = lax.broadcasted_iota(jnp.int32, (LANES, LANES), 1) // HEAD_SIZE
    mean = jnp.where(i == j, 1.0 / HEAD_SIZE, 0.0).astype(bf16)
    high = x.astype(bf16)
    low = (x - high.astype(f32)).astype(bf16)
    return jnp.dot(high, mean, preferred_element_type=f32) + jnp.dot(
        low, mean, preferred_element_type=f32
    )


def turn(x, cosine, sines):
    lane = lax.broadcasted_iota(jnp.int32, x.shape, 1) % HEAD_SIZE
    half = HEAD_SIZE // 2
    other = jnp.where(
        lane < half, pltpu.roll(x, LANES - half, axis=1), pltpu.roll(x, half, axis=1)
    )
    return x * cosine + other * sines


def row_scale(x):
    return lax.rsqrt(jnp.mean(x * x, axis=-1, keepdims=True) + EPSILON)


def norm_back(upstream, x, scale, gain):
    inner = upstream * gain
    return scale * (inner - x * (scale * scale * jnp.mean(inner * x, axis=-1, keepdims=True)))


def head_norm_back(upstream, x, gain):
    scale = lax.rsqrt(head_mean(x * x) + EPSILON)
    inner = upstream * gain
    back = scale * (inner - x * (scale * scale * head_mean(inner * x)))
    return back, jnp.sum(upstream * x * scale, axis=0, keepdims=True)


def lanes(tile):
    return slice(tile * LANES, (tile + 1) * LANES)


def project_kv_kernel(
    tiles, last, order, segments, tokens, gain, w_key, w_value, key_gain, inverse, *refs
):
    starts, hidden, kv_raw, kv, w_kv, cosine, sines = refs
    x = tokens[...].astype(f32)
    hidden[...] = (x * row_scale(x) * gain[...]).astype(bf16)
    rows = x.shape[0]
    blk = rows // tiles
    mine = order[lax.axis_index("ctx")]
    lane = lax.broadcasted_iota(jnp.int32, (blk, LANES), 1) % HEAD_SIZE
    for t in range(tiles):
        block = last - mine if t % 2 else mine
        place = block * blk + lax.broadcasted_iota(jnp.int32, (blk, LANES), 0)
        angles = place.astype(f32) * inverse[...]
        at = slice(t * blk, (t + 1) * blk)
        cosine[at] = jnp.cos(angles)
        sine = jnp.sin(angles)
        sines[at] = jnp.where(lane < HEAD_SIZE // 2, -sine, sine)
    first = first_lanes(rows)
    for h in range(kv.shape[1] // LANES):
        cols = slice(h * HEAD_SIZE, (h + 1) * HEAD_SIZE)
        w_kv[:, lanes(h)] = jnp.concatenate([w_key[:, cols], w_value[:, cols]], axis=1)
        raw = jnp.dot(hidden[...], w_kv[:, lanes(h)], preferred_element_type=f32)
        kv_raw[:, lanes(h)] = raw
        normed = raw * lax.rsqrt(head_mean(raw * raw) + EPSILON) * key_gain[...]
        kv[:, lanes(h)] = jnp.where(first, turn(normed, cosine[...], sines[...]), raw).astype(bf16)
    for seq in range(segments.shape[0]):
        for d in range(3):
            before = jnp.where(segments[seq : seq + 1] <= d, 1.0, 0.0)
            starts[seq, d] = jnp.sum(before).astype(jnp.int32)


def project_q_kernel(tiles, hidden, w_query, query_gain, cosine, sines, query_raw, q_tiles):
    rows = hidden.shape[0]
    blk = rows // tiles
    first = first_lanes(rows)
    for h in range(q_tiles.shape[0]):
        raw = jnp.dot(hidden[...], w_query[:, lanes(h)], preferred_element_type=f32)
        query_raw[:, lanes(h)] = raw
        normed = raw * lax.rsqrt(head_mean(raw * raw) + EPSILON) * query_gain[...]
        turned = turn(normed, cosine[...], sines[...]).astype(bf16).astype(f32) * 0.125
        pair = [
            jnp.where(first, turned, 0.0),
            jnp.where(first, pltpu.roll(turned, HEAD_SIZE, axis=1), 0.0),
        ]
        for g, one in enumerate(pair):
            for t in range(tiles):
                q_tiles[h, t, g * blk : (g + 1) * blk] = one[t * blk : (t + 1) * blk].astype(bf16)


def mix_kernel(acc, w_out, *refs):
    attended, o, lse, halves = refs[0], refs[1], refs[2], refs[3:]
    heads, tiles, rows, _ = acc.shape
    blk = rows // 2
    first = first_lanes(rows)
    for h in range(heads):
        for t in range(tiles):
            x = acc[h, t]
            value = jnp.where(first, 0.0, x * pltpu.roll(1.0 / x, HEAD_SIZE, axis=1))
            o[h, t] = value
            lse[h, t] = jnp.log2(x.T[:8])
            low = pltpu.roll(value[:blk], HEAD_SIZE, axis=1) + value[blk:]
            attended[t * blk : (t + 1) * blk, lanes(h)] = low.astype(bf16)
    part = attended.shape[0] // len(halves)
    for i, half in enumerate(halves):
        half[...] = jnp.dot(
            attended[i * part : (i + 1) * part], w_out[...], preferred_element_type=f32
        ).astype(bf16)


def ffn_kernel(
    terms,
    tokens,
    gain,
    hidden_back,
    w_gate,
    w_up,
    *refs,
):
    mine, theirs, refs = refs[:terms], refs[terms : 2 * terms], refs[2 * terms :]
    mixed, hidden_two, hidden_ffn, back_gate, back_up, gain_grad = refs[:6]
    halves, sums = refs[6:-1], refs[-1]
    step, last = pl.program_id(0), pl.num_programs(0) - 1

    @pl.when(step == 0)
    def _():
        part = tokens.shape[0] // terms
        for i in range(terms):
            rows = slice(i * part, (i + 1) * part)
            x = tokens[rows].astype(f32) + (mine[i][...].astype(f32) + theirs[i][...].astype(f32))
            mixed[rows] = x
            hidden_two[rows] = (x * row_scale(x) * gain[...]).astype(bf16)
        sums[...] = jnp.zeros_like(sums)

    gating = jnp.dot(hidden_two[...], w_gate[...], preferred_element_type=f32)
    lifted = jnp.dot(hidden_two[...], w_up[...], preferred_element_type=f32)
    upstream = hidden_back[...]
    logistic = jax.nn.sigmoid(gating)
    silu = gating * logistic
    hidden_ffn[...] = (silu * lifted).astype(bf16)
    back_gate[...] = (
        upstream * lifted * logistic * (1.0 + gating * (1.0 - logistic))
    ).astype(bf16)
    back_up[...] = (upstream * silu).astype(bf16)
    sums[...] += lax.dot_general(
        back_gate[...], w_gate[...], NT, preferred_element_type=f32
    ) + lax.dot_general(back_up[...], w_up[...], NT, preferred_element_type=f32)

    @pl.when(step == last)
    def _():
        x = mixed[...]
        gain_grad[...] = jnp.sum(sums[...] * x * row_scale(x), axis=0, keepdims=True)
        part = sums.shape[0] // len(halves)
        for i, half in enumerate(halves):
            half[...] = sums[i * part : (i + 1) * part].astype(bf16)


def feed_forward(tokens, gain, hidden_back, w_gate, w_up, mine, theirs):
    rows, width = tokens.shape
    units = w_gate.shape[1]
    cols = FFN_COLS if units % FFN_COLS == 0 else units
    whole = pl.BlockSpec((rows, width), lambda j: (0, 0))
    line = pl.BlockSpec((1, width), lambda j: (0, 0))
    block = pl.BlockSpec((rows, cols), lambda j: (0, j))
    weight = pl.BlockSpec((width, cols), lambda j: (0, j))
    part = pl.BlockSpec((rows // len(mine), width), lambda j: (0, 0))
    half = pl.BlockSpec((rows // 2, width), lambda j: (0, 0))
    low = shape(rows, units, dtype=bf16)
    return pl.pallas_call(
        functools.partial(ffn_kernel, len(mine)),
        grid=(units // cols,),
        out_shape=[shape(rows, width), shape(rows, width, dtype=bf16), low, low, low]
        + [shape(1, width)]
        + [shape(rows // 2, width, dtype=bf16)] * 2,
        in_specs=[whole, line, block, weight, weight] + [part] * (2 * len(mine)),
        out_specs=[whole, whole, block, block, block, line, half, half],
        scratch_shapes=[pltpu.VMEM((rows, width), f32)],
        compiler_params=pltpu.CompilerParams(vmem_limit_bytes=VMEM_BYTES),
        cost_estimate=pl.CostEstimate(
            flops=8 * rows * width * units // COST_SCALE, bytes_accessed=2**20, transcendentals=0
        ),
        name="feed_forward",
    )(tokens, gain, hidden_back, w_gate, w_up, *mine, *theirs)


def back_kernel(terms, cotangent, mixed, gain, w_out, o, lse, *refs):
    mine, theirs, (back_mixed, back_proj, do_tiles, stats) = (
        refs[:terms],
        refs[terms : 2 * terms],
        refs[2 * terms :],
    )
    part = cotangent.shape[0] // terms
    for i in range(terms):
        rows = slice(i * part, (i + 1) * part)
        x = mixed[rows]
        upstream = mine[i][...].astype(f32) + theirs[i][...].astype(f32)
        back = cotangent[rows].astype(f32) + norm_back(upstream, x, row_scale(x), gain[...])
        back_mixed[rows] = back
        back_proj[rows] = back.astype(bf16)
    heads, tiles, rows, _ = o.shape
    blk = rows // 2
    first = first_lanes(blk)
    row = lax.broadcasted_iota(jnp.int32, (8, rows), 0)
    for h in range(heads):
        attn = lax.dot_general(back_proj[...], w_out[lanes(h)], NT, preferred_element_type=f32)
        for t in range(tiles):
            here = attn[t * blk : (t + 1) * blk]
            do = jnp.concatenate(
                [
                    jnp.where(first, 0.0, pltpu.roll(here, HEAD_SIZE, axis=1)),
                    jnp.where(first, 0.0, here),
                ],
                axis=0,
            ).astype(bf16)
            do_tiles[h, t] = do
            delta = jnp.sum((do.astype(f32) * o[h, t]).T, axis=0, keepdims=True)
            stats[h, t] = jnp.where(row == 0, lse[h, t], delta)


def back_query_kernel(dq, query_raw, query_gain, cosine, sines, query_delta, gain_grad):
    heads, tiles, _, rows = dq.shape
    blk = rows // 2
    gain_grad[...] = jnp.zeros_like(gain_grad)
    for t in range(tiles):
        at = slice(t * blk, (t + 1) * blk)
        for h in range(heads):
            both = jnp.concatenate([dq[h, t, :, :blk], dq[h, t, :, blk:]], axis=0) * 0.125
            turned = turn(both.T, cosine[at], -sines[at])
            back, gain_terms = head_norm_back(turned, query_raw[at, lanes(h)], query_gain[...])
            query_delta[at, lanes(h)] = back.astype(bf16)
            gain_grad[...] += gain_terms


def back_project_kernel(
    ring,
    tokens,
    hidden,
    query_delta,
    own_dkv,
    kv_raw,
    key_gain,
    cosine,
    sines,
    w_query,
    w_kv,
    attended,
    back_proj,
    *refs,
):
    low, norm_grad, gain_grad, kv_delta = refs[:4]
    outs, all_ref = refs[4:-1], refs[-1]
    rows, width = tokens.shape
    first = first_lanes(rows)
    gain_grad[...] = jnp.zeros_like(gain_grad)
    for h in range(own_dkv.shape[1] // LANES):
        dkv = own_dkv[:, lanes(h)].astype(f32)
        turned = turn(dkv, cosine[...], -sines[...])
        back, gain_terms = head_norm_back(turned, kv_raw[:, lanes(h)], key_gain[...])
        kv_delta[:, lanes(h)] = jnp.where(first, back, dkv).astype(bf16)
        gain_grad[...] += gain_terms
    part = lax.dot_general(
        query_delta[...], w_query[...], NT, preferred_element_type=f32
    ) + lax.dot_general(kv_delta[...], w_kv[...], NT, preferred_element_type=f32)
    low[...] = part.astype(bf16)
    x = tokens[...].astype(f32)
    norm_grad[...] = jnp.sum(part * x * row_scale(x), axis=0, keepdims=True)
    if not outs:
        return
    lhs = hidden[...].T
    n = ring.n
    unit = width // (2 * n)
    q_cols = query_delta.shape[1]
    for cols, right in (
        (slice(0, q_cols), query_delta),
        (slice(q_cols, q_cols + kv_delta.shape[1]), kv_delta),
    ):
        grad = jnp.dot(lhs, right[...], preferred_element_type=f32).astype(bf16)
        all_ref[:, :unit, cols] = grad.reshape(2 * n, unit, grad.shape[1])
    grad = jnp.dot(attended[...].T, back_proj[...], preferred_element_type=f32).astype(bf16)
    all_ref[:, unit:] = grad.reshape(2 * n, -1, width)
    deal(ring, lambda at: all_ref[at], lambda ref, x: ref.__setitem__(..., x), outs)


def dot(a, b, dims):
    return lax.dot_general(a, b, ((dims[:1], dims[1:]), ((), ())), preferred_element_type=f32)


def on_device(
    tokens,
    cotangent,
    block_order,
    segment_ids,
    norm_gain,
    w_query,
    key_weight,
    value_weight,
    query_gain,
    key_gain,
    w_out,
    ffn_gain,
    w_gate,
    w_up,
    w_down,
):
    devices = lax.axis_size("ctx")
    ring = Ring(devices)
    far = ring.n // 2
    rows, width = tokens.shape
    seq_count = segment_ids.shape[0]
    blk = rows // seq_count // 2
    tiles = 2 * seq_count
    kv_heads = key_weight.shape[1] // HEAD_SIZE
    q_cols, k_cols = w_query.shape[1], key_weight.shape[1]
    units = w_gate.shape[1]
    packed = units % 256 == 0 and width % (32 * ring.n) == 0 and w_out.shape[0] % (32 * ring.n) == 0
    pair = lax.axis_size("tp") == 2

    def shared(halves):
        if pair:
            return from_other(halves), list(halves)
        return [lax.psum(x, "tp") for x in halves], [jnp.zeros_like(x) for x in halves]

    def line(x):
        return x.astype(f32).reshape(1, -1)

    def head_line(x):
        return jnp.tile(line(x), (1, 2))

    inverse = ROPE_BASE ** (-np.arange(0, HEAD_SIZE, 2) / HEAD_SIZE)
    inverse = np.tile(inverse, 4)[None, :].astype(np.float32)
    starts, hidden_input, kv_raw, own_kv, w_kv, cosine, sines = whole_call(
        functools.partial(project_kv_kernel, tiles, 2 * devices - 1),
        "project_kv",
        [
            shape(seq_count, 3, dtype=jnp.int32),
            shape(rows, width, dtype=bf16),
            shape(rows, 2 * k_cols),
            shape(rows, 2 * k_cols, dtype=bf16),
            shape(width, 2 * k_cols, dtype=bf16),
            shape(rows, LANES),
            shape(rows, LANES),
        ],
        [
            block_order,
            segment_ids,
            tokens,
            line(norm_gain),
            key_weight,
            value_weight,
            head_line(key_gain),
            jnp.asarray(inverse),
        ],
        4 * rows * width * k_cols,
        scalars=(1, 1),
    )
    gather = RingGather(ring, own_kv)
    flying = gather.send(gather.sends())
    query_raw, q_tiles = whole_call(
        functools.partial(project_q_kernel, tiles),
        "project_q",
        [shape(rows, q_cols), shape(kv_heads, tiles, 2 * blk, LANES, dtype=bf16)],
        [hidden_input, w_query, head_line(query_gain), cosine, sines],
        2 * rows * width * q_cols,
    )

    attention = Attention(ring, block_order, starts, blk)
    acc = attention.forward(gather.pieces[:1], q_tiles, None)
    late = gather.pieces[1]
    while True:
        *came, acc = lax.optimization_barrier((*flying, acc))
        now = gather.arrive(came)
        if gather.done():
            break
        flying = gather.send(gather.sends())
        acc = attention.forward([late, *now], q_tiles, acc)
        late = gather.pieces[-1]
        if gather.step == far:
            acc = attention.forward([late], q_tiles, acc)
    acc = attention.forward(gather.pieces[-2:], q_tiles, acc)
    kv_pieces = {
        max(abs(d) for d, _ in slots): gather.pieces[i - 1 : i + 1]
        for i, (slots, _) in enumerate(gather.pieces)
        if i % 2
    }
    attended, o, lse, *mix_halves = whole_call(
        mix_kernel,
        "mix",
        [
            shape(rows, q_cols, dtype=bf16),
            shape(*acc.shape),
            shape(kv_heads, tiles, 8, 2 * blk),
            shape(rows // 2, width, dtype=bf16),
            shape(rows // 2, width, dtype=bf16),
        ],
        [acc, w_out],
        2 * rows * width * q_cols,
    )
    theirs, mine = shared(mix_halves)
    back_hidden = dot(cotangent, w_down, (1, 1))
    back_hidden, *theirs = lax.optimization_barrier((back_hidden, *theirs))

    mixed, hidden_two, hidden_ffn, back_gate, back_up, grad_ffn_gain, *halves = feed_forward(
        tokens, line(ffn_gain), back_hidden, w_gate, w_up, mine, theirs
    )
    if packed:
        first, mine_first = shared(halves[:1])
        dealt_out = ffn_grads(ring, hidden_two, back_gate, back_up, hidden_ffn, cotangent)
        second, first[0], *dealt_out = lax.optimization_barrier((halves[1], first[0], *dealt_out))
        second, mine_second = shared([second])
        hidden_ffn, dealt_out[0] = lax.optimization_barrier((hidden_ffn, dealt_out[0]))
        output_part = dot(hidden_ffn, w_down, (1, 0)).astype(bf16)
        ffn_box = []
        ffn_sum = Steps(sum_steps(ring, dealt_terms(ring, dealt_out), ffn_box))
        advance([ffn_sum])
        *theirs, output_part = advance([ffn_sum], first[0], second[0], output_part)
        mine = mine_first + mine_second
    else:
        theirs, mine = shared(halves)
        grad_w_down = dot(hidden_ffn, cotangent, (0, 0)).astype(bf16)
        grad_w_gate = dot(hidden_two, back_gate, (0, 0)).astype(bf16)
        grad_w_up = dot(hidden_two, back_up, (0, 0)).astype(bf16)
        grad_w_gate, grad_w_up, grad_w_down = sum_over_ctx(
            ring, [grad_w_gate, grad_w_up, grad_w_down]
        )
        ffn_sum = None
        output_part = dot(hidden_ffn, w_down, (1, 0)).astype(bf16)
    back_mixed, back_proj, do_tiles, stats = whole_call(
        functools.partial(back_kernel, 2),
        "back",
        [
            shape(rows, width),
            shape(rows, width, dtype=bf16),
            shape(*q_tiles.shape, dtype=bf16),
            shape(*lse.shape),
        ],
        [cotangent, mixed, line(ffn_gain), w_out, o, lse, *mine, *theirs],
        2 * rows * width * q_cols,
    )
    output_swap = Steps(exchange_steps(output_part)) if pair else None
    dq = None
    terms = {}

    dkv_sum = Steps(sum_steps(ring, lambda d: terms[d]))
    for d in range(far, -1, -1):
        if d < far:
            chains = [ffn_sum, dkv_sum if d < far - 1 else None]
            if d == 0:
                chains.append(output_swap)
            do_tiles, dq = advance(chains, do_tiles, dq)
        dq, keep, give = attention.backward(kv_pieces[d], q_tiles, do_tiles, stats, dq)
        terms[d] = [keep, ring.sibling(give)]
    placed, done = [], 0
    (dq,) = advance([None if LATE else ffn_sum, dkv_sum], dq)
    query_delta, grad_query_gain = whole_call(
        back_query_kernel,
        "back_query",
        [shape(rows, q_cols, dtype=bf16), shape(1, LANES)],
        [dq, query_raw, head_line(query_gain), cosine, sines],
        2 * rows * width,
    )
    if packed:
        placed, done = place_ffn(ring, ffn_box[0].pieces[:4], width, []), 4
    query_delta, *placed = advance([dkv_sum], query_delta, *placed)
    own_dkv = dkv_sum.result
    wide = width // (2 * ring.n) + w_out.shape[0] // (2 * ring.n)
    one_low, grad_norm_gain, grad_key_gain, kv_delta, *cuts = whole_call(
        functools.partial(back_project_kernel, ring),
        "back_project",
        [
            shape(rows, width, dtype=bf16),
            shape(1, width),
            shape(1, LANES),
            shape(rows, 2 * k_cols, dtype=bf16),
        ]
        + (dealt(ring, shape(wide, width, dtype=bf16)) if packed else []),
        [
            tokens,
            hidden_input,
            query_delta,
            own_dkv,
            kv_raw,
            head_line(key_gain),
            cosine,
            sines,
            w_query,
            w_kv,
            attended,
            back_proj,
        ],
        4 * rows * width * (q_cols + 2 * k_cols),
        [pltpu.VMEM((2 * ring.n, wide, width), bf16)],
    )

    gains = jnp.concatenate(
        [
            grad_norm_gain[0],
            grad_ffn_gain[0],
            grad_query_gain[0, :HEAD_SIZE] + grad_query_gain[0, HEAD_SIZE:],
            grad_key_gain[0, :HEAD_SIZE],
        ]
    )
    gain_sum = Steps(pair_steps(gains, [("tp", lax.axis_size("tp")), ("ctx", devices)]))
    one_swap = Steps(exchange_steps(one_low)) if pair else None
    if packed:
        qkv_box = []
        qkv_sum = Steps(sum_steps(ring, dealt_terms(ring, cuts), qkv_box))
        gather = ffn_box[0]
        round_at = 0
        while qkv_sum.generator is not None:
            came = len(gather.pieces)
            chains = [ffn_sum if round_at % 2 == 0 else None, qkv_sum, gain_sum]
            if round_at == 0:
                chains.append(output_swap)
            elif round_at in (1, 4):
                chains.append(one_swap)
            placed = advance(chains, *placed)
            if came > done:
                placed = place_ffn(ring, gather.pieces[done:came], width, placed)
                done = came
            round_at += 1
        if done < len(gather.pieces):
            placed = place_ffn(ring, gather.pieces[done:], width, placed)
        grad_w_gate, grad_w_up, grad_w_down = placed
        grad_w_query, grad_w_key, grad_w_value, grad_w_out = place_qkv(
            ring, qkv_box[0].pieces, width, (q_cols, k_cols, k_cols)
        )
    else:
        while gain_sum.generator is not None:
            advance([gain_sum])
        grad_w_query, grad_kv, grad_w_out = sum_over_ctx(
            ring,
            [
                dot(hidden_input, query_delta, (0, 0)).astype(bf16),
                dot(hidden_input, kv_delta, (0, 0)).astype(bf16),
                dot(attended, back_proj, (0, 0)).astype(bf16),
            ],
        )
        grad_kv = grad_kv.reshape(width, kv_heads, 2, HEAD_SIZE)
        grad_w_key = grad_kv[:, :, 0].reshape(width, k_cols)
        grad_w_value = grad_kv[:, :, 1].reshape(width, k_cols)
    gains = gain_sum.result
    if pair:
        for swap in (output_swap, one_swap):
            while swap.generator is not None:
                advance([swap])
        output = output_part.astype(f32) + output_swap.result.astype(f32)
        back_one = one_low.astype(f32) + one_swap.result.astype(f32)
    else:
        output = lax.psum(output_part, "tp").astype(f32)
        back_one = lax.psum(one_low, "tp").astype(f32)
    output = (mixed + output).astype(bf16)
    inputs = tokens.astype(f32)
    input_grad = back_mixed + norm_back(back_one, inputs, row_scale(inputs), norm_gain)

    return (
        output,
        input_grad,
        gains[:width],
        grad_w_query,
        grad_w_key,
        grad_w_value,
        gains[2 * width : 2 * width + HEAD_SIZE],
        gains[2 * width + HEAD_SIZE :],
        grad_w_out,
        gains[width : 2 * width],
        grad_w_gate,
        grad_w_up,
        grad_w_down,
    )


def solution(mesh):
    return jax.shard_map(
        on_device,
        mesh=mesh,
        in_specs=(
            P("ctx", None),
            P("ctx", None),
            P(),
            P(),
            P(),
            P(None, "tp"),
            P(None, "tp"),
            P(None, "tp"),
            P(),
            P(),
            P("tp", None),
            P(),
            P(None, "tp"),
            P(None, "tp"),
            P("tp", None),
        ),
        out_specs=(
            P("ctx", None),
            P("ctx", None),
            P(),
            P(None, "tp"),
            P(None, "tp"),
            P(None, "tp"),
            P(),
            P(),
            P("tp", None),
            P(),
            P(None, "tp"),
            P(None, "tp"),
            P("tp", None),
        ),
        check_vma=False,
    )
```

```python
import functools

import jax
import jax.numpy as jnp
import numpy as np
from jax import lax
from jax.experimental import pallas as pl
from jax.experimental.pallas import tpu as pltpu
from jax.sharding import PartitionSpec as P

HEAD_SIZE = 64
LANES = 2 * HEAD_SIZE
EPSILON = 1e-05
ROPE_BASE = 1000000.0
LOG2E = 1.4426950408889634
VMEM_BYTES = 24 * 2**20
COST_SCALE = 4
FFN_COLS = 768
LATE = True
ALL_VMEM = 56 * 2**20
f32, bf16 = jnp.float32, jnp.bfloat16
NT = (((1,), (1,)), ((), ()))


class Ring:
    def __init__(self, n_ctx):
        n = self.n = n_ctx // 2
        self.zs = 4 if n % 4 == 0 else n
        self.ys = n // self.zs
        order = [int(self.chip_at(np.int32(place))) for place in range(n)]

        def steps(flip, turned):
            return [
                (order[i] * 2 + c, order[(i + (1 - 2 * (c ^ turned))) % n] * 2 + (c ^ flip))
                for i in range(n)
                for c in (0, 1)
            ]

        self.onward, self.across, self.spread = steps(0, 0), steps(1, 0), steps(1, 1)
        self.to_sibling = [(i, i ^ 1) for i in range(n_ctx)]

    def chip_at(self, place):
        if self.ys == 1:
            return place
        where = np.where if isinstance(place, np.integer) else jnp.where
        turn = place - self.zs
        k, r = turn // (self.ys - 1), turn % (self.ys - 1)
        back = (self.zs - 1 - k) * self.ys + where(k % 2 == 0, 1 + r, self.ys - 1 - r)
        return where(place < self.zs, place * self.ys, back)

    def here(self):
        index = lax.axis_index("ctx")
        chip, core = index // 2, index % 2
        if self.ys == 1:
            return chip, core
        z, y = chip // self.ys, chip % self.ys
        k = self.zs - 1 - z
        back = self.zs + k * (self.ys - 1) + jnp.where(k % 2 == 0, y - 1, self.ys - 1 - y)
        return jnp.where(y == 0, z, back), core

    def at(self, slot):
        place, core = self.here()
        distance, other = slot
        return (place + (1 - 2 * core) * distance + self.n) % self.n, (core + other) % 2

    def device_at(self, slot):
        place, core = self.at(slot)
        return self.chip_at(place) * 2 + core

    def hop(self, x):
        return lax.ppermute(x, "ctx", self.onward)

    def sibling(self, x):
        return lax.ppermute(x, "ctx", self.to_sibling)


def total(*terms):
    out = terms[0].astype(f32)
    for term in terms[1:]:
        out = out + term.astype(f32)
    return out.astype(bf16)


class RingGather:
    def __init__(self, ring, own):
        self.ring, self.far = ring, ring.n // 2
        self.pieces = [([(0, 0)], own), ([(0, 1)], ring.sibling(own))]
        self.step = 0

    def sends(self):
        last = self.pieces[-2][1]
        if self.step == 0:
            return [self.pieces[0][1]]
        return [last[0]] if self.step + 1 == self.far else [last]

    def send(self, arrays):
        (x,) = arrays
        self.step += 1
        new = [self.ring.hop(x)]
        if self.step == 1:
            new.append(lax.ppermute(x, "ctx", self.ring.spread))
        return new

    def arrive(self, arrays):
        d = self.step
        if d == 1:
            new = [([(-1, c)], x) for c, x in enumerate(arrays)]
            pair = jnp.stack(arrays)
            self.pieces += [([(-1, 0), (-1, 1)], pair), ([(1, 1), (1, 0)], self.ring.sibling(pair))]
            return new
        (x,) = arrays
        if d == self.far:
            new = [([(d, 0)], x), ([(d, 1)], self.ring.sibling(x))]
        else:
            new = [([(-d, 0), (-d, 1)], x), ([(d, 1), (d, 0)], self.ring.sibling(x))]
        self.pieces += new
        return new[:1]

    def done(self):
        return self.step == self.far


def sum_steps(ring, terms, box=None):
    _, core = ring.here()
    far = ring.n // 2
    (x,) = yield [total(*terms(far))]
    (got,) = yield [ring.hop(x)]
    for d in range(far - 1, 1, -1):
        here = terms(d)
        if d == far - 1:
            x = jnp.stack([total(*[y[0] for y in here], got), total(*[y[1] for y in here])])
        else:
            x = total(*here, got)
        (x,) = yield [x]
        (got,) = yield [ring.hop(x)]
    here = terms(1)
    x = yield [total(*[y[c] for y in here], got[c]) for c in (0, 1)]
    got = yield [ring.hop(x[0]), lax.ppermute(x[1], "ctx", ring.across)]
    own = total(*terms(0), *got)
    if box is None:
        return own
    gather = RingGather(ring, own)
    box.append(gather)
    while not gather.done():
        late = [x for _, x in gather.pieces[-1:]]
        new = gather.send((yield gather.sends()))
        came = yield new + late
        gather.arrive(came[: len(new)])
    return gather


class Steps:
    def __init__(self, generator):
        self.generator, self.result = generator, None
        self.sent = self.came = None

    def arrivals(self):
        return self.generator.send(self.sent) if self.sent is not None else []

    def sends(self):
        try:
            return self.generator.send(self.came or None)
        except StopIteration as stop:
            self.result, self.generator = stop.value, None
            return []


def tied(lists, others):
    flat = lax.optimization_barrier((*[x for xs in lists for x in xs], *others))
    out = []
    for xs in lists:
        out.append(list(flat[: len(xs)]))
        flat = flat[len(xs) :]
    return out, flat


def advance(steps, *others):
    steps = [x for x in steps if x is not None and x.generator is not None]
    came, others = tied([x.arrivals() for x in steps], others)
    for x, arrays in zip(steps, came):
        x.came = arrays
    sends, others = tied([x.sends() for x in steps], others)
    for x, arrays in zip(steps, sends):
        x.sent = arrays
    return others


def sum_over_ctx(ring, arrays):
    n = ring.n
    far = n // 2
    outs = []
    for x in arrays:
        unit = x.shape[0] // (2 * n)
        cut = x.reshape(2, n, unit, x.shape[1])

        def piece(distance, other):
            place, core = ring.at((distance, other))
            return cut[core, place]

        def terms(d):
            if d in (0, far):
                return [piece(d, 0), ring.sibling(piece(d, 1))]
            keep = jnp.stack([piece(d, 0), piece(d, 1)])
            return [keep, ring.sibling(jnp.stack([piece(-d, 1), piece(-d, 0)]))]

        box = []
        steps = Steps(sum_steps(ring, terms, box))
        while steps.generator is not None:
            advance([steps])
        out = jnp.zeros(x.shape, f32)
        for slots, part in box[0].pieces:
            for i, slot in enumerate(slots):
                place, core = ring.at(slot)
                one = part if len(slots) == 1 else part[i]
                out = lax.dynamic_update_slice_in_dim(
                    out, one.astype(f32), (core * n + place) * unit, 0
                )
        outs.append(out)
    return outs


def exchange_steps(x):
    (x,) = yield [x]
    (theirs,) = yield [lax.ppermute(x, "tp", [(0, 1), (1, 0)])]
    return theirs


def pair_steps(x, axes):
    for axis, size in axes:
        step = 1
        while step < size:
            (mine,) = yield [x]
            (theirs,) = yield [lax.ppermute(mine, axis, [(i, i ^ step) for i in range(size)])]
            x = mine + theirs
            step *= 2
    return x


def from_other(xs):
    return [lax.ppermute(x, "tp", [(0, 1), (1, 0)]) for x in xs]


def sum_over_tp(x):
    size = lax.axis_size("tp")
    if size == 2:
        return x.astype(f32) + lax.ppermute(x, "tp", [(0, 1), (1, 0)]).astype(f32)
    return lax.psum(x, "tp").astype(f32)


def pair_count(slots, seq_count):
    return seq_count * (2 * len(slots) + ((0, 0) in slots))


class Tiles:
    def __init__(self, ring, slots, seq_count, blk, order_ref, starts_ref):
        self.ring, self.slots = ring, slots
        self.seq_count, self.blk = seq_count, blk
        self.order, self.starts = order_ref, starts_ref
        self.last = 4 * ring.n - 1
        self.rows = pair_count(slots, seq_count)

    def start_of(self, seq, place):
        start = jnp.int32(0)
        for d in range(3):
            at = self.starts[seq, d]
            start = jnp.where(place >= at, at, start)
        return start

    def pair(self, row):
        seq, row = row % self.seq_count, row // self.seq_count
        slot, which = row // 2, row % 2
        own = self.slots.index((0, 0)) if (0, 0) in self.slots else None
        if own is not None:
            both_high = slot == len(self.slots)
            slot = jnp.where(both_high, own, slot)
        distance, other = self.slots[0]
        for i, (d, c) in enumerate(self.slots):
            distance, other = jnp.where(slot == i, d, distance), jnp.where(slot == i, c, other)
        mine = self.order[lax.axis_index("ctx")]
        theirs = self.order[self.ring.device_at((distance, other))]
        low = (which == 1) & (theirs <= mine)
        high = (which == 1) & (theirs > mine)
        if own is not None:
            low, high = low & jnp.logical_not(both_high), high | both_high
        q_place = jnp.where(low, mine, self.last - mine) * self.blk
        k_place = jnp.where(high, self.last - theirs, theirs) * self.blk
        q_tile = 2 * seq + jnp.where(low, 0, 1)
        k_tile = 2 * (self.seq_count * slot + seq) + jnp.where(high, 1, 0)
        k_end, q_end = k_place + self.blk - 1, q_place + self.blk - 1
        whole = (k_end <= q_place) & (k_place >= self.start_of(seq, q_end))
        empty = k_end < self.start_of(seq, q_place)
        kind = jnp.where(whole, 0, jnp.where(empty, 2, 1))
        return q_tile, k_tile, kind, (seq, q_place, k_place)

    def allowed(self, at, query_axis, shape):
        seq, q_place, k_place = at
        query = q_place + lax.broadcasted_iota(jnp.int32, shape, query_axis) % self.blk
        key = k_place + lax.broadcasted_iota(jnp.int32, shape, 1 - query_axis)
        return (key <= query) & (key >= self.start_of(seq, query))

    def run(self, tile):
        def body(row, carry):
            q_tile, k_tile, kind, at = self.pair(row)
            keys = pl.ds(pl.multiple_of(k_tile * self.blk, self.blk), self.blk)
            pl.when(kind == 0)(lambda: tile(q_tile, keys, None))
            pl.when(kind == 1)(lambda: tile(q_tile, keys, functools.partial(self.allowed, at)))
            return carry

        lax.fori_loop(0, self.rows, body, 0)


def load_chunks(chunks, kv_ref):
    at = 0
    for chunk in chunks:
        for part in [chunk] if len(chunk.shape) == 2 else [chunk.at[0], chunk.at[1]]:
            kv_ref[at : at + part.shape[0]] = part[...]
            at += part.shape[0]


def forward_kernel(make, parts, heads, order_ref, starts_ref, q_ref, *refs):
    chunks, held, (out_ref, kv_ref) = refs[:parts], refs[parts:-2], refs[-2:]
    tiles = make(order_ref, starts_ref)
    blk = tiles.blk
    first = lax.broadcasted_iota(jnp.int32, (blk, LANES), 1) < HEAD_SIZE
    load_chunks(chunks, kv_ref)
    out_ref[...] = held[0][...] if held else jnp.zeros_like(out_ref)

    def tile(q_tile, keys, mask):
        if mask is not None:
            allowed = mask(0, (q_ref.shape[2], blk))
        for h in range(heads):
            kv = kv_ref[keys, h * LANES : (h + 1) * LANES]
            scores = lax.dot_general(q_ref[h, q_tile], kv, NT, preferred_element_type=f32)
            weights = jnp.exp2(scores * LOG2E)
            if mask is not None:
                weights = jnp.where(allowed, weights, 0.0)
            one_v = jnp.where(first, jnp.ones_like(kv), kv)
            out_ref[h, q_tile] += jnp.dot(weights.astype(bf16), one_v, preferred_element_type=f32)

    tiles.run(tile)


def backward_kernel(make, parts, held, heads, order_ref, starts_ref, q_ref, do_ref, stat_ref, *refs):
    chunks, held, refs = refs[:parts], refs[parts : parts + held], refs[parts + held :]
    dq_ref, keep_ref, give_ref, kv_ref, dkv_ref = refs
    tiles = make(order_ref, starts_ref)
    blk = tiles.blk
    load_chunks(chunks, kv_ref)
    dq_ref[...] = held[0][...] if held else jnp.zeros_like(dq_ref)
    dkv_ref[...] = jnp.zeros_like(dkv_ref)

    def tile(q_tile, keys, mask):
        if mask is not None:
            allowed = mask(1, (blk, q_ref.shape[2]))
        for h in range(heads):
            cols = slice(h * LANES, (h + 1) * LANES)
            kv = kv_ref[keys, cols]
            q = q_ref[h, q_tile]
            do = do_ref[h, q_tile]
            scores = lax.dot_general(kv, q, NT, preferred_element_type=f32)
            back_probs = lax.dot_general(kv, do, NT, preferred_element_type=f32)
            probs = jnp.exp2(scores * LOG2E - stat_ref[h, q_tile, 0:1])
            if mask is not None:
                probs = jnp.where(allowed, probs, 0.0)
            back_scores = (probs * (back_probs - stat_ref[h, q_tile, 1:2])).astype(bf16)
            both = jnp.concatenate([probs.astype(bf16), back_scores], axis=1)
            dkv_ref[keys, cols] += jnp.dot(
                both, jnp.concatenate([do, q], axis=0), preferred_element_type=f32
            )
            dq_ref[h, q_tile] += jnp.dot(kv.T[:HEAD_SIZE], back_scores, preferred_element_type=f32)

    tiles.run(tile)
    rows = keep_ref.shape[-2]
    if len(keep_ref.shape) == 2:
        keep_ref[...] = dkv_ref[:rows]
        give_ref[...] = dkv_ref[rows:].astype(bf16)
        return
    for c in (0, 1):
        keep_ref[c] = dkv_ref[(3 - c) * rows : (4 - c) * rows]
        give_ref[c] = dkv_ref[(1 - c) * rows : (2 - c) * rows].astype(bf16)


def in_smem():
    return pl.BlockSpec(memory_space=pltpu.SMEM)


def in_vmem():
    return pl.BlockSpec(memory_space=pltpu.VMEM)


class Attention:
    def __init__(self, ring, block_order, starts, blk):
        self.ring, self.order, self.starts = ring, block_order, starts
        self.blk, self.seq_count = blk, starts.shape[0]

    def _make(self, slots):
        return lambda order_ref, starts_ref: Tiles(
            self.ring, slots, self.seq_count, self.blk, order_ref, starts_ref
        )

    def _cost(self, slots, heads, products, arrays):
        tile = 2 * self.blk * self.blk * heads * pair_count(slots, self.seq_count)
        return pl.CostEstimate(
            flops=2 * tile * 256 * products // COST_SCALE,
            bytes_accessed=sum(x.size * x.dtype.itemsize for x in arrays) // COST_SCALE,
            transcendentals=tile // COST_SCALE,
        )

    def forward(self, pieces, q, acc):
        heads, tiles, rows, _ = q.shape
        out = jax.ShapeDtypeStruct((heads, tiles, rows, LANES), f32)
        held = [] if acc is None else [acc]
        slots, chunks = [x for xs, _ in pieces for x in xs], [x for _, x in pieces]
        keys, width = len(slots) * chunks[0].shape[-2], chunks[0].shape[-1]
        return pl.pallas_call(
            functools.partial(forward_kernel, self._make(slots), len(chunks), heads),
            out_shape=out,
            in_specs=[in_smem()] * 2 + [in_vmem()] * (1 + len(chunks) + len(held)),
            out_specs=in_vmem(),
            scratch_shapes=[pltpu.VMEM((keys, width), bf16)],
            compiler_params=pltpu.CompilerParams(vmem_limit_bytes=VMEM_BYTES),
            cost_estimate=self._cost(slots, heads, 2, [q, *chunks, out, out]),
            name="attend_forward",
        )(self.order, self.starts, q, *chunks, *held)

    def backward(self, pieces, q, do, stats, acc):
        heads, tiles, rows, _ = q.shape
        slots, chunks = [x for xs, _ in pieces for x in xs], [x for _, x in pieces]
        keys, width = len(slots) * chunks[0].shape[-2], chunks[0].shape[-1]
        outs = [
            jax.ShapeDtypeStruct((heads, tiles, HEAD_SIZE, rows), f32),
            jax.ShapeDtypeStruct(chunks[0].shape, f32),
            jax.ShapeDtypeStruct(chunks[0].shape, bf16),
        ]
        held = [] if acc is None else [acc]
        return pl.pallas_call(
            functools.partial(
                backward_kernel, self._make(slots), len(chunks), len(held), heads
            ),
            out_shape=outs,
            in_specs=[in_smem()] * 2 + [in_vmem()] * (3 + len(chunks) + len(held)),
            out_specs=[in_vmem()] * len(outs),
            scratch_shapes=[pltpu.VMEM((keys, width), bf16), pltpu.VMEM((keys, width), f32)],
            compiler_params=pltpu.CompilerParams(vmem_limit_bytes=VMEM_BYTES),
            cost_estimate=self._cost(slots, heads, 5, [q, do, outs[0], *chunks, *outs]),
            name="attend_backward",
        )(self.order, self.starts, q, do, stats, *chunks, *held)


def grads_kernel(ring, *refs):
    two, gate, up, ffn, cot = (refs[2 * i : 2 * i + 2] for i in range(5))
    outs, (lhs_ref, cot_ref, all_ref) = refs[10:-3], refs[-3:]

    @pl.when(pl.program_id(0) == 0)
    def _():
        lhs_ref[...] = jnp.concatenate([x[...] for x in two], axis=0).T
        cot_ref[...] = jnp.concatenate([x[...] for x in cot], axis=0)

    n = ring.n
    unit = lhs_ref.shape[0] // (2 * n)
    cols = gate[0].shape[2]
    thin = cols // (2 * n)
    for i, half in enumerate((gate, up)):
        right = jnp.concatenate([x[0] for x in half], axis=0)
        grad = jnp.dot(lhs_ref[...], right, preferred_element_type=f32).astype(bf16)
        all_ref[:, i * unit : (i + 1) * unit] = grad.reshape(2 * n, unit, cols)
    left = jnp.concatenate([x[0] for x in ffn], axis=0).T
    down = jnp.dot(left, cot_ref[...], preferred_element_type=f32).astype(bf16)
    down = down.reshape(2 * n, thin, down.shape[1])
    for k in range(down.shape[2] // cols):
        at = 2 * unit + k * thin
        all_ref[:, at : at + thin] = down[:, :, k * cols : (k + 1) * cols]
    deal(ring, lambda at: all_ref[at], lambda ref, x: ref.at[0].__setitem__(..., x), outs)


def deal(ring, read, write, outs):
    far = ring.n // 2

    def part(distance, other):
        place, core = ring.at((distance, other))
        return read(core * ring.n + place)

    keep_far, give_far, *keep, give = outs
    write(keep_far, part(far, 0))
    write(give_far, part(far, 1))
    write(keep[0], part(0, 0))
    write(give.at[0], part(0, 1))
    for d in range(1, far):
        for c in (0, 1):
            write(keep[d].at[c], part(d, c))
            write(give.at[2 * d - 1 + c], part(-d, 1 - c))


def dealt(ring, cut):
    far = ring.n // 2
    heads = [(), (), ()] + [(2,)] * (far - 1) + [(2 * far - 1,)]
    return [jax.ShapeDtypeStruct((*head, *cut.shape), cut.dtype) for head in heads]


def dealt_terms(ring, outs):
    far = ring.n // 2
    keep_far, give_far, *keep, give = outs
    got_far = ring.sibling(give_far)
    give, got_far = lax.optimization_barrier((give, got_far))
    got = ring.sibling(give)

    def terms(d):
        if d == far:
            return [keep_far, got_far]
        if d == 0:
            return [keep[0], got[0]]
        return [keep[d], got[2 * d - 1 : 2 * d + 1]]

    return terms


def ffn_grads(ring, hidden_two, back_gate, back_up, hidden_ffn, cotangent):
    rows, width = hidden_two[0].shape
    blocks, _, cols = back_gate[0].shape
    units = blocks * cols
    n = ring.n
    wide = width // (2 * n) * 3
    whole = [pl.BlockSpec((rows, width), lambda j: (0, 0))] * 2
    block = [pl.BlockSpec((1, rows, cols), lambda j: (j, 0, 0))] * 2
    outs = dealt(ring, shape(units // cols, wide, cols, dtype=bf16))
    cuts = [
        pl.BlockSpec(
            (*x.shape[:-3], 1, wide, cols), lambda j, k=len(x.shape): (0,) * (k - 3) + (j, 0, 0)
        )
        for x in outs
    ]
    return pl.pallas_call(
        functools.partial(grads_kernel, ring),
        grid=(units // cols,),
        out_shape=outs,
        in_specs=whole + block * 3 + whole,
        out_specs=cuts,
        scratch_shapes=[
            pltpu.VMEM((width, 2 * rows), bf16),
            pltpu.VMEM((2 * rows, width), bf16),
            pltpu.VMEM((2 * n, wide, cols), bf16),
        ],
        compiler_params=pltpu.CompilerParams(vmem_limit_bytes=VMEM_BYTES),
        cost_estimate=pl.CostEstimate(
            flops=12 * rows * width * units // COST_SCALE, bytes_accessed=2**20, transcendentals=0
        ),
        name="ffn_grads",
    )(*hidden_two, *back_gate, *back_up, *hidden_ffn, *cotangent)


def place_kernel(ring, slots, count, *refs):
    arrays, outs, (wide_ref, down_ref, sem) = refs[:count], refs[-6:-3], refs[-3:]
    parts = [y for x in arrays for y in ([x] if len(x.shape) == 3 else [x.at[0], x.at[1]])]
    n = ring.n
    blocks, _, cols = parts[0].shape
    unit = outs[0].shape[0] // (2 * n)
    thin = cols // (2 * n)
    copies = []
    for i, slot in enumerate(slots):
        part = parts[i]
        place, core = ring.at(slot)
        r = core * n + place
        for w in range(2):
            for j in range(blocks):
                wide_ref[i, w, :, j * cols : (j + 1) * cols] = part[
                    j, w * unit : (w + 1) * unit
                ].astype(f32)
            rows = pl.ds(pl.multiple_of(r * unit, unit), unit)
            copies.append((wide_ref.at[i, w], outs[w].at[rows]))
        for j in range(blocks):
            for k in range(outs[2].shape[1] // cols):
                at = 2 * unit + k * thin
                down_ref[i, j, :, k * cols : (k + 1) * cols] = part[j, at : at + thin].astype(f32)
            rows = pl.ds(pl.multiple_of(j * cols + r * thin, thin), thin)
            copies.append((down_ref.at[i, j], outs[2].at[rows]))
        for k in range(i * (2 + blocks), (i + 1) * (2 + blocks)):
            pltpu.make_async_copy(*copies[k], sem.at[k]).start()
    for k, pair in enumerate(copies):
        pltpu.make_async_copy(*pair, sem.at[k]).wait()


def place_ffn(ring, pieces, width, held):
    slots, parts = [x for xs, _ in pieces for x in xs], [x for _, x in pieces]
    blocks, wide, cols = parts[0].shape[-3:]
    units = blocks * cols
    count = len(slots)
    thin = cols // (2 * ring.n)
    anywhere = pl.BlockSpec(memory_space=pl.ANY)
    return pl.pallas_call(
        functools.partial(place_kernel, ring, slots, len(parts)),
        out_shape=[shape(width, units), shape(width, units), shape(units, width)],
        in_specs=[in_vmem()] * len(parts) + [anywhere] * len(held),
        out_specs=[anywhere] * 3,
        input_output_aliases={len(parts) + i: i for i in range(len(held))},
        scratch_shapes=[
            pltpu.VMEM((count, 2, width // (2 * ring.n), units), f32),
            pltpu.VMEM((count, blocks, thin, width), f32),
            pltpu.SemaphoreType.DMA((count * (2 + blocks),)),
        ],
        compiler_params=pltpu.CompilerParams(vmem_limit_bytes=VMEM_BYTES),
        cost_estimate=pl.CostEstimate(
            flops=0, bytes_accessed=8 * count * wide * units, transcendentals=0
        ),
        name="place_ffn",
    )(*parts, *held)


def place_qkv_kernel(ring, slots, *refs):
    arrays, (query_ref, key_ref, value_ref, out_ref) = refs[:-4], refs[-4:]
    parts = [y for x in arrays for y in ([x] if len(x.shape) == 2 else [x.at[0], x.at[1]])]
    n = ring.n
    unit, thin = query_ref.shape[0] // (2 * n), out_ref.shape[0] // (2 * n)
    for slot, part in zip(slots, parts):
        place, core = ring.at(slot)
        r = core * n + place
        rows = pl.ds(pl.multiple_of(r * unit, unit), unit)
        at = query_ref.shape[1]
        query_ref[rows] = part[:unit, :at].astype(f32)
        for h in range(key_ref.shape[1] // HEAD_SIZE):
            cols = slice(h * HEAD_SIZE, (h + 1) * HEAD_SIZE)
            both = part[:unit, at + h * LANES : at + (h + 1) * LANES].astype(f32)
            key_ref[rows, cols] = both[:, :HEAD_SIZE]
            value_ref[rows, cols] = both[:, HEAD_SIZE:]
        rows = pl.ds(pl.multiple_of(r * thin, thin), thin)
        out_ref[rows] = part[unit:].astype(f32)


def place_qkv(ring, pieces, width, cols):
    slots, parts = [x for xs, _ in pieces for x in xs], [x for _, x in pieces]
    thin = parts[0].shape[-2] - width // (2 * ring.n)
    return whole_call(
        functools.partial(place_qkv_kernel, ring, slots),
        "place_qkv",
        [shape(width, c) for c in cols] + [shape(thin * 2 * ring.n, width)],
        parts,
        0,
    )


def whole_call(kernel, name, outs, args, flops, scratch=(), scalars=(0, 0), vmem=VMEM_BYTES):
    moved = sum(x.size * x.dtype.itemsize for x in (*outs, *args))
    return pl.pallas_call(
        kernel,
        out_shape=list(outs),
        in_specs=[in_smem()] * scalars[0] + [in_vmem()] * (len(args) - scalars[0]),
        out_specs=[in_smem()] * scalars[1] + [in_vmem()] * (len(outs) - scalars[1]),
        scratch_shapes=list(scratch),
        compiler_params=pltpu.CompilerParams(vmem_limit_bytes=vmem),
        cost_estimate=pl.CostEstimate(
            flops=flops // COST_SCALE, bytes_accessed=moved // COST_SCALE, transcendentals=0
        ),
        name=name,
    )(*args)


def shape(*dims, dtype=f32):
    return jax.ShapeDtypeStruct(dims, dtype)


def first_lanes(rows):
    return lax.broadcasted_iota(jnp.int32, (rows, LANES), 1) < HEAD_SIZE


def head_mean(x):
    i = lax.broadcasted_iota(jnp.int32, (LANES, LANES), 0) // HEAD_SIZE
    j = lax.broadcasted_iota(jnp.int32, (LANES, LANES), 1) // HEAD_SIZE
    mean = jnp.where(i == j, 1.0 / HEAD_SIZE, 0.0).astype(bf16)
    high = x.astype(bf16)
    low = (x - high.astype(f32)).astype(bf16)
    return jnp.dot(high, mean, preferred_element_type=f32) + jnp.dot(
        low, mean, preferred_element_type=f32
    )


def turn(x, cosine, sines):
    lane = lax.broadcasted_iota(jnp.int32, x.shape, 1) % HEAD_SIZE
    half = HEAD_SIZE // 2
    other = jnp.where(
        lane < half, pltpu.roll(x, LANES - half, axis=1), pltpu.roll(x, half, axis=1)
    )
    return x * cosine + other * sines


def row_scale(x):
    return lax.rsqrt(jnp.mean(x * x, axis=-1, keepdims=True) + EPSILON)


def norm_back(upstream, x, scale, gain):
    inner = upstream * gain
    return scale * (inner - x * (scale * scale * jnp.mean(inner * x, axis=-1, keepdims=True)))


def head_norm_back(upstream, x, gain):
    scale = lax.rsqrt(head_mean(x * x) + EPSILON)
    inner = upstream * gain
    back = scale * (inner - x * (scale * scale * head_mean(inner * x)))
    return back, jnp.sum(upstream * x * scale, axis=0, keepdims=True)


def gain_of(ref):
    return ref[...].astype(f32)


def head_gain(ref):
    return jnp.concatenate([gain_of(ref)] * 2, axis=1)


def lanes(tile):
    return slice(tile * LANES, (tile + 1) * LANES)


def project_kv_kernel(
    tiles, last, order, segments, tokens, gain, w_key, w_value, key_gain, inverse, *refs
):
    starts, hidden, kv_raw, kv, w_kv, cosine, sines = refs
    x = tokens[...].astype(f32)
    hidden[...] = (x * row_scale(x) * gain_of(gain)).astype(bf16)
    rows = x.shape[0]
    blk = rows // tiles
    mine = order[lax.axis_index("ctx")]
    lane = lax.broadcasted_iota(jnp.int32, (blk, LANES), 1) % HEAD_SIZE
    for t in range(tiles):
        block = last - mine if t % 2 else mine
        place = block * blk + lax.broadcasted_iota(jnp.int32, (blk, LANES), 0)
        angles = place.astype(f32) * inverse[...]
        at = slice(t * blk, (t + 1) * blk)
        cosine[at] = jnp.cos(angles)
        sine = jnp.sin(angles)
        sines[at] = jnp.where(lane < HEAD_SIZE // 2, -sine, sine)
    first = first_lanes(rows)
    for h in range(kv.shape[1] // LANES):
        cols = slice(h * HEAD_SIZE, (h + 1) * HEAD_SIZE)
        w_kv[:, lanes(h)] = jnp.concatenate([w_key[:, cols], w_value[:, cols]], axis=1)
        raw = jnp.dot(hidden[...], w_kv[:, lanes(h)], preferred_element_type=f32)
        kv_raw[:, lanes(h)] = raw
        normed = raw * lax.rsqrt(head_mean(raw * raw) + EPSILON) * head_gain(key_gain)
        kv[:, lanes(h)] = jnp.where(first, turn(normed, cosine[...], sines[...]), raw).astype(bf16)
    for seq in range(segments.shape[0]):
        for d in range(3):
            before = jnp.where(segments[seq : seq + 1] <= d, 1.0, 0.0)
            starts[seq, d] = jnp.sum(before).astype(jnp.int32)


def project_q_kernel(tiles, hidden, w_query, query_gain, cosine, sines, query_raw, q_tiles):
    rows = hidden.shape[0]
    blk = rows // tiles
    first = first_lanes(rows)
    for h in range(q_tiles.shape[0]):
        raw = jnp.dot(hidden[...], w_query[:, lanes(h)], preferred_element_type=f32)
        query_raw[:, lanes(h)] = raw
        normed = raw * lax.rsqrt(head_mean(raw * raw) + EPSILON) * head_gain(query_gain)
        turned = turn(normed, cosine[...], sines[...]).astype(bf16).astype(f32) * 0.125
        pair = [
            jnp.where(first, turned, 0.0),
            jnp.where(first, pltpu.roll(turned, HEAD_SIZE, axis=1), 0.0),
        ]
        for g, one in enumerate(pair):
            for t in range(tiles):
                q_tiles[h, t, g * blk : (g + 1) * blk] = one[t * blk : (t + 1) * blk].astype(bf16)


def half_rows(pair, rows, which):
    first = (lax.axis_index("tp") + which) % 2 if pair else which
    return pl.ds(pl.multiple_of(first * (rows // 2), rows // 2), rows // 2)


def mix_kernel(pair, acc, w_out, attended, o, lse, *halves):
    heads, tiles, rows, _ = acc.shape
    blk = rows // 2
    first = first_lanes(rows)
    for h in range(heads):
        for t in range(tiles):
            x = acc[h, t]
            value = jnp.where(first, 0.0, x * pltpu.roll(1.0 / x, HEAD_SIZE, axis=1))
            o[h, t] = value
            lse[h, t] = jnp.log2(x.T[:8])
            low = pltpu.roll(value[:blk], HEAD_SIZE, axis=1) + value[blk:]
            attended[t * blk : (t + 1) * blk, lanes(h)] = low.astype(bf16)
    for which, half in enumerate(halves):
        rows = half_rows(pair, attended.shape[0], which)
        half[...] = jnp.dot(attended[rows], w_out[...], preferred_element_type=f32).astype(bf16)


def ffn_kernel(tokens, attn, gain, hidden_back, w_gate, w_up, *refs):
    mixed, hidden_two, hidden_ffn, back_gate, back_up, gain_grad, low, sums = refs
    step, last = pl.program_id(0), pl.num_programs(0) - 1

    @pl.when(step == 0)
    def _():
        x = tokens[...].astype(f32) + attn[...].astype(f32)
        mixed[...] = x
        hidden_two[...] = (x * row_scale(x) * gain_of(gain)).astype(bf16)
        sums[...] = jnp.zeros_like(sums)

    gating = jnp.dot(hidden_two[...], w_gate[...], preferred_element_type=f32)
    lifted = jnp.dot(hidden_two[...], w_up[...], preferred_element_type=f32)
    upstream = hidden_back[...]
    logistic = jax.nn.sigmoid(gating)
    silu = gating * logistic
    gate = (upstream * lifted * logistic * (1.0 + gating * (1.0 - logistic))).astype(bf16)
    up = (upstream * silu).astype(bf16)
    ffn = (silu * lifted).astype(bf16)
    for ref, value in ((hidden_ffn, ffn), (back_gate, gate), (back_up, up)):
        cols = ref.shape[2]
        for k in range(ref.shape[0]):
            ref[k] = value[:, k * cols : (k + 1) * cols]
    sums[...] += lax.dot_general(gate, w_gate[...], NT, preferred_element_type=f32)
    sums[...] += lax.dot_general(up, w_up[...], NT, preferred_element_type=f32)

    @pl.when(step == last)
    def _():
        x = mixed[...]
        gain_grad[...] = jnp.sum(sums[...] * x * row_scale(x), axis=0, keepdims=True)
        low[...] = sums[...].astype(bf16)


def block_cols(units):
    return 256 if units % 256 == 0 else units


def feed_forward(tokens, attn, gain, hidden_back, w_gate, w_up):
    rows, width = tokens.shape
    units = w_gate.shape[1]
    cols = FFN_COLS if units % FFN_COLS == 0 else units
    thin = block_cols(units)
    whole = pl.BlockSpec((rows, width), lambda j: (0, 0))
    line = pl.BlockSpec((1, width), lambda j: (0, 0))
    weight = pl.BlockSpec((width, cols), lambda j: (0, j))
    block = pl.BlockSpec((cols // thin, rows, thin), lambda j: (j, 0, 0))
    low = shape(units // thin, rows, thin, dtype=bf16)
    return pl.pallas_call(
        ffn_kernel,
        grid=(units // cols,),
        out_shape=[shape(rows, width), shape(rows, width, dtype=bf16), low, low, low]
        + [shape(1, width), shape(rows, width, dtype=bf16)],
        in_specs=[whole, whole, line, pl.BlockSpec((rows, cols), lambda j: (0, j)), weight, weight],
        out_specs=[whole, whole, block, block, block, line, whole],
        scratch_shapes=[pltpu.VMEM((rows, width), f32)],
        compiler_params=pltpu.CompilerParams(vmem_limit_bytes=VMEM_BYTES),
        cost_estimate=pl.CostEstimate(
            flops=8 * rows * width * units // COST_SCALE, bytes_accessed=2**20, transcendentals=0
        ),
        name="feed_forward",
    )(tokens, attn, gain, hidden_back, w_gate, w_up)


def down_kernel(pair, *refs):
    ffn, w_down, out = refs[:2], refs[2], refs[3]
    cols = ffn[0].shape[2]
    for which, x in enumerate(ffn):
        part = jnp.zeros((x.shape[1], out.shape[1]), f32)
        for k in range(x.shape[0]):
            part += jnp.dot(
                x[k], w_down[k * cols : (k + 1) * cols], preferred_element_type=f32
            )
        out[half_rows(pair, out.shape[0], which)] = part.astype(bf16)


def back_kernel(pair, cotangent, gain, w_out, o, lse, *refs):
    mixed, mine, theirs, (back_mixed, back_proj, do_tiles, stats) = (
        refs[:2],
        refs[2:4],
        refs[4:6],
        refs[6:],
    )
    for which in (0, 1):
        rows = half_rows(pair, cotangent.shape[0], which)
        x = mixed[which][...]
        upstream = mine[which][...].astype(f32) + theirs[which][...].astype(f32)
        back = cotangent[rows].astype(f32) + norm_back(upstream, x, row_scale(x), gain_of(gain))
        back_mixed[rows] = back
        back_proj[rows] = back.astype(bf16)
    heads, tiles, rows, _ = o.shape
    blk = rows // 2
    first = first_lanes(blk)
    row = lax.broadcasted_iota(jnp.int32, (8, rows), 0)
    for h in range(heads):
        attn = lax.dot_general(back_proj[...], w_out[lanes(h)], NT, preferred_element_type=f32)
        for t in range(tiles):
            here = attn[t * blk : (t + 1) * blk]
            do = jnp.concatenate(
                [
                    jnp.where(first, 0.0, pltpu.roll(here, HEAD_SIZE, axis=1)),
                    jnp.where(first, 0.0, here),
                ],
                axis=0,
            ).astype(bf16)
            do_tiles[h, t] = do
            delta = jnp.sum((do.astype(f32) * o[h, t]).T, axis=0, keepdims=True)
            stats[h, t] = jnp.where(row == 0, lse[h, t], delta)


def back_query_kernel(dq, query_raw, query_gain, cosine, sines, query_delta, gain_grad):
    heads, tiles, _, rows = dq.shape
    blk = rows // 2
    gain_grad[...] = jnp.zeros_like(gain_grad)
    for t in range(tiles):
        at = slice(t * blk, (t + 1) * blk)
        for h in range(heads):
            both = jnp.concatenate([dq[h, t, :, :blk], dq[h, t, :, blk:]], axis=0) * 0.125
            turned = turn(both.T, cosine[at], -sines[at])
            back, gain_terms = head_norm_back(turned, query_raw[at, lanes(h)], head_gain(query_gain))
            query_delta[at, lanes(h)] = back.astype(bf16)
            gain_grad[...] += gain_terms


def back_project_kernel(
    ring,
    tokens,
    hidden,
    query_delta,
    own_dkv,
    kv_raw,
    key_gain,
    cosine,
    sines,
    w_query,
    w_kv,
    attended,
    back_proj,
    *refs,
):
    low, norm_grad, gain_grad, kv_delta = refs[:4]
    outs, all_ref = refs[4:-1], refs[-1]
    rows, width = tokens.shape
    first = first_lanes(rows)
    gain_grad[...] = jnp.zeros_like(gain_grad)
    for h in range(own_dkv.shape[1] // LANES):
        dkv = own_dkv[:, lanes(h)].astype(f32)
        turned = turn(dkv, cosine[...], -sines[...])
        back, gain_terms = head_norm_back(turned, kv_raw[:, lanes(h)], head_gain(key_gain))
        kv_delta[:, lanes(h)] = jnp.where(first, back, dkv).astype(bf16)
        gain_grad[...] += gain_terms
    part = lax.dot_general(
        query_delta[...], w_query[...], NT, preferred_element_type=f32
    ) + lax.dot_general(kv_delta[...], w_kv[...], NT, preferred_element_type=f32)
    low[...] = part.astype(bf16)
    x = tokens[...].astype(f32)
    norm_grad[...] = jnp.sum(part * x * row_scale(x), axis=0, keepdims=True)
    if not outs:
        return
    lhs = hidden[...].T
    n = ring.n
    unit = width // (2 * n)
    q_cols = query_delta.shape[1]
    for cols, right in (
        (slice(0, q_cols), query_delta),
        (slice(q_cols, q_cols + kv_delta.shape[1]), kv_delta),
    ):
        grad = jnp.dot(lhs, right[...], preferred_element_type=f32).astype(bf16)
        all_ref[:, :unit, cols] = grad.reshape(2 * n, unit, grad.shape[1])
    grad = jnp.dot(attended[...].T, back_proj[...], preferred_element_type=f32).astype(bf16)
    all_ref[:, unit:] = grad.reshape(2 * n, -1, width)
    deal(ring, lambda at: all_ref[at], lambda ref, x: ref.__setitem__(..., x), outs)


def dot(a, b, dims):
    return lax.dot_general(a, b, ((dims[:1], dims[1:]), ((), ())), preferred_element_type=f32)


def on_device(
    tokens,
    cotangent,
    block_order,
    segment_ids,
    norm_gain,
    w_query,
    key_weight,
    value_weight,
    query_gain,
    key_gain,
    w_out,
    ffn_gain,
    w_gate,
    w_up,
    w_down,
):
    devices = lax.axis_size("ctx")
    ring = Ring(devices)
    far = ring.n // 2
    rows, width = tokens.shape
    seq_count = segment_ids.shape[0]
    blk = rows // seq_count // 2
    tiles = 2 * seq_count
    kv_heads = key_weight.shape[1] // HEAD_SIZE
    q_cols, k_cols = w_query.shape[1], key_weight.shape[1]
    units = w_gate.shape[1]
    packed = units % 256 == 0 and width % (32 * ring.n) == 0 and w_out.shape[0] % (32 * ring.n) == 0
    pair = lax.axis_size("tp") == 2

    def line(x):
        return x.reshape(1, -1)

    inverse = ROPE_BASE ** (-np.arange(0, HEAD_SIZE, 2) / HEAD_SIZE)
    inverse = np.tile(inverse, 4)[None, :].astype(np.float32)
    starts, hidden_input, kv_raw, own_kv, w_kv, cosine, sines = whole_call(
        functools.partial(project_kv_kernel, tiles, 2 * devices - 1),
        "project_kv",
        [
            shape(seq_count, 3, dtype=jnp.int32),
            shape(rows, width, dtype=bf16),
            shape(rows, 2 * k_cols),
            shape(rows, 2 * k_cols, dtype=bf16),
            shape(width, 2 * k_cols, dtype=bf16),
            shape(rows, LANES),
            shape(rows, LANES),
        ],
        [
            block_order,
            segment_ids,
            tokens,
            line(norm_gain),
            key_weight,
            value_weight,
            line(key_gain),
            jnp.asarray(inverse),
        ],
        4 * rows * width * k_cols,
        scalars=(1, 1),
        vmem=ALL_VMEM,
    )
    gather = RingGather(ring, own_kv)
    flying = gather.send(gather.sends())
    query_raw, q_tiles = whole_call(
        functools.partial(project_q_kernel, tiles),
        "project_q",
        [shape(rows, q_cols), shape(kv_heads, tiles, 2 * blk, LANES, dtype=bf16)],
        [hidden_input, w_query, line(query_gain), cosine, sines],
        2 * rows * width * q_cols,
    )

    attention = Attention(ring, block_order, starts, blk)
    acc = attention.forward(gather.pieces[:1], q_tiles, None)
    late = gather.pieces[1]
    while True:
        *came, acc = lax.optimization_barrier((*flying, acc))
        now = gather.arrive(came)
        if gather.done():
            break
        flying = gather.send(gather.sends())
        acc = attention.forward([late, *now], q_tiles, acc)
        late = gather.pieces[-1]
    acc = attention.forward([late], q_tiles, acc)
    acc = attention.forward(gather.pieces[-2:], q_tiles, acc)
    kv_pieces = {
        max(abs(d) for d, _ in slots): gather.pieces[i - 1 : i + 1]
        for i, (slots, _) in enumerate(gather.pieces)
        if i % 2
    }
    attended, o, lse, attn_mine, attn_send = whole_call(
        functools.partial(mix_kernel, pair),
        "mix",
        [
            shape(rows, q_cols, dtype=bf16),
            shape(*acc.shape),
            shape(kv_heads, tiles, 8, 2 * blk),
            shape(rows // 2, width, dtype=bf16),
            shape(rows // 2, width, dtype=bf16),
        ],
        [acc, w_out],
        2 * rows * width * q_cols,
    )

    def halves_of(x):
        at = lax.axis_index("tp") if pair else 0
        return [
            lax.dynamic_slice_in_dim(x, (at + k) % 2 * (rows // 2), rows // 2, 0) for k in (0, 1)
        ]

    def from_first(xs):
        at = lax.axis_index("tp") if pair else 0
        return jnp.concatenate([jnp.where(at == k, xs[0], xs[1]) for k in (0, 1)])

    cots, toks = halves_of(cotangent), halves_of(tokens)
    if pair:
        (attn_theirs,) = from_other([attn_send])
        upstream = [dot(x, w_down, (1, 1)) for x in cots]
        attn_theirs, *upstream = lax.optimization_barrier((attn_theirs, *upstream))
        attn = total(attn_mine, attn_theirs)
    else:
        attn, attn_next = lax.psum((attn_mine, attn_send), "tp")
        upstream = [dot(x, w_down, (1, 1)) for x in cots]

    def feed(k, attn):
        return feed_forward(toks[k], attn, line(ffn_gain), upstream[k], w_gate, w_up)

    if pair:
        (attn_next,) = from_other([attn])
        fed = [feed(0, attn)]
        attn_next, *fed[0] = lax.optimization_barrier((attn_next, *fed[0]))
        (last,) = from_other([fed[0][-1]])
        fed.append(feed(1, attn_next))
        last, *fed[1] = lax.optimization_barrier((last, *fed[1]))
        (first,) = from_other([fed[1][-1]])
    else:
        fed = [feed(0, attn), feed(1, attn_next)]
        first, last = lax.psum((fed[0][-1], fed[1][-1]), "tp")
    mixed, hidden_two, hidden_ffn, back_gate, back_up, ffn_gain_grads, mine = zip(*fed)
    if not pair:
        mine = [jnp.zeros_like(x) for x in mine]
    grad_ffn_gain = ffn_gain_grads[0] + ffn_gain_grads[1]
    if packed:
        dealt_out = ffn_grads(ring, hidden_two, back_gate, back_up, hidden_ffn, cots)
        first, *dealt_out = lax.optimization_barrier((first, *dealt_out))
        ffn_box = []
        ffn_sum = Steps(sum_steps(ring, dealt_terms(ring, dealt_out), ffn_box))
        first, last = advance([ffn_sum], first, last)
    else:

        def by_units(xs):
            return jnp.concatenate(xs, axis=1).transpose(1, 0, 2).reshape(rows, units)

        two, cot = jnp.concatenate(hidden_two), jnp.concatenate(cots)
        grad_w_gate, grad_w_up, grad_w_down = sum_over_ctx(
            ring,
            [
                dot(two, by_units(back_gate), (0, 0)).astype(bf16),
                dot(two, by_units(back_up), (0, 0)).astype(bf16),
                dot(by_units(hidden_ffn), cot, (0, 0)).astype(bf16),
            ],
        )
        ffn_sum = None

    back_mixed, back_proj, do_tiles, stats = whole_call(
        functools.partial(back_kernel, pair),
        "back",
        [
            shape(rows, width),
            shape(rows, width, dtype=bf16),
            shape(*q_tiles.shape, dtype=bf16),
            shape(*lse.shape),
        ],
        [cotangent, line(ffn_gain), w_out, o, lse, *mixed, *mine, first, last],
        2 * rows * width * q_cols,
    )
    output_swap, more = None, hidden_ffn
    dq = None
    terms = {}

    dkv_sum = Steps(sum_steps(ring, lambda d: terms[d]))
    for d in range(far, -1, -1):
        if d < far:
            chains = [ffn_sum, dkv_sum if d < far - 1 else None]
            if d == 0 and pair:
                output_swap = Steps(exchange_steps(output_part))
                chains.append(output_swap)
            do_tiles, dq, *more = advance(chains, do_tiles, dq, *more)
            if d == far - 1:
                (output_part,) = whole_call(
                    functools.partial(down_kernel, pair),
                    "down",
                    [shape(rows, width, dtype=bf16)],
                    [*more, w_down],
                    2 * rows * width * units,
                )
                more = [output_part]
        dq, keep, give = attention.backward(kv_pieces[d], q_tiles, do_tiles, stats, dq)
        terms[d] = [keep, ring.sibling(give)]
    placed, done = [], 0
    (dq,) = advance([None if LATE else ffn_sum, dkv_sum], dq)
    query_delta, grad_query_gain = whole_call(
        back_query_kernel,
        "back_query",
        [shape(rows, q_cols, dtype=bf16), shape(1, LANES)],
        [dq, query_raw, line(query_gain), cosine, sines],
        2 * rows * width,
    )
    if packed:
        done = len(ffn_box[0].pieces)
        placed = place_ffn(ring, ffn_box[0].pieces, width, [])
    query_delta, *placed = advance([dkv_sum], query_delta, *placed)
    own_dkv = dkv_sum.result
    wide = width // (2 * ring.n) + w_out.shape[0] // (2 * ring.n)
    one_low, grad_norm_gain, grad_key_gain, kv_delta, *cuts = whole_call(
        functools.partial(back_project_kernel, ring),
        "back_project",
        [
            shape(rows, width, dtype=bf16),
            shape(1, width),
            shape(1, LANES),
            shape(rows, 2 * k_cols, dtype=bf16),
        ]
        + (dealt(ring, shape(wide, width, dtype=bf16)) if packed else []),
        [
            tokens,
            hidden_input,
            query_delta,
            own_dkv,
            kv_raw,
            line(key_gain),
            cosine,
            sines,
            w_query,
            w_kv,
            attended,
            back_proj,
        ],
        4 * rows * width * (q_cols + 2 * k_cols),
        [pltpu.VMEM((2 * ring.n, wide, width), bf16)],
    )

    gains = jnp.concatenate(
        [
            grad_norm_gain[0],
            grad_ffn_gain[0],
            grad_query_gain[0, :HEAD_SIZE] + grad_query_gain[0, HEAD_SIZE:],
            grad_key_gain[0, :HEAD_SIZE],
        ]
    )
    gain_sum = Steps(pair_steps(gains, [("tp", lax.axis_size("tp")), ("ctx", devices)]))
    one_swap = Steps(exchange_steps(one_low)) if pair else None
    if packed:
        qkv_box = []
        qkv_sum = Steps(sum_steps(ring, dealt_terms(ring, cuts), qkv_box))
        gather = ffn_box[0]
        round_at = 0
        while qkv_sum.generator is not None:
            came = len(gather.pieces)
            chains = [qkv_sum, gain_sum]
            if round_at == 0:
                chains.append(output_swap)
            elif round_at in (1, 4):
                chains.append(one_swap)
            placed = advance(chains, *placed)
            if round_at % 2 == 0:
                placed = advance([ffn_sum, gain_sum], *placed)
            if came > done:
                placed = place_ffn(ring, gather.pieces[done:came], width, placed)
                done = came
            round_at += 1
        if done < len(gather.pieces):
            placed = place_ffn(ring, gather.pieces[done:], width, placed)
        grad_w_gate, grad_w_up, grad_w_down = placed
        grad_w_query, grad_w_key, grad_w_value, grad_w_out = place_qkv(
            ring, qkv_box[0].pieces, width, (q_cols, k_cols, k_cols)
        )
    else:
        while gain_sum.generator is not None:
            advance([gain_sum])
        grad_w_query, grad_kv, grad_w_out = sum_over_ctx(
            ring,
            [
                dot(hidden_input, query_delta, (0, 0)).astype(bf16),
                dot(hidden_input, kv_delta, (0, 0)).astype(bf16),
                dot(attended, back_proj, (0, 0)).astype(bf16),
            ],
        )
        grad_kv = grad_kv.reshape(width, kv_heads, 2, HEAD_SIZE)
        grad_w_key = grad_kv[:, :, 0].reshape(width, k_cols)
        grad_w_value = grad_kv[:, :, 1].reshape(width, k_cols)
    gains = gain_sum.result
    if pair:
        for swap in (output_swap, one_swap):
            while swap.generator is not None:
                advance([swap])
        output = output_part.astype(f32) + output_swap.result.astype(f32)
        back_one = one_low.astype(f32) + one_swap.result.astype(f32)
    else:
        output = lax.psum(output_part, "tp").astype(f32)
        back_one = lax.psum(one_low, "tp").astype(f32)
    output = (from_first(mixed) + output).astype(bf16)
    inputs = tokens.astype(f32)
    input_grad = back_mixed + norm_back(back_one, inputs, row_scale(inputs), norm_gain)

    return (
        output,
        input_grad,
        gains[:width],
        grad_w_query,
        grad_w_key,
        grad_w_value,
        gains[2 * width : 2 * width + HEAD_SIZE],
        gains[2 * width + HEAD_SIZE :],
        grad_w_out,
        gains[width : 2 * width],
        grad_w_gate,
        grad_w_up,
        grad_w_down,
    )


def solution(mesh):
    return jax.shard_map(
        on_device,
        mesh=mesh,
        in_specs=(
            P("ctx", None),
            P("ctx", None),
            P(),
            P(),
            P(),
            P(None, "tp"),
            P(None, "tp"),
            P(None, "tp"),
            P(),
            P(),
            P("tp", None),
            P(),
            P(None, "tp"),
            P(None, "tp"),
            P("tp", None),
        ),
        out_specs=(
            P("ctx", None),
            P("ctx", None),
            P(),
            P(None, "tp"),
            P(None, "tp"),
            P(None, "tp"),
            P(),
            P(),
            P("tp", None),
            P(),
            P(None, "tp"),
            P(None, "tp"),
            P("tp", None),
        ),
        check_vma=False,
    )
```

```python
import functools

import jax
import jax.numpy as jnp
import numpy as np
from jax import lax
from jax.experimental import pallas as pl
from jax.experimental.pallas import tpu as pltpu
from jax.sharding import PartitionSpec as P

HEAD_SIZE = 64
LANES = 2 * HEAD_SIZE
EPSILON = 1e-05
ROPE_BASE = 1000000.0
LOG2E = 1.4426950408889634
VMEM_BYTES = 18 * 2**20
COST_SCALE = 4
FFN_COLS = 768
LATE = True
ALL_VMEM = 56 * 2**20
f32, bf16 = jnp.float32, jnp.bfloat16
NT = (((1,), (1,)), ((), ()))


class Ring:
    def __init__(self, n_ctx, sign=1):
        self.sign = sign
        n = self.n = n_ctx // 2
        self.zs = 4 if n % 4 == 0 else n
        self.ys = n // self.zs
        order = [int(self.chip_at(np.int32(place))) for place in range(n)]

        def steps(flip, turned):
            return [
                (order[i] * 2 + c, order[(i + sign * (1 - 2 * (c ^ turned))) % n] * 2 + (c ^ flip))
                for i in range(n)
                for c in (0, 1)
            ]

        self.onward, self.across, self.spread = steps(0, 0), steps(1, 0), steps(1, 1)
        self.to_sibling = [(i, i ^ 1) for i in range(n_ctx)]

    def chip_at(self, place):
        if self.ys == 1:
            return place
        where = np.where if isinstance(place, np.integer) else jnp.where
        turn = place - self.zs
        k, r = turn // (self.ys - 1), turn % (self.ys - 1)
        back = (self.zs - 1 - k) * self.ys + where(k % 2 == 0, 1 + r, self.ys - 1 - r)
        return where(place < self.zs, place * self.ys, back)

    def here(self):
        index = lax.axis_index("ctx")
        chip, core = index // 2, index % 2
        if self.ys == 1:
            return chip, core
        z, y = chip // self.ys, chip % self.ys
        k = self.zs - 1 - z
        back = self.zs + k * (self.ys - 1) + jnp.where(k % 2 == 0, y - 1, self.ys - 1 - y)
        return jnp.where(y == 0, z, back), core

    def at(self, slot):
        place, core = self.here()
        distance, other = slot
        ahead = self.sign * (1 - 2 * core) * distance
        return (place + ahead + self.n) % self.n, (core + other) % 2

    def device_at(self, slot):
        place, core = self.at(slot)
        return self.chip_at(place) * 2 + core

    def hop(self, x):
        return lax.ppermute(x, "ctx", self.onward)

    def sibling(self, x):
        return lax.ppermute(x, "ctx", self.to_sibling)


def total(*terms):
    out = terms[0].astype(f32)
    for term in terms[1:]:
        out = out + term.astype(f32)
    return out.astype(bf16)


class RingGather:
    def __init__(self, ring, own):
        self.ring, self.far = ring, ring.n // 2
        self.pieces = [([(0, 0)], own), ([(0, 1)], ring.sibling(own))]
        self.step = 0

    def sends(self):
        last = self.pieces[-2][1]
        if self.step == 0:
            return [self.pieces[0][1]]
        return [last[0]] if self.step + 1 == self.far else [last]

    def send(self, arrays):
        (x,) = arrays
        self.step += 1
        new = [self.ring.hop(x)]
        if self.step == 1:
            new.append(lax.ppermute(x, "ctx", self.ring.spread))
        return new

    def arrive(self, arrays):
        d = self.step
        if d == 1:
            new = [([(-1, c)], x) for c, x in enumerate(arrays)]
            pair = jnp.stack(arrays)
            self.pieces += [([(-1, 0), (-1, 1)], pair), ([(1, 1), (1, 0)], self.ring.sibling(pair))]
            return new
        (x,) = arrays
        if d == self.far:
            new = [([(d, 0)], x), ([(d, 1)], self.ring.sibling(x))]
        else:
            new = [([(-d, 0), (-d, 1)], x), ([(d, 1), (d, 0)], self.ring.sibling(x))]
        self.pieces += new
        return new[:1]

    def done(self):
        return self.step == self.far


def sum_steps(ring, terms, box=None):
    _, core = ring.here()
    far = ring.n // 2
    (x,) = yield [total(*terms(far))]
    (got,) = yield [ring.hop(x)]
    for d in range(far - 1, 1, -1):
        here = terms(d)
        if d == far - 1:
            x = jnp.stack([total(*[y[0] for y in here], got), total(*[y[1] for y in here])])
        else:
            x = total(*here, got)
        (x,) = yield [x]
        (got,) = yield [ring.hop(x)]
    here = terms(1)
    x = yield [total(*[y[c] for y in here], got[c]) for c in (0, 1)]
    got = yield [ring.hop(x[0]), lax.ppermute(x[1], "ctx", ring.across)]
    own = total(*terms(0), *got)
    if box is None:
        return own
    gather = RingGather(ring, own)
    box.append(gather)
    while not gather.done():
        late = [x for _, x in gather.pieces[-1:]]
        new = gather.send((yield gather.sends()))
        came = yield new + late
        gather.arrive(came[: len(new)])
    return gather


class Steps:
    def __init__(self, generator):
        self.generator, self.result = generator, None
        self.sent = self.came = None

    def arrivals(self):
        return self.generator.send(self.sent) if self.sent is not None else []

    def sends(self):
        try:
            return self.generator.send(self.came or None)
        except StopIteration as stop:
            self.result, self.generator = stop.value, None
            return []


def tied(lists, others):
    flat = lax.optimization_barrier((*[x for xs in lists for x in xs], *others))
    out = []
    for xs in lists:
        out.append(list(flat[: len(xs)]))
        flat = flat[len(xs) :]
    return out, flat


def advance(steps, *others):
    steps = [x for x in steps if x is not None and x.generator is not None]
    came, others = tied([x.arrivals() for x in steps], others)
    for x, arrays in zip(steps, came):
        x.came = arrays
    sends, others = tied([x.sends() for x in steps], others)
    for x, arrays in zip(steps, sends):
        x.sent = arrays
    return others


def sum_over_ctx(ring, arrays):
    n = ring.n
    far = n // 2
    outs = []
    for x in arrays:
        unit = x.shape[0] // (2 * n)
        cut = x.reshape(2, n, unit, x.shape[1])

        def piece(distance, other):
            place, core = ring.at((distance, other))
            return cut[core, place]

        def terms(d):
            if d in (0, far):
                return [piece(d, 0), ring.sibling(piece(d, 1))]
            keep = jnp.stack([piece(d, 0), piece(d, 1)])
            return [keep, ring.sibling(jnp.stack([piece(-d, 1), piece(-d, 0)]))]

        box = []
        steps = Steps(sum_steps(ring, terms, box))
        while steps.generator is not None:
            advance([steps])
        out = jnp.zeros(x.shape, f32)
        for slots, part in box[0].pieces:
            for i, slot in enumerate(slots):
                place, core = ring.at(slot)
                one = part if len(slots) == 1 else part[i]
                out = lax.dynamic_update_slice_in_dim(
                    out, one.astype(f32), (core * n + place) * unit, 0
                )
        outs.append(out)
    return outs


def exchange_steps(x):
    (x,) = yield [x]
    (theirs,) = yield [lax.ppermute(x, "tp", [(0, 1), (1, 0)])]
    return theirs


def pair_steps(x, exchanges):
    for axis, size, step in exchanges:
        (mine,) = yield [x]
        (theirs,) = yield [lax.ppermute(mine, axis, [(i, i ^ step) for i in range(size)])]
        x = mine + theirs
    return x


def bits(size):
    return [1 << k for k in range(size.bit_length() - 1)]


def from_other(xs):
    return [lax.ppermute(x, "tp", [(0, 1), (1, 0)]) for x in xs]


def sum_over_tp(x):
    size = lax.axis_size("tp")
    if size == 2:
        return x.astype(f32) + lax.ppermute(x, "tp", [(0, 1), (1, 0)]).astype(f32)
    return lax.psum(x, "tp").astype(f32)


def pair_count(slots, seq_count):
    return seq_count * (2 * len(slots) + ((0, 0) in slots))


class Tiles:
    def __init__(self, ring, slots, seq_count, blk, order_ref, starts_ref):
        self.ring, self.slots = ring, slots
        self.seq_count, self.blk = seq_count, blk
        self.order, self.starts = order_ref, starts_ref
        self.last = 4 * ring.n - 1
        self.rows = pair_count(slots, seq_count)

    def start_of(self, seq, place):
        start = jnp.int32(0)
        for d in range(3):
            at = self.starts[seq, d]
            start = jnp.where(place >= at, at, start)
        return start

    def pair(self, row):
        seq, row = row % self.seq_count, row // self.seq_count
        slot, which = row // 2, row % 2
        own = self.slots.index((0, 0)) if (0, 0) in self.slots else None
        if own is not None:
            both_high = slot == len(self.slots)
            slot = jnp.where(both_high, own, slot)
        distance, other = self.slots[0]
        for i, (d, c) in enumerate(self.slots):
            distance, other = jnp.where(slot == i, d, distance), jnp.where(slot == i, c, other)
        mine = self.order[lax.axis_index("ctx")]
        theirs = self.order[self.ring.device_at((distance, other))]
        low = (which == 1) & (theirs <= mine)
        high = (which == 1) & (theirs > mine)
        if own is not None:
            low, high = low & jnp.logical_not(both_high), high | both_high
        q_place = jnp.where(low, mine, self.last - mine) * self.blk
        k_place = jnp.where(high, self.last - theirs, theirs) * self.blk
        q_tile = 2 * seq + jnp.where(low, 0, 1)
        k_tile = 2 * (self.seq_count * slot + seq) + jnp.where(high, 1, 0)
        k_end, q_end = k_place + self.blk - 1, q_place + self.blk - 1
        whole = (k_end <= q_place) & (k_place >= self.start_of(seq, q_end))
        empty = k_end < self.start_of(seq, q_place)
        kind = jnp.where(whole, 0, jnp.where(empty, 2, 1))
        return q_tile, k_tile, kind, (seq, q_place, k_place)

    def allowed(self, at, query_axis, shape):
        seq, q_place, k_place = at
        query = q_place + lax.broadcasted_iota(jnp.int32, shape, query_axis) % self.blk
        key = k_place + lax.broadcasted_iota(jnp.int32, shape, 1 - query_axis)
        return (key <= query) & (key >= self.start_of(seq, query))

    def run(self, tile):
        def body(row, carry):
            q_tile, k_tile, kind, at = self.pair(row)
            keys = pl.ds(pl.multiple_of(k_tile * self.blk, self.blk), self.blk)
            pl.when(kind == 0)(lambda: tile(q_tile, keys, None))
            pl.when(kind == 1)(lambda: tile(q_tile, keys, functools.partial(self.allowed, at)))
            return carry

        lax.fori_loop(0, self.rows, body, 0)


def load_chunks(chunks, kv_ref):
    at = 0
    for chunk in chunks:
        for part in [chunk] if len(chunk.shape) == 2 else [chunk.at[0], chunk.at[1]]:
            kv_ref[at : at + part.shape[0]] = part[...]
            at += part.shape[0]


def forward_kernel(make, parts, heads, order_ref, starts_ref, q_ref, *refs):
    chunks, held, (out_ref, kv_ref) = refs[:parts], refs[parts:-2], refs[-2:]
    tiles = make(order_ref, starts_ref)
    blk = tiles.blk
    first = lax.broadcasted_iota(jnp.int32, (blk, LANES), 1) < HEAD_SIZE
    load_chunks(chunks, kv_ref)
    out_ref[...] = held[0][...] if held else jnp.zeros_like(out_ref)

    def tile(q_tile, keys, mask):
        if mask is not None:
            allowed = mask(0, (q_ref.shape[2], blk))
        for h in range(heads):
            kv = kv_ref[keys, h * LANES : (h + 1) * LANES]
            scores = lax.dot_general(q_ref[h, q_tile], kv, NT, preferred_element_type=f32)
            weights = jnp.exp2(scores * LOG2E)
            if mask is not None:
                weights = jnp.where(allowed, weights, 0.0)
            one_v = jnp.where(first, jnp.ones_like(kv), kv)
            out_ref[h, q_tile] += jnp.dot(weights.astype(bf16), one_v, preferred_element_type=f32)

    tiles.run(tile)


def backward_kernel(make, parts, held, heads, order_ref, starts_ref, q_ref, do_ref, stat_ref, *refs):
    chunks, held, refs = refs[:parts], refs[parts : parts + held], refs[parts + held :]
    dq_ref, keep_ref, give_ref, kv_ref, dkv_ref = refs
    tiles = make(order_ref, starts_ref)
    blk = tiles.blk
    load_chunks(chunks, kv_ref)
    dq_ref[...] = held[0][...] if held else jnp.zeros_like(dq_ref)
    dkv_ref[...] = jnp.zeros_like(dkv_ref)

    def tile(q_tile, keys, mask):
        if mask is not None:
            allowed = mask(1, (blk, q_ref.shape[2]))
        for h in range(heads):
            cols = slice(h * LANES, (h + 1) * LANES)
            kv = kv_ref[keys, cols]
            q = q_ref[h, q_tile]
            do = do_ref[h, q_tile]
            scores = lax.dot_general(kv, q, NT, preferred_element_type=f32)
            back_probs = lax.dot_general(kv, do, NT, preferred_element_type=f32)
            probs = jnp.exp2(scores * LOG2E - stat_ref[h, q_tile, 0:1])
            if mask is not None:
                probs = jnp.where(allowed, probs, 0.0)
            back_scores = (probs * (back_probs - stat_ref[h, q_tile, 1:2])).astype(bf16)
            both = jnp.concatenate([probs.astype(bf16), back_scores], axis=1)
            dkv_ref[keys, cols] += jnp.dot(
                both, jnp.concatenate([do, q], axis=0), preferred_element_type=f32
            )
            dq_ref[h, q_tile] += jnp.dot(kv.T[:HEAD_SIZE], back_scores, preferred_element_type=f32)

    tiles.run(tile)
    rows = keep_ref.shape[-2]
    if len(keep_ref.shape) == 2:
        keep_ref[...] = dkv_ref[:rows]
        give_ref[...] = dkv_ref[rows:].astype(bf16)
        return
    for c in (0, 1):
        keep_ref[c] = dkv_ref[(3 - c) * rows : (4 - c) * rows]
        give_ref[c] = dkv_ref[(1 - c) * rows : (2 - c) * rows].astype(bf16)


def in_smem():
    return pl.BlockSpec(memory_space=pltpu.SMEM)


def in_vmem():
    return pl.BlockSpec(memory_space=pltpu.VMEM)


class Attention:
    def __init__(self, ring, block_order, starts, blk):
        self.ring, self.order, self.starts = ring, block_order, starts
        self.blk, self.seq_count = blk, starts.shape[0]

    def _make(self, slots):
        return lambda order_ref, starts_ref: Tiles(
            self.ring, slots, self.seq_count, self.blk, order_ref, starts_ref
        )

    def _cost(self, slots, heads, products, arrays):
        tile = 2 * self.blk * self.blk * heads * pair_count(slots, self.seq_count)
        return pl.CostEstimate(
            flops=2 * tile * 256 * products // COST_SCALE,
            bytes_accessed=sum(x.size * x.dtype.itemsize for x in arrays) // COST_SCALE,
            transcendentals=tile // COST_SCALE,
        )

    def forward(self, pieces, q, acc):
        heads, tiles, rows, _ = q.shape
        out = jax.ShapeDtypeStruct((heads, tiles, rows, LANES), f32)
        held = [] if acc is None else [acc]
        slots, chunks = [x for xs, _ in pieces for x in xs], [x for _, x in pieces]
        keys, width = len(slots) * chunks[0].shape[-2], chunks[0].shape[-1]
        return pl.pallas_call(
            functools.partial(forward_kernel, self._make(slots), len(chunks), heads),
            out_shape=out,
            in_specs=[in_smem()] * 2 + [in_vmem()] * (1 + len(chunks) + len(held)),
            out_specs=in_vmem(),
            scratch_shapes=[pltpu.VMEM((keys, width), bf16)],
            compiler_params=pltpu.CompilerParams(vmem_limit_bytes=VMEM_BYTES),
            cost_estimate=self._cost(slots, heads, 2, [q, *chunks, out, out]),
            name="attend_forward",
        )(self.order, self.starts, q, *chunks, *held)

    def backward(self, pieces, q, do, stats, acc):
        heads, tiles, rows, _ = q.shape
        slots, chunks = [x for xs, _ in pieces for x in xs], [x for _, x in pieces]
        keys, width = len(slots) * chunks[0].shape[-2], chunks[0].shape[-1]
        outs = [
            jax.ShapeDtypeStruct((heads, tiles, HEAD_SIZE, rows), f32),
            jax.ShapeDtypeStruct(chunks[0].shape, f32),
            jax.ShapeDtypeStruct(chunks[0].shape, bf16),
        ]
        held = [] if acc is None else [acc]
        return pl.pallas_call(
            functools.partial(
                backward_kernel, self._make(slots), len(chunks), len(held), heads
            ),
            out_shape=outs,
            in_specs=[in_smem()] * 2 + [in_vmem()] * (3 + len(chunks) + len(held)),
            out_specs=[in_vmem()] * len(outs),
            scratch_shapes=[pltpu.VMEM((keys, width), bf16), pltpu.VMEM((keys, width), f32)],
            compiler_params=pltpu.CompilerParams(vmem_limit_bytes=VMEM_BYTES),
            cost_estimate=self._cost(slots, heads, 5, [q, do, outs[0], *chunks, *outs]),
            name="attend_backward",
        )(self.order, self.starts, q, do, stats, *chunks, *held)


def grads_kernel(ring, *refs):
    two, gate, up, ffn, cot = (refs[2 * i : 2 * i + 2] for i in range(5))
    outs, (lhs_ref, cot_ref, all_ref) = refs[10:-3], refs[-3:]

    @pl.when(pl.program_id(0) == 0)
    def _():
        lhs_ref[...] = jnp.concatenate([x[...] for x in two], axis=0).T
        cot_ref[...] = jnp.concatenate([x[...] for x in cot], axis=0)

    n = ring.n
    unit = lhs_ref.shape[0] // (2 * n)
    cols = gate[0].shape[2]
    thin = cols // (2 * n)
    for i, half in enumerate((gate, up)):
        right = jnp.concatenate([x[0] for x in half], axis=0)
        grad = jnp.dot(lhs_ref[...], right, preferred_element_type=f32).astype(bf16)
        all_ref[:, i * unit : (i + 1) * unit] = grad.reshape(2 * n, unit, cols)
    left = jnp.concatenate([x[0] for x in ffn], axis=0).T
    down = jnp.dot(left, cot_ref[...], preferred_element_type=f32).astype(bf16)
    down = down.reshape(2 * n, thin, down.shape[1])
    for k in range(down.shape[2] // cols):
        at = 2 * unit + k * thin
        all_ref[:, at : at + thin] = down[:, :, k * cols : (k + 1) * cols]
    deal(ring, lambda at: all_ref[at], lambda ref, x: ref.at[0].__setitem__(..., x), outs)


def deal(ring, read, write, outs):
    far = ring.n // 2

    def part(distance, other):
        place, core = ring.at((distance, other))
        return read(core * ring.n + place)

    keep_far, give_far, *keep, give = outs
    write(keep_far, part(far, 0))
    write(give_far, part(far, 1))
    write(keep[0], part(0, 0))
    write(give.at[0], part(0, 1))
    for d in range(1, far):
        for c in (0, 1):
            write(keep[d].at[c], part(d, c))
            write(give.at[2 * d - 1 + c], part(-d, 1 - c))


def dealt(ring, cut):
    far = ring.n // 2
    heads = [(), (), ()] + [(2,)] * (far - 1) + [(2 * far - 1,)]
    return [jax.ShapeDtypeStruct((*head, *cut.shape), cut.dtype) for head in heads]


def exchanged(ring, outs, *others):
    keep_far, give_far, *keep, give = outs
    give, got_far, *others = lax.optimization_barrier((give, ring.sibling(give_far), *others))
    return [keep_far, got_far, *keep, ring.sibling(give)], others


def dealt_terms(ring, outs):
    far = ring.n // 2
    keep_far, got_far, *keep, got = outs

    def terms(d):
        if d == far:
            return [keep_far, got_far]
        if d == 0:
            return [keep[0], got[0]]
        return [keep[d], got[2 * d - 1 : 2 * d + 1]]

    return terms


def ffn_grads(ring, hidden_two, back_gate, back_up, hidden_ffn, cotangent):
    rows, width = hidden_two[0].shape
    blocks, _, cols = back_gate[0].shape
    units = blocks * cols
    n = ring.n
    wide = width // (2 * n) * 3
    whole = [pl.BlockSpec((rows, width), lambda j: (0, 0))] * 2
    block = [pl.BlockSpec((1, rows, cols), lambda j: (j, 0, 0))] * 2
    outs = dealt(ring, shape(units // cols, wide, cols, dtype=bf16))
    cuts = [
        pl.BlockSpec(
            (*x.shape[:-3], 1, wide, cols), lambda j, k=len(x.shape): (0,) * (k - 3) + (j, 0, 0)
        )
        for x in outs
    ]
    return pl.pallas_call(
        functools.partial(grads_kernel, ring),
        grid=(units // cols,),
        out_shape=outs,
        in_specs=whole + block * 3 + whole,
        out_specs=cuts,
        scratch_shapes=[
            pltpu.VMEM((width, 2 * rows), bf16),
            pltpu.VMEM((2 * rows, width), bf16),
            pltpu.VMEM((2 * n, wide, cols), bf16),
        ],
        compiler_params=pltpu.CompilerParams(vmem_limit_bytes=VMEM_BYTES),
        cost_estimate=pl.CostEstimate(
            flops=12 * rows * width * units // COST_SCALE, bytes_accessed=2**20, transcendentals=0
        ),
        name="ffn_grads",
    )(*hidden_two, *back_gate, *back_up, *hidden_ffn, *cotangent)


def place_kernel(ring, slots, count, *refs):
    arrays, outs, (wide_ref, down_ref, sem) = refs[:count], refs[-6:-3], refs[-3:]
    parts = [y for x in arrays for y in ([x] if len(x.shape) == 3 else [x.at[0], x.at[1]])]
    n = ring.n
    blocks, _, cols = parts[0].shape
    unit = outs[0].shape[0] // (2 * n)
    thin = cols // (2 * n)
    copies = []
    for i, slot in enumerate(slots):
        part = parts[i]
        place, core = ring.at(slot)
        r = core * n + place
        for w in range(2):
            for j in range(blocks):
                wide_ref[i, w, :, j * cols : (j + 1) * cols] = part[
                    j, w * unit : (w + 1) * unit
                ].astype(f32)
            rows = pl.ds(pl.multiple_of(r * unit, unit), unit)
            copies.append((wide_ref.at[i, w], outs[w].at[rows]))
        for j in range(blocks):
            for k in range(outs[2].shape[1] // cols):
                at = 2 * unit + k * thin
                down_ref[i, j, :, k * cols : (k + 1) * cols] = part[j, at : at + thin].astype(f32)
            rows = pl.ds(pl.multiple_of(j * cols + r * thin, thin), thin)
            copies.append((down_ref.at[i, j], outs[2].at[rows]))
        for k in range(i * (2 + blocks), (i + 1) * (2 + blocks)):
            pltpu.make_async_copy(*copies[k], sem.at[k]).start()
    for k, pair in enumerate(copies):
        pltpu.make_async_copy(*pair, sem.at[k]).wait()


def place_ffn(ring, pieces, width, held):
    slots, parts = [x for xs, _ in pieces for x in xs], [x for _, x in pieces]
    blocks, wide, cols = parts[0].shape[-3:]
    units = blocks * cols
    count = len(slots)
    thin = cols // (2 * ring.n)
    anywhere = pl.BlockSpec(memory_space=pl.ANY)
    return pl.pallas_call(
        functools.partial(place_kernel, ring, slots, len(parts)),
        out_shape=[shape(width, units), shape(width, units), shape(units, width)],
        in_specs=[in_vmem()] * len(parts) + [anywhere] * len(held),
        out_specs=[anywhere] * 3,
        input_output_aliases={len(parts) + i: i for i in range(len(held))},
        scratch_shapes=[
            pltpu.VMEM((count, 2, width // (2 * ring.n), units), f32),
            pltpu.VMEM((count, blocks, thin, width), f32),
            pltpu.SemaphoreType.DMA((count * (2 + blocks),)),
        ],
        compiler_params=pltpu.CompilerParams(vmem_limit_bytes=VMEM_BYTES),
        cost_estimate=pl.CostEstimate(
            flops=0, bytes_accessed=8 * count * wide * units, transcendentals=0
        ),
        name="place_ffn",
    )(*parts, *held)


def place_qkv_kernel(ring, slots, *refs):
    arrays, (query_ref, key_ref, value_ref, out_ref) = refs[:-4], refs[-4:]
    parts = [y for x in arrays for y in ([x] if len(x.shape) == 2 else [x.at[0], x.at[1]])]
    n = ring.n
    unit, thin = query_ref.shape[0] // (2 * n), out_ref.shape[0] // (2 * n)
    for slot, part in zip(slots, parts):
        place, core = ring.at(slot)
        r = core * n + place
        rows = pl.ds(pl.multiple_of(r * unit, unit), unit)
        at = query_ref.shape[1]
        query_ref[rows] = part[:unit, :at].astype(f32)
        for h in range(key_ref.shape[1] // HEAD_SIZE):
            cols = slice(h * HEAD_SIZE, (h + 1) * HEAD_SIZE)
            both = part[:unit, at + h * LANES : at + (h + 1) * LANES].astype(f32)
            key_ref[rows, cols] = both[:, :HEAD_SIZE]
            value_ref[rows, cols] = both[:, HEAD_SIZE:]
        rows = pl.ds(pl.multiple_of(r * thin, thin), thin)
        out_ref[rows] = part[unit:].astype(f32)


def place_qkv(ring, pieces, width, cols):
    slots, parts = [x for xs, _ in pieces for x in xs], [x for _, x in pieces]
    thin = parts[0].shape[-2] - width // (2 * ring.n)
    return whole_call(
        functools.partial(place_qkv_kernel, ring, slots),
        "place_qkv",
        [shape(width, c) for c in cols] + [shape(thin * 2 * ring.n, width)],
        parts,
        0,
    )


def whole_call(kernel, name, outs, args, flops, scratch=(), scalars=(0, 0), vmem=VMEM_BYTES):
    moved = sum(x.size * x.dtype.itemsize for x in (*outs, *args))
    return pl.pallas_call(
        kernel,
        out_shape=list(outs),
        in_specs=[in_smem()] * scalars[0] + [in_vmem()] * (len(args) - scalars[0]),
        out_specs=[in_smem()] * scalars[1] + [in_vmem()] * (len(outs) - scalars[1]),
        scratch_shapes=list(scratch),
        compiler_params=pltpu.CompilerParams(vmem_limit_bytes=vmem),
        cost_estimate=pl.CostEstimate(
            flops=flops // COST_SCALE, bytes_accessed=moved // COST_SCALE, transcendentals=0
        ),
        name=name,
    )(*args)


def shape(*dims, dtype=f32):
    return jax.ShapeDtypeStruct(dims, dtype)


def first_lanes(rows):
    return lax.broadcasted_iota(jnp.int32, (rows, LANES), 1) < HEAD_SIZE


def head_mean(x):
    i = lax.broadcasted_iota(jnp.int32, (LANES, LANES), 0) // HEAD_SIZE
    j = lax.broadcasted_iota(jnp.int32, (LANES, LANES), 1) // HEAD_SIZE
    mean = jnp.where(i == j, 1.0 / HEAD_SIZE, 0.0).astype(bf16)
    high = x.astype(bf16)
    low = (x - high.astype(f32)).astype(bf16)
    return jnp.dot(high, mean, preferred_element_type=f32) + jnp.dot(
        low, mean, preferred_element_type=f32
    )


def turn(x, cosine, sines):
    lane = lax.broadcasted_iota(jnp.int32, x.shape, 1) % HEAD_SIZE
    half = HEAD_SIZE // 2
    other = jnp.where(
        lane < half, pltpu.roll(x, LANES - half, axis=1), pltpu.roll(x, half, axis=1)
    )
    return x * cosine + other * sines


def row_scale(x):
    return lax.rsqrt(jnp.mean(x * x, axis=-1, keepdims=True) + EPSILON)


def norm_back(upstream, x, scale, gain):
    inner = upstream * gain
    return scale * (inner - x * (scale * scale * jnp.mean(inner * x, axis=-1, keepdims=True)))


def head_norm_back(upstream, x, gain):
    scale = lax.rsqrt(head_mean(x * x) + EPSILON)
    inner = upstream * gain
    back = scale * (inner - x * (scale * scale * head_mean(inner * x)))
    return back, jnp.sum(upstream * x * scale, axis=0, keepdims=True)


def gain_of(ref):
    return ref[...].astype(f32)


def head_gain(ref):
    return jnp.concatenate([gain_of(ref)] * 2, axis=1)


def lanes(tile):
    return slice(tile * LANES, (tile + 1) * LANES)


def project_kv_kernel(
    tiles, last, order, segments, tokens, gain, w_key, w_value, key_gain, inverse, *refs
):
    starts, hidden, kv_raw, kv, w_kv, cosine, sines = refs
    x = tokens[...].astype(f32)
    hidden[...] = (x * row_scale(x) * gain_of(gain)).astype(bf16)
    rows = x.shape[0]
    blk = rows // tiles
    mine = order[lax.axis_index("ctx")]
    lane = lax.broadcasted_iota(jnp.int32, (blk, LANES), 1) % HEAD_SIZE
    for t in range(tiles):
        block = last - mine if t % 2 else mine
        place = block * blk + lax.broadcasted_iota(jnp.int32, (blk, LANES), 0)
        angles = place.astype(f32) * inverse[...]
        at = slice(t * blk, (t + 1) * blk)
        cosine[at] = jnp.cos(angles)
        sine = jnp.sin(angles)
        sines[at] = jnp.where(lane < HEAD_SIZE // 2, -sine, sine)
    first = first_lanes(rows)
    for h in range(kv.shape[1] // LANES):
        cols = slice(h * HEAD_SIZE, (h + 1) * HEAD_SIZE)
        w_kv[:, lanes(h)] = jnp.concatenate([w_key[:, cols], w_value[:, cols]], axis=1)
        raw = jnp.dot(hidden[...], w_kv[:, lanes(h)], preferred_element_type=f32)
        kv_raw[:, lanes(h)] = raw
        normed = raw * lax.rsqrt(head_mean(raw * raw) + EPSILON) * head_gain(key_gain)
        kv[:, lanes(h)] = jnp.where(first, turn(normed, cosine[...], sines[...]), raw).astype(bf16)
    for seq in range(segments.shape[0]):
        for d in range(3):
            before = jnp.where(segments[seq : seq + 1] <= d, 1.0, 0.0)
            starts[seq, d] = jnp.sum(before).astype(jnp.int32)


def project_q_kernel(tiles, hidden, w_query, query_gain, cosine, sines, query_raw, q_tiles):
    rows = hidden.shape[0]
    blk = rows // tiles
    first = first_lanes(rows)
    for h in range(q_tiles.shape[0]):
        raw = jnp.dot(hidden[...], w_query[:, lanes(h)], preferred_element_type=f32)
        query_raw[:, lanes(h)] = raw
        normed = raw * lax.rsqrt(head_mean(raw * raw) + EPSILON) * head_gain(query_gain)
        turned = turn(normed, cosine[...], sines[...]).astype(bf16).astype(f32) * 0.125
        pair = [
            jnp.where(first, turned, 0.0),
            jnp.where(first, pltpu.roll(turned, HEAD_SIZE, axis=1), 0.0),
        ]
        for g, one in enumerate(pair):
            for t in range(tiles):
                q_tiles[h, t, g * blk : (g + 1) * blk] = one[t * blk : (t + 1) * blk].astype(bf16)


def half_rows(pair, rows, which):
    first = (lax.axis_index("tp") + which) % 2 if pair else which
    return pl.ds(pl.multiple_of(first * (rows // 2), rows // 2), rows // 2)


def mix_kernel(pair, acc, w_out, attended, o, lse, *halves):
    heads, tiles, rows, _ = acc.shape
    blk = rows // 2
    first = first_lanes(rows)
    for h in range(heads):
        for t in range(tiles):
            x = acc[h, t]
            value = jnp.where(first, 0.0, x * pltpu.roll(1.0 / x, HEAD_SIZE, axis=1))
            o[h, t] = value
            lse[h, t] = jnp.log2(x.T[:8])
            low = pltpu.roll(value[:blk], HEAD_SIZE, axis=1) + value[blk:]
            attended[t * blk : (t + 1) * blk, lanes(h)] = low.astype(bf16)
    for which, half in enumerate(halves):
        rows = half_rows(pair, attended.shape[0], which)
        half[...] = jnp.dot(attended[rows], w_out[...], preferred_element_type=f32).astype(bf16)


def ffn_kernel(tokens, attn, gain, hidden_back, w_gate, w_up, *refs):
    mixed, hidden_two, hidden_ffn, back_gate, back_up, gain_grad, low, sums = refs
    step, last = pl.program_id(0), pl.num_programs(0) - 1

    @pl.when(step == 0)
    def _():
        x = tokens[...].astype(f32) + attn[...].astype(f32)
        mixed[...] = x
        hidden_two[...] = (x * row_scale(x) * gain_of(gain)).astype(bf16)
        sums[...] = jnp.zeros_like(sums)

    gating = jnp.dot(hidden_two[...], w_gate[...], preferred_element_type=f32)
    lifted = jnp.dot(hidden_two[...], w_up[...], preferred_element_type=f32)
    upstream = hidden_back[...]
    logistic = jax.nn.sigmoid(gating)
    silu = gating * logistic
    gate = (upstream * lifted * logistic * (1.0 + gating * (1.0 - logistic))).astype(bf16)
    up = (upstream * silu).astype(bf16)
    ffn = (silu * lifted).astype(bf16)
    for ref, value in ((hidden_ffn, ffn), (back_gate, gate), (back_up, up)):
        cols = ref.shape[2]
        for k in range(ref.shape[0]):
            ref[k] = value[:, k * cols : (k + 1) * cols]
    sums[...] += lax.dot_general(gate, w_gate[...], NT, preferred_element_type=f32)
    sums[...] += lax.dot_general(up, w_up[...], NT, preferred_element_type=f32)

    @pl.when(step == last)
    def _():
        x = mixed[...]
        gain_grad[...] = jnp.sum(sums[...] * x * row_scale(x), axis=0, keepdims=True)
        low[...] = sums[...].astype(bf16)


def block_cols(units):
    return 256 if units % 256 == 0 else units


def feed_forward(tokens, attn, gain, hidden_back, w_gate, w_up):
    rows, width = tokens.shape
    units = w_gate.shape[1]
    cols = FFN_COLS if units % FFN_COLS == 0 else units
    thin = block_cols(units)
    whole = pl.BlockSpec((rows, width), lambda j: (0, 0))
    line = pl.BlockSpec((1, width), lambda j: (0, 0))
    weight = pl.BlockSpec((width, cols), lambda j: (0, j))
    block = pl.BlockSpec((cols // thin, rows, thin), lambda j: (j, 0, 0))
    low = shape(units // thin, rows, thin, dtype=bf16)
    return pl.pallas_call(
        ffn_kernel,
        grid=(units // cols,),
        out_shape=[shape(rows, width), shape(rows, width, dtype=bf16), low, low, low]
        + [shape(1, width), shape(rows, width, dtype=bf16)],
        in_specs=[whole, whole, line, pl.BlockSpec((rows, cols), lambda j: (0, j)), weight, weight],
        out_specs=[whole, whole, block, block, block, line, whole],
        scratch_shapes=[pltpu.VMEM((rows, width), f32)],
        compiler_params=pltpu.CompilerParams(vmem_limit_bytes=VMEM_BYTES),
        cost_estimate=pl.CostEstimate(
            flops=8 * rows * width * units // COST_SCALE, bytes_accessed=2**20, transcendentals=0
        ),
        name="feed_forward",
    )(tokens, attn, gain, hidden_back, w_gate, w_up)


def down_kernel(pair, *refs):
    ffn, w_down, out = refs[:2], refs[2], refs[3]
    cols = ffn[0].shape[2]
    for which, x in enumerate(ffn):
        part = jnp.zeros((x.shape[1], out.shape[1]), f32)
        for k in range(x.shape[0]):
            part += jnp.dot(
                x[k], w_down[k * cols : (k + 1) * cols], preferred_element_type=f32
            )
        out[half_rows(pair, out.shape[0], which)] = part.astype(bf16)


def back_kernel(pair, cotangent, gain, w_out, o, lse, *refs):
    mixed, mine, theirs, (back_mixed, back_proj, do_tiles, stats) = (
        refs[:2],
        refs[2:4],
        refs[4:6],
        refs[6:],
    )
    for which in (0, 1):
        rows = half_rows(pair, cotangent.shape[0], which)
        x = mixed[which][...]
        upstream = mine[which][...].astype(f32) + theirs[which][...].astype(f32)
        back = cotangent[rows].astype(f32) + norm_back(upstream, x, row_scale(x), gain_of(gain))
        back_mixed[rows] = back
        back_proj[rows] = back.astype(bf16)
    heads, tiles, rows, _ = o.shape
    blk = rows // 2
    first = first_lanes(blk)
    row = lax.broadcasted_iota(jnp.int32, (8, rows), 0)
    for h in range(heads):
        attn = lax.dot_general(back_proj[...], w_out[lanes(h)], NT, preferred_element_type=f32)
        for t in range(tiles):
            here = attn[t * blk : (t + 1) * blk]
            do = jnp.concatenate(
                [
                    jnp.where(first, 0.0, pltpu.roll(here, HEAD_SIZE, axis=1)),
                    jnp.where(first, 0.0, here),
                ],
                axis=0,
            ).astype(bf16)
            do_tiles[h, t] = do
            delta = jnp.sum((do.astype(f32) * o[h, t]).T, axis=0, keepdims=True)
            stats[h, t] = jnp.where(row == 0, lse[h, t], delta)


def back_query_kernel(dq, query_raw, query_gain, cosine, sines, query_delta, gain_grad):
    heads, tiles, _, rows = dq.shape
    blk = rows // 2
    gain_grad[...] = jnp.zeros_like(gain_grad)
    for t in range(tiles):
        at = slice(t * blk, (t + 1) * blk)
        for h in range(heads):
            both = jnp.concatenate([dq[h, t, :, :blk], dq[h, t, :, blk:]], axis=0) * 0.125
            turned = turn(both.T, cosine[at], -sines[at])
            back, gain_terms = head_norm_back(turned, query_raw[at, lanes(h)], head_gain(query_gain))
            query_delta[at, lanes(h)] = back.astype(bf16)
            gain_grad[...] += gain_terms


def back_project_kernel(
    ring,
    tokens,
    hidden,
    query_delta,
    own_dkv,
    kv_raw,
    key_gain,
    cosine,
    sines,
    w_query,
    w_kv,
    attended,
    back_proj,
    *refs,
):
    low, norm_grad, gain_grad, kv_delta = refs[:4]
    outs, all_ref = refs[4:-1], refs[-1]
    rows, width = tokens.shape
    first = first_lanes(rows)
    gain_grad[...] = jnp.zeros_like(gain_grad)
    for h in range(own_dkv.shape[1] // LANES):
        dkv = own_dkv[:, lanes(h)].astype(f32)
        turned = turn(dkv, cosine[...], -sines[...])
        back, gain_terms = head_norm_back(turned, kv_raw[:, lanes(h)], head_gain(key_gain))
        kv_delta[:, lanes(h)] = jnp.where(first, back, dkv).astype(bf16)
        gain_grad[...] += gain_terms
    part = lax.dot_general(
        query_delta[...], w_query[...], NT, preferred_element_type=f32
    ) + lax.dot_general(kv_delta[...], w_kv[...], NT, preferred_element_type=f32)
    low[...] = part.astype(bf16)
    x = tokens[...].astype(f32)
    norm_grad[...] = jnp.sum(part * x * row_scale(x), axis=0, keepdims=True)
    if not outs:
        return
    lhs = hidden[...].T
    n = ring.n
    unit = width // (2 * n)
    q_cols = query_delta.shape[1]
    for cols, right in (
        (slice(0, q_cols), query_delta),
        (slice(q_cols, q_cols + kv_delta.shape[1]), kv_delta),
    ):
        grad = jnp.dot(lhs, right[...], preferred_element_type=f32).astype(bf16)
        all_ref[:, :unit, cols] = grad.reshape(2 * n, unit, grad.shape[1])
    grad = jnp.dot(attended[...].T, back_proj[...], preferred_element_type=f32).astype(bf16)
    all_ref[:, unit:] = grad.reshape(2 * n, -1, width)
    deal(ring, lambda at: all_ref[at], lambda ref, x: ref.__setitem__(..., x), outs)


def dot(a, b, dims):
    return lax.dot_general(a, b, ((dims[:1], dims[1:]), ((), ())), preferred_element_type=f32)


def on_device(
    tokens,
    cotangent,
    block_order,
    segment_ids,
    norm_gain,
    w_query,
    key_weight,
    value_weight,
    query_gain,
    key_gain,
    w_out,
    ffn_gain,
    w_gate,
    w_up,
    w_down,
):
    devices = lax.axis_size("ctx")
    ring = Ring(devices)
    other_ring = Ring(devices, -1)
    far = ring.n // 2
    rows, width = tokens.shape
    seq_count = segment_ids.shape[0]
    blk = rows // seq_count // 2
    tiles = 2 * seq_count
    kv_heads = key_weight.shape[1] // HEAD_SIZE
    q_cols, k_cols = w_query.shape[1], key_weight.shape[1]
    units = w_gate.shape[1]
    packed = units % 256 == 0 and width % (32 * ring.n) == 0 and w_out.shape[0] % (32 * ring.n) == 0
    pair = lax.axis_size("tp") == 2

    def line(x):
        return x.reshape(1, -1)

    inverse = ROPE_BASE ** (-np.arange(0, HEAD_SIZE, 2) / HEAD_SIZE)
    inverse = np.tile(inverse, 4)[None, :].astype(np.float32)
    starts, hidden_input, kv_raw, own_kv, w_kv, cosine, sines = whole_call(
        functools.partial(project_kv_kernel, tiles, 2 * devices - 1),
        "project_kv",
        [
            shape(seq_count, 3, dtype=jnp.int32),
            shape(rows, width, dtype=bf16),
            shape(rows, 2 * k_cols),
            shape(rows, 2 * k_cols, dtype=bf16),
            shape(width, 2 * k_cols, dtype=bf16),
            shape(rows, LANES),
            shape(rows, LANES),
        ],
        [
            block_order,
            segment_ids,
            tokens,
            line(norm_gain),
            key_weight,
            value_weight,
            line(key_gain),
            jnp.asarray(inverse),
        ],
        4 * rows * width * k_cols,
        scalars=(1, 1),
        vmem=ALL_VMEM,
    )
    gather = RingGather(ring, own_kv)
    flying = gather.send(gather.sends())
    query_raw, q_tiles = whole_call(
        functools.partial(project_q_kernel, tiles),
        "project_q",
        [shape(rows, q_cols), shape(kv_heads, tiles, 2 * blk, LANES, dtype=bf16)],
        [hidden_input, w_query, line(query_gain), cosine, sines],
        2 * rows * width * q_cols,
    )

    attention = Attention(ring, block_order, starts, blk)
    acc = attention.forward(gather.pieces[:1], q_tiles, None)
    late = gather.pieces[1]
    while True:
        *came, acc = lax.optimization_barrier((*flying, acc))
        now = gather.arrive(came)
        if gather.done():
            break
        flying = gather.send(gather.sends())
        acc = attention.forward([late, *now], q_tiles, acc)
        late = gather.pieces[-1]
    acc = attention.forward([late], q_tiles, acc)
    acc = attention.forward(gather.pieces[-2:], q_tiles, acc)
    kv_pieces = {
        max(abs(d) for d, _ in slots): gather.pieces[i - 1 : i + 1]
        for i, (slots, _) in enumerate(gather.pieces)
        if i % 2
    }
    attended, o, lse, attn_mine, attn_send = whole_call(
        functools.partial(mix_kernel, pair),
        "mix",
        [
            shape(rows, q_cols, dtype=bf16),
            shape(*acc.shape),
            shape(kv_heads, tiles, 8, 2 * blk),
            shape(rows // 2, width, dtype=bf16),
            shape(rows // 2, width, dtype=bf16),
        ],
        [acc, w_out],
        2 * rows * width * q_cols,
    )

    def halves_of(x):
        at = lax.axis_index("tp") if pair else 0
        return [
            lax.dynamic_slice_in_dim(x, (at + k) % 2 * (rows // 2), rows // 2, 0) for k in (0, 1)
        ]

    def from_first(xs):
        at = lax.axis_index("tp") if pair else 0
        return jnp.concatenate([jnp.where(at == k, xs[0], xs[1]) for k in (0, 1)])

    cots, toks = halves_of(cotangent), halves_of(tokens)
    if pair:
        (attn_theirs,) = from_other([attn_send])
        upstream = [dot(x, w_down, (1, 1)) for x in cots]
        attn_theirs, *upstream = lax.optimization_barrier((attn_theirs, *upstream))
        attn = total(attn_mine, attn_theirs)
    else:
        attn, attn_next = lax.psum((attn_mine, attn_send), "tp")
        upstream = [dot(x, w_down, (1, 1)) for x in cots]

    def feed(k, attn):
        return feed_forward(toks[k], attn, line(ffn_gain), upstream[k], w_gate, w_up)

    if pair:
        (attn_next,) = from_other([attn])
        fed = [feed(0, attn)]
        attn_next, *fed[0] = lax.optimization_barrier((attn_next, *fed[0]))
        (last,) = from_other([fed[0][-1]])
        fed.append(feed(1, attn_next))
        last, *fed[1] = lax.optimization_barrier((last, *fed[1]))
        (first,) = from_other([fed[1][-1]])
    else:
        fed = [feed(0, attn), feed(1, attn_next)]
        first, last = lax.psum((fed[0][-1], fed[1][-1]), "tp")
    mixed, hidden_two, hidden_ffn, back_gate, back_up, ffn_gain_grads, mine = zip(*fed)
    if not pair:
        mine = [jnp.zeros_like(x) for x in mine]
    grad_ffn_gain = ffn_gain_grads[0] + ffn_gain_grads[1]
    if packed:
        dealt_out = ffn_grads(ring, hidden_two, back_gate, back_up, hidden_ffn, cots)
        first, *dealt_out = lax.optimization_barrier((first, *dealt_out))
        dealt_out, _ = exchanged(ring, dealt_out)
        ffn_box = []
        ffn_sum = Steps(sum_steps(ring, dealt_terms(ring, dealt_out), ffn_box))
        first, last = advance([ffn_sum], first, last)
    else:

        def by_units(xs):
            return jnp.concatenate(xs, axis=1).transpose(1, 0, 2).reshape(rows, units)

        two, cot = jnp.concatenate(hidden_two), jnp.concatenate(cots)
        grad_w_gate, grad_w_up, grad_w_down = sum_over_ctx(
            ring,
            [
                dot(two, by_units(back_gate), (0, 0)).astype(bf16),
                dot(two, by_units(back_up), (0, 0)).astype(bf16),
                dot(by_units(hidden_ffn), cot, (0, 0)).astype(bf16),
            ],
        )
        ffn_sum = None

    back_mixed, back_proj, do_tiles, stats = whole_call(
        functools.partial(back_kernel, pair),
        "back",
        [
            shape(rows, width),
            shape(rows, width, dtype=bf16),
            shape(*q_tiles.shape, dtype=bf16),
            shape(*lse.shape),
        ],
        [cotangent, line(ffn_gain), w_out, o, lse, *mixed, *mine, first, last],
        2 * rows * width * q_cols,
    )
    output_swap, more = None, hidden_ffn
    dq = None
    terms = {}

    dkv_sum = Steps(sum_steps(ring, lambda d: terms[d]))
    for d in range(far, -1, -1):
        if d < far:
            chains = [ffn_sum, dkv_sum if d < far - 1 else None]
            if d == far - 2 and pair:
                output_swap = Steps(exchange_steps(output_part))
            if d in (far - 2, far - 3):
                chains.append(output_swap)
            do_tiles, dq, *more = advance(chains, do_tiles, dq, *more)
            if d == far - 1:
                (output_part,) = whole_call(
                    functools.partial(down_kernel, pair),
                    "down",
                    [shape(rows, width, dtype=bf16)],
                    [*more, w_down],
                    2 * rows * width * units,
                )
                more = [output_part]
        dq, keep, give = attention.backward(kv_pieces[d], q_tiles, do_tiles, stats, dq)
        terms[d] = [keep, ring.sibling(give)]
    placed, done = [], 0
    (dq,) = advance([None if LATE else ffn_sum, dkv_sum], dq)
    query_delta, grad_query_gain = whole_call(
        back_query_kernel,
        "back_query",
        [shape(rows, q_cols, dtype=bf16), shape(1, LANES)],
        [dq, query_raw, line(query_gain), cosine, sines],
        2 * rows * width,
    )
    if packed:
        done = len(ffn_box[0].pieces)
        placed = place_ffn(ring, ffn_box[0].pieces, width, [])
    query_delta, *placed = advance([dkv_sum], query_delta, *placed)
    own_dkv = dkv_sum.result
    wide = width // (2 * ring.n) + w_out.shape[0] // (2 * ring.n)
    one_low, grad_norm_gain, grad_key_gain, kv_delta, *cuts = whole_call(
        functools.partial(back_project_kernel, other_ring),
        "back_project",
        [
            shape(rows, width, dtype=bf16),
            shape(1, width),
            shape(1, LANES),
            shape(rows, 2 * k_cols, dtype=bf16),
        ]
        + (dealt(ring, shape(wide, width, dtype=bf16)) if packed else []),
        [
            tokens,
            hidden_input,
            query_delta,
            own_dkv,
            kv_raw,
            line(key_gain),
            cosine,
            sines,
            w_query,
            w_kv,
            attended,
            back_proj,
        ],
        4 * rows * width * (q_cols + 2 * k_cols),
        [pltpu.VMEM((2 * ring.n, wide, width), bf16)],
    )

    gains = jnp.concatenate(
        [
            grad_norm_gain[0],
            grad_ffn_gain[0],
            grad_query_gain[0, :HEAD_SIZE] + grad_query_gain[0, HEAD_SIZE:],
            grad_key_gain[0, :HEAD_SIZE],
        ]
    )
    exchanges = [("ctx", devices, k) for k in bits(devices)[2:] + bits(devices)[1::-1]]
    exchanges += [("tp", lax.axis_size("tp"), k) for k in bits(lax.axis_size("tp"))]
    gain_sum = Steps(pair_steps(gains, exchanges))
    one_swap = Steps(exchange_steps(one_low)) if pair else None
    if packed:
        qkv_box = []
        cuts, _ = exchanged(other_ring, cuts)
        qkv_sum = Steps(sum_steps(other_ring, dealt_terms(other_ring, cuts), qkv_box))
        gather = ffn_box[0]
        round_at = 0
        while qkv_sum.generator is not None:
            came = len(gather.pieces)
            chains = [qkv_sum]
            if round_at in (1, 4):
                chains.append(one_swap)
            if round_at > 5:
                chains.append(gain_sum)
            placed = advance(chains, *placed)
            if round_at % 2 == 0:
                placed = advance([ffn_sum, gain_sum if round_at < 5 else None], *placed)
            if came > done:
                placed = place_ffn(ring, gather.pieces[done:came], width, placed)
                done = came
            round_at += 1
        if done < len(gather.pieces):
            placed = place_ffn(ring, gather.pieces[done:], width, placed)
        grad_w_gate, grad_w_up, grad_w_down = placed
        grad_w_query, grad_w_key, grad_w_value, grad_w_out = place_qkv(
            other_ring, qkv_box[0].pieces, width, (q_cols, k_cols, k_cols)
        )
    else:
        grad_w_query, grad_kv, grad_w_out = sum_over_ctx(
            ring,
            [
                dot(hidden_input, query_delta, (0, 0)).astype(bf16),
                dot(hidden_input, kv_delta, (0, 0)).astype(bf16),
                dot(attended, back_proj, (0, 0)).astype(bf16),
            ],
        )
        grad_kv = grad_kv.reshape(width, kv_heads, 2, HEAD_SIZE)
        grad_w_key = grad_kv[:, :, 0].reshape(width, k_cols)
        grad_w_value = grad_kv[:, :, 1].reshape(width, k_cols)
    while gain_sum.generator is not None:
        advance([gain_sum])
    gains = gain_sum.result
    if pair:
        for swap in (output_swap, one_swap):
            while swap.generator is not None:
                advance([swap])
        output = output_part.astype(f32) + output_swap.result.astype(f32)
        back_one = one_low.astype(f32) + one_swap.result.astype(f32)
    else:
        output = lax.psum(output_part, "tp").astype(f32)
        back_one = lax.psum(one_low, "tp").astype(f32)
    output = (from_first(mixed) + output).astype(bf16)
    inputs = tokens.astype(f32)
    input_grad = back_mixed + norm_back(back_one, inputs, row_scale(inputs), norm_gain)

    return (
        output,
        input_grad,
        gains[:width],
        grad_w_query,
        grad_w_key,
        grad_w_value,
        gains[2 * width : 2 * width + HEAD_SIZE],
        gains[2 * width + HEAD_SIZE :],
        grad_w_out,
        gains[width : 2 * width],
        grad_w_gate,
        grad_w_up,
        grad_w_down,
    )


def solution(mesh):
    return jax.shard_map(
        on_device,
        mesh=mesh,
        in_specs=(
            P("ctx", None),
            P("ctx", None),
            P(),
            P(),
            P(),
            P(None, "tp"),
            P(None, "tp"),
            P(None, "tp"),
            P(),
            P(),
            P("tp", None),
            P(),
            P(None, "tp"),
            P(None, "tp"),
            P("tp", None),
        ),
        out_specs=(
            P("ctx", None),
            P("ctx", None),
            P(),
            P(None, "tp"),
            P(None, "tp"),
            P(None, "tp"),
            P(),
            P(),
            P("tp", None),
            P(),
            P(None, "tp"),
            P(None, "tp"),
            P("tp", None),
        ),
        check_vma=False,
    )
```

```python
import functools

import jax
import jax.numpy as jnp
import numpy as np
from jax import lax
from jax.experimental import pallas as pl
from jax.experimental.pallas import tpu as pltpu
from jax.sharding import PartitionSpec as P

HEAD_SIZE = 64
LANES = 2 * HEAD_SIZE
EPSILON = 1e-05
ROPE_BASE = 1000000.0
LOG2E = 1.4426950408889634
VMEM_BYTES = 18 * 2**20
COST_SCALE = 4
FFN_COLS = 768
LATE = True
ALL_VMEM = 56 * 2**20
f32, bf16 = jnp.float32, jnp.bfloat16
NT = (((1,), (1,)), ((), ()))


class Ring:
    def __init__(self, n_ctx, sign=1):
        self.sign = sign
        n = self.n = n_ctx // 2
        self.zs = 4 if n % 4 == 0 else n
        self.ys = n // self.zs
        order = [int(self.chip_at(np.int32(place))) for place in range(n)]

        def steps(flip, turned):
            return [
                (order[i] * 2 + c, order[(i + sign * (1 - 2 * (c ^ turned))) % n] * 2 + (c ^ flip))
                for i in range(n)
                for c in (0, 1)
            ]

        self.onward, self.across, self.spread = steps(0, 0), steps(1, 0), steps(1, 1)
        self.to_sibling = [(i, i ^ 1) for i in range(n_ctx)]

    def chip_at(self, place):
        if self.ys == 1:
            return place
        where = np.where if isinstance(place, np.integer) else jnp.where
        turn = place - self.zs
        k, r = turn // (self.ys - 1), turn % (self.ys - 1)
        back = (self.zs - 1 - k) * self.ys + where(k % 2 == 0, 1 + r, self.ys - 1 - r)
        return where(place < self.zs, place * self.ys, back)

    def here(self):
        index = lax.axis_index("ctx")
        chip, core = index // 2, index % 2
        if self.ys == 1:
            return chip, core
        z, y = chip // self.ys, chip % self.ys
        k = self.zs - 1 - z
        back = self.zs + k * (self.ys - 1) + jnp.where(k % 2 == 0, y - 1, self.ys - 1 - y)
        return jnp.where(y == 0, z, back), core

    def at(self, slot):
        place, core = self.here()
        distance, other = slot
        ahead = self.sign * (1 - 2 * core) * distance
        return (place + ahead + self.n) % self.n, (core + other) % 2

    def device_at(self, slot):
        place, core = self.at(slot)
        return self.chip_at(place) * 2 + core

    def hop(self, x):
        return lax.ppermute(x, "ctx", self.onward)

    def sibling(self, x):
        return lax.ppermute(x, "ctx", self.to_sibling)


def total(*terms):
    out = terms[0].astype(f32)
    for term in terms[1:]:
        out = out + term.astype(f32)
    return out.astype(bf16)


class RingGather:
    def __init__(self, ring, own):
        self.ring, self.far = ring, ring.n // 2
        self.pieces = [([(0, 0)], own), ([(0, 1)], ring.sibling(own))]
        self.step = 0

    def sends(self):
        last = self.pieces[-2][1]
        if self.step == 0:
            return [self.pieces[0][1]]
        return [last[0]] if self.step + 1 == self.far else [last]

    def send(self, arrays):
        (x,) = arrays
        self.step += 1
        new = [self.ring.hop(x)]
        if self.step == 1:
            new.append(lax.ppermute(x, "ctx", self.ring.spread))
        return new

    def arrive(self, arrays):
        d = self.step
        if d == 1:
            new = [([(-1, c)], x) for c, x in enumerate(arrays)]
            pair = jnp.stack(arrays)
            self.pieces += [([(-1, 0), (-1, 1)], pair), ([(1, 1), (1, 0)], self.ring.sibling(pair))]
            return new
        (x,) = arrays
        if d == self.far:
            new = [([(d, 0)], x), ([(d, 1)], self.ring.sibling(x))]
        else:
            new = [([(-d, 0), (-d, 1)], x), ([(d, 1), (d, 0)], self.ring.sibling(x))]
        self.pieces += new
        return new[:1]

    def done(self):
        return self.step == self.far


def sum_steps(ring, terms, box=None):
    _, core = ring.here()
    far = ring.n // 2
    (x,) = yield [total(*terms(far))]
    (got,) = yield [ring.hop(x)]
    for d in range(far - 1, 1, -1):
        here = terms(d)
        if d == far - 1:
            x = jnp.stack([total(*[y[0] for y in here], got), total(*[y[1] for y in here])])
        else:
            x = total(*here, got)
        (x,) = yield [x]
        (got,) = yield [ring.hop(x)]
    here = terms(1)
    x = yield [total(*[y[c] for y in here], got[c]) for c in (0, 1)]
    got = yield [ring.hop(x[0]), lax.ppermute(x[1], "ctx", ring.across)]
    own = total(*terms(0), *got)
    if box is None:
        return own
    gather = RingGather(ring, own)
    box.append(gather)
    while not gather.done():
        late = [x for _, x in gather.pieces[-1:]]
        new = gather.send((yield gather.sends()))
        came = yield new + late
        gather.arrive(came[: len(new)])
    return gather


class Steps:
    def __init__(self, generator):
        self.generator, self.result = generator, None
        self.sent = self.came = None

    def arrivals(self):
        return self.generator.send(self.sent) if self.sent is not None else []

    def sends(self):
        try:
            return self.generator.send(self.came or None)
        except StopIteration as stop:
            self.result, self.generator = stop.value, None
            return []


def tied(lists, others):
    flat = lax.optimization_barrier((*[x for xs in lists for x in xs], *others))
    out = []
    for xs in lists:
        out.append(list(flat[: len(xs)]))
        flat = flat[len(xs) :]
    return out, flat


def advance(steps, *others):
    steps = [x for x in steps if x is not None and x.generator is not None]
    came, others = tied([x.arrivals() for x in steps], others)
    for x, arrays in zip(steps, came):
        x.came = arrays
    sends, others = tied([x.sends() for x in steps], others)
    for x, arrays in zip(steps, sends):
        x.sent = arrays
    return others


def sum_over_ctx(ring, arrays):
    n = ring.n
    far = n // 2
    outs = []
    for x in arrays:
        unit = x.shape[0] // (2 * n)
        cut = x.reshape(2, n, unit, x.shape[1])

        def piece(distance, other):
            place, core = ring.at((distance, other))
            return cut[core, place]

        def terms(d):
            if d in (0, far):
                return [piece(d, 0), ring.sibling(piece(d, 1))]
            keep = jnp.stack([piece(d, 0), piece(d, 1)])
            return [keep, ring.sibling(jnp.stack([piece(-d, 1), piece(-d, 0)]))]

        box = []
        steps = Steps(sum_steps(ring, terms, box))
        while steps.generator is not None:
            advance([steps])
        out = jnp.zeros(x.shape, f32)
        for slots, part in box[0].pieces:
            for i, slot in enumerate(slots):
                place, core = ring.at(slot)
                one = part if len(slots) == 1 else part[i]
                out = lax.dynamic_update_slice_in_dim(
                    out, one.astype(f32), (core * n + place) * unit, 0
                )
        outs.append(out)
    return outs


def exchange_steps(x):
    (x,) = yield [x]
    (theirs,) = yield [lax.ppermute(x, "tp", [(0, 1), (1, 0)])]
    return theirs


def pair_steps(x, exchanges):
    for axis, size, step in exchanges:
        (mine,) = yield [x]
        (theirs,) = yield [lax.ppermute(mine, axis, [(i, i ^ step) for i in range(size)])]
        x = mine + theirs
    return x


def bits(size):
    return [1 << k for k in range(size.bit_length() - 1)]


def from_other(xs):
    return [lax.ppermute(x, "tp", [(0, 1), (1, 0)]) for x in xs]


def sum_over_tp(x):
    size = lax.axis_size("tp")
    if size == 2:
        return x.astype(f32) + lax.ppermute(x, "tp", [(0, 1), (1, 0)]).astype(f32)
    return lax.psum(x, "tp").astype(f32)


def pair_count(slots, seq_count):
    return seq_count * (2 * len(slots) + ((0, 0) in slots))


class Tiles:
    def __init__(self, ring, slots, seq_count, blk, order_ref, starts_ref):
        self.ring, self.slots = ring, slots
        self.seq_count, self.blk = seq_count, blk
        self.order, self.starts = order_ref, starts_ref
        self.last = 4 * ring.n - 1
        self.rows = pair_count(slots, seq_count)

    def start_of(self, seq, place):
        start = jnp.int32(0)
        for d in range(3):
            at = self.starts[seq, d]
            start = jnp.where(place >= at, at, start)
        return start

    def pair(self, row):
        seq, row = row % self.seq_count, row // self.seq_count
        slot, which = row // 2, row % 2
        own = self.slots.index((0, 0)) if (0, 0) in self.slots else None
        if own is not None:
            both_high = slot == len(self.slots)
            slot = jnp.where(both_high, own, slot)
        distance, other = self.slots[0]
        for i, (d, c) in enumerate(self.slots):
            distance, other = jnp.where(slot == i, d, distance), jnp.where(slot == i, c, other)
        mine = self.order[lax.axis_index("ctx")]
        theirs = self.order[self.ring.device_at((distance, other))]
        low = (which == 1) & (theirs <= mine)
        high = (which == 1) & (theirs > mine)
        if own is not None:
            low, high = low & jnp.logical_not(both_high), high | both_high
        q_place = jnp.where(low, mine, self.last - mine) * self.blk
        k_place = jnp.where(high, self.last - theirs, theirs) * self.blk
        q_tile = 2 * seq + jnp.where(low, 0, 1)
        k_tile = 2 * (self.seq_count * slot + seq) + jnp.where(high, 1, 0)
        k_end, q_end = k_place + self.blk - 1, q_place + self.blk - 1
        whole = (k_end <= q_place) & (k_place >= self.start_of(seq, q_end))
        empty = k_end < self.start_of(seq, q_place)
        kind = jnp.where(whole, 0, jnp.where(empty, 2, 1))
        return q_tile, k_tile, kind, (seq, q_place, k_place)

    def allowed(self, at, query_axis, shape):
        seq, q_place, k_place = at
        query = q_place + lax.broadcasted_iota(jnp.int32, shape, query_axis) % self.blk
        key = k_place + lax.broadcasted_iota(jnp.int32, shape, 1 - query_axis)
        return (key <= query) & (key >= self.start_of(seq, query))

    def run(self, tile):
        def body(row, carry):
            q_tile, k_tile, kind, at = self.pair(row)
            keys = pl.ds(pl.multiple_of(k_tile * self.blk, self.blk), self.blk)
            pl.when(kind == 0)(lambda: tile(q_tile, keys, None))
            pl.when(kind == 1)(lambda: tile(q_tile, keys, functools.partial(self.allowed, at)))
            return carry

        lax.fori_loop(0, self.rows, body, 0)


def load_chunks(chunks, kv_ref):
    at = 0
    for chunk in chunks:
        for part in [chunk] if len(chunk.shape) == 2 else [chunk.at[0], chunk.at[1]]:
            kv_ref[at : at + part.shape[0]] = part[...]
            at += part.shape[0]


def forward_kernel(make, parts, heads, order_ref, starts_ref, q_ref, *refs):
    chunks, held, (out_ref, kv_ref) = refs[:parts], refs[parts:-2], refs[-2:]
    tiles = make(order_ref, starts_ref)
    blk = tiles.blk
    first = lax.broadcasted_iota(jnp.int32, (blk, LANES), 1) < HEAD_SIZE
    load_chunks(chunks, kv_ref)
    out_ref[...] = held[0][...] if held else jnp.zeros_like(out_ref)

    def tile(q_tile, keys, mask):
        if mask is not None:
            allowed = mask(0, (q_ref.shape[2], blk))
        for h in range(heads):
            kv = kv_ref[keys, h * LANES : (h + 1) * LANES]
            scores = lax.dot_general(q_ref[h, q_tile], kv, NT, preferred_element_type=f32)
            weights = jnp.exp2(scores * LOG2E)
            if mask is not None:
                weights = jnp.where(allowed, weights, 0.0)
            one_v = jnp.where(first, jnp.ones_like(kv), kv)
            out_ref[h, q_tile] += jnp.dot(weights.astype(bf16), one_v, preferred_element_type=f32)

    tiles.run(tile)


def backward_kernel(make, parts, held, heads, order_ref, starts_ref, q_ref, do_ref, stat_ref, *refs):
    chunks, held, refs = refs[:parts], refs[parts : parts + held], refs[parts + held :]
    dq_ref, keep_ref, give_ref, kv_ref, dkv_ref = refs
    tiles = make(order_ref, starts_ref)
    blk = tiles.blk
    load_chunks(chunks, kv_ref)
    dq_ref[...] = held[0][...] if held else jnp.zeros_like(dq_ref)
    dkv_ref[...] = jnp.zeros_like(dkv_ref)

    def tile(q_tile, keys, mask):
        if mask is not None:
            allowed = mask(1, (blk, q_ref.shape[2]))
        for h in range(heads):
            cols = slice(h * LANES, (h + 1) * LANES)
            kv = kv_ref[keys, cols]
            q = q_ref[h, q_tile]
            do = do_ref[h, q_tile]
            scores = lax.dot_general(kv, q, NT, preferred_element_type=f32)
            back_probs = lax.dot_general(kv, do, NT, preferred_element_type=f32)
            probs = jnp.exp2(scores * LOG2E - stat_ref[h, q_tile, 0:1])
            if mask is not None:
                probs = jnp.where(allowed, probs, 0.0)
            back_scores = (probs * (back_probs - stat_ref[h, q_tile, 1:2])).astype(bf16)
            both = jnp.concatenate([probs.astype(bf16), back_scores], axis=1)
            dkv_ref[keys, cols] += jnp.dot(
                both, jnp.concatenate([do, q], axis=0), preferred_element_type=f32
            )
            dq_ref[h, q_tile] += jnp.dot(kv.T[:HEAD_SIZE], back_scores, preferred_element_type=f32)

    tiles.run(tile)
    rows = keep_ref.shape[-2]
    if len(keep_ref.shape) == 2:
        keep_ref[...] = dkv_ref[:rows]
        give_ref[...] = dkv_ref[rows:].astype(bf16)
        return
    for c in (0, 1):
        keep_ref[c] = dkv_ref[(3 - c) * rows : (4 - c) * rows]
        give_ref[c] = dkv_ref[(1 - c) * rows : (2 - c) * rows].astype(bf16)


def in_smem():
    return pl.BlockSpec(memory_space=pltpu.SMEM)


def in_vmem():
    return pl.BlockSpec(memory_space=pltpu.VMEM)


class Attention:
    def __init__(self, ring, block_order, starts, blk):
        self.ring, self.order, self.starts = ring, block_order, starts
        self.blk, self.seq_count = blk, starts.shape[0]

    def _make(self, slots):
        return lambda order_ref, starts_ref: Tiles(
            self.ring, slots, self.seq_count, self.blk, order_ref, starts_ref
        )

    def _cost(self, slots, heads, products, arrays):
        tile = 2 * self.blk * self.blk * heads * pair_count(slots, self.seq_count)
        return pl.CostEstimate(
            flops=2 * tile * 256 * products // COST_SCALE,
            bytes_accessed=sum(x.size * x.dtype.itemsize for x in arrays) // COST_SCALE,
            transcendentals=tile // COST_SCALE,
        )

    def forward(self, pieces, q, acc):
        heads, tiles, rows, _ = q.shape
        out = jax.ShapeDtypeStruct((heads, tiles, rows, LANES), f32)
        held = [] if acc is None else [acc]
        slots, chunks = [x for xs, _ in pieces for x in xs], [x for _, x in pieces]
        keys, width = len(slots) * chunks[0].shape[-2], chunks[0].shape[-1]
        return pl.pallas_call(
            functools.partial(forward_kernel, self._make(slots), len(chunks), heads),
            out_shape=out,
            in_specs=[in_smem()] * 2 + [in_vmem()] * (1 + len(chunks) + len(held)),
            out_specs=in_vmem(),
            scratch_shapes=[pltpu.VMEM((keys, width), bf16)],
            compiler_params=pltpu.CompilerParams(vmem_limit_bytes=VMEM_BYTES),
            cost_estimate=self._cost(slots, heads, 2, [q, *chunks, out, out]),
            name="attend_forward",
        )(self.order, self.starts, q, *chunks, *held)

    def backward(self, pieces, q, do, stats, acc):
        heads, tiles, rows, _ = q.shape
        slots, chunks = [x for xs, _ in pieces for x in xs], [x for _, x in pieces]
        keys, width = len(slots) * chunks[0].shape[-2], chunks[0].shape[-1]
        outs = [
            jax.ShapeDtypeStruct((heads, tiles, HEAD_SIZE, rows), f32),
            jax.ShapeDtypeStruct(chunks[0].shape, f32),
            jax.ShapeDtypeStruct(chunks[0].shape, bf16),
        ]
        held = [] if acc is None else [acc]
        return pl.pallas_call(
            functools.partial(
                backward_kernel, self._make(slots), len(chunks), len(held), heads
            ),
            out_shape=outs,
            in_specs=[in_smem()] * 2 + [in_vmem()] * (3 + len(chunks) + len(held)),
            out_specs=[in_vmem()] * len(outs),
            scratch_shapes=[pltpu.VMEM((keys, width), bf16), pltpu.VMEM((keys, width), f32)],
            compiler_params=pltpu.CompilerParams(vmem_limit_bytes=VMEM_BYTES),
            cost_estimate=self._cost(slots, heads, 5, [q, do, outs[0], *chunks, *outs]),
            name="attend_backward",
        )(self.order, self.starts, q, do, stats, *chunks, *held)


def grads_kernel(ring, *refs):
    two, gate, up, ffn, cot = (refs[2 * i : 2 * i + 2] for i in range(5))
    outs, (lhs_ref, cot_ref, all_ref) = refs[10:-3], refs[-3:]

    @pl.when(pl.program_id(0) == 0)
    def _():
        lhs_ref[...] = jnp.concatenate([x[...] for x in two], axis=0).T
        cot_ref[...] = jnp.concatenate([x[...] for x in cot], axis=0)

    n = ring.n
    unit = lhs_ref.shape[0] // (2 * n)
    cols = gate[0].shape[2]
    thin = cols // (2 * n)
    for i, half in enumerate((gate, up)):
        right = jnp.concatenate([x[0] for x in half], axis=0)
        grad = jnp.dot(lhs_ref[...], right, preferred_element_type=f32).astype(bf16)
        all_ref[:, i * unit : (i + 1) * unit] = grad.reshape(2 * n, unit, cols)
    left = jnp.concatenate([x[0] for x in ffn], axis=0).T
    down = jnp.dot(left, cot_ref[...], preferred_element_type=f32).astype(bf16)
    down = down.reshape(2 * n, thin, down.shape[1])
    for k in range(down.shape[2] // cols):
        at = 2 * unit + k * thin
        all_ref[:, at : at + thin] = down[:, :, k * cols : (k + 1) * cols]
    deal(ring, lambda at: all_ref[at], lambda ref, x: ref.at[0].__setitem__(..., x), outs)


def deal(ring, read, write, outs):
    far = ring.n // 2

    def part(distance, other):
        place, core = ring.at((distance, other))
        return read(core * ring.n + place)

    keep_far, give_far, *keep, give = outs
    write(keep_far, part(far, 0))
    write(give_far, part(far, 1))
    write(keep[0], part(0, 0))
    write(give.at[0], part(0, 1))
    for d in range(1, far):
        for c in (0, 1):
            write(keep[d].at[c], part(d, c))
            write(give.at[2 * d - 1 + c], part(-d, 1 - c))


def dealt(ring, cut):
    far = ring.n // 2
    heads = [(), (), ()] + [(2,)] * (far - 1) + [(2 * far - 1,)]
    return [jax.ShapeDtypeStruct((*head, *cut.shape), cut.dtype) for head in heads]


def exchanged(ring, outs, *others):
    keep_far, give_far, *keep, give = outs
    give, got_far, *others = lax.optimization_barrier((give, ring.sibling(give_far), *others))
    return [keep_far, got_far, *keep, ring.sibling(give)], others


def dealt_terms(ring, outs):
    far = ring.n // 2
    keep_far, got_far, *keep, got = outs

    def terms(d):
        if d == far:
            return [keep_far, got_far]
        if d == 0:
            return [keep[0], got[0]]
        return [keep[d], got[2 * d - 1 : 2 * d + 1]]

    return terms


def ffn_grads(ring, hidden_two, back_gate, back_up, hidden_ffn, cotangent):
    rows, width = hidden_two[0].shape
    blocks, _, cols = back_gate[0].shape
    units = blocks * cols
    n = ring.n
    wide = width // (2 * n) * 3
    whole = [pl.BlockSpec((rows, width), lambda j: (0, 0))] * 2
    block = [pl.BlockSpec((1, rows, cols), lambda j: (j, 0, 0))] * 2
    outs = dealt(ring, shape(units // cols, wide, cols, dtype=bf16))
    cuts = [
        pl.BlockSpec(
            (*x.shape[:-3], 1, wide, cols), lambda j, k=len(x.shape): (0,) * (k - 3) + (j, 0, 0)
        )
        for x in outs
    ]
    return pl.pallas_call(
        functools.partial(grads_kernel, ring),
        grid=(units // cols,),
        out_shape=outs,
        in_specs=whole + block * 3 + whole,
        out_specs=cuts,
        scratch_shapes=[
            pltpu.VMEM((width, 2 * rows), bf16),
            pltpu.VMEM((2 * rows, width), bf16),
            pltpu.VMEM((2 * n, wide, cols), bf16),
        ],
        compiler_params=pltpu.CompilerParams(vmem_limit_bytes=VMEM_BYTES),
        cost_estimate=pl.CostEstimate(
            flops=12 * rows * width * units // COST_SCALE, bytes_accessed=2**20, transcendentals=0
        ),
        name="ffn_grads",
    )(*hidden_two, *back_gate, *back_up, *hidden_ffn, *cotangent)


def place_kernel(ring, slots, count, *refs):
    arrays, outs, (wide_ref, down_ref, sem) = refs[:count], refs[-6:-3], refs[-3:]
    parts = [y for x in arrays for y in ([x] if len(x.shape) == 3 else [x.at[0], x.at[1]])]
    n = ring.n
    blocks, _, cols = parts[0].shape
    unit = outs[0].shape[0] // (2 * n)
    thin = cols // (2 * n)
    copies = []
    for i, slot in enumerate(slots):
        part = parts[i]
        place, core = ring.at(slot)
        r = core * n + place
        for w in range(2):
            for j in range(blocks):
                wide_ref[i, w, :, j * cols : (j + 1) * cols] = part[
                    j, w * unit : (w + 1) * unit
                ].astype(f32)
            rows = pl.ds(pl.multiple_of(r * unit, unit), unit)
            copies.append((wide_ref.at[i, w], outs[w].at[rows]))
        for j in range(blocks):
            for k in range(outs[2].shape[1] // cols):
                at = 2 * unit + k * thin
                down_ref[i, j, :, k * cols : (k + 1) * cols] = part[j, at : at + thin].astype(f32)
            rows = pl.ds(pl.multiple_of(j * cols + r * thin, thin), thin)
            copies.append((down_ref.at[i, j], outs[2].at[rows]))
        for k in range(i * (2 + blocks), (i + 1) * (2 + blocks)):
            pltpu.make_async_copy(*copies[k], sem.at[k]).start()
    for k, pair in enumerate(copies):
        pltpu.make_async_copy(*pair, sem.at[k]).wait()


def place_ffn(ring, pieces, width, held):
    slots, parts = [x for xs, _ in pieces for x in xs], [x for _, x in pieces]
    blocks, wide, cols = parts[0].shape[-3:]
    units = blocks * cols
    count = len(slots)
    thin = cols // (2 * ring.n)
    anywhere = pl.BlockSpec(memory_space=pl.ANY)
    return pl.pallas_call(
        functools.partial(place_kernel, ring, slots, len(parts)),
        out_shape=[shape(width, units), shape(width, units), shape(units, width)],
        in_specs=[in_vmem()] * len(parts) + [anywhere] * len(held),
        out_specs=[anywhere] * 3,
        input_output_aliases={len(parts) + i: i for i in range(len(held))},
        scratch_shapes=[
            pltpu.VMEM((count, 2, width // (2 * ring.n), units), f32),
            pltpu.VMEM((count, blocks, thin, width), f32),
            pltpu.SemaphoreType.DMA((count * (2 + blocks),)),
        ],
        compiler_params=pltpu.CompilerParams(vmem_limit_bytes=VMEM_BYTES),
        cost_estimate=pl.CostEstimate(
            flops=0, bytes_accessed=8 * count * wide * units, transcendentals=0
        ),
        name="place_ffn",
    )(*parts, *held)


def place_qkv_kernel(ring, slots, *refs):
    arrays, (query_ref, key_ref, value_ref, out_ref) = refs[:-4], refs[-4:]
    parts = [y for x in arrays for y in ([x] if len(x.shape) == 2 else [x.at[0], x.at[1]])]
    n = ring.n
    unit, thin = query_ref.shape[0] // (2 * n), out_ref.shape[0] // (2 * n)
    for slot, part in zip(slots, parts):
        place, core = ring.at(slot)
        r = core * n + place
        rows = pl.ds(pl.multiple_of(r * unit, unit), unit)
        at = query_ref.shape[1]
        query_ref[rows] = part[:unit, :at].astype(f32)
        for h in range(key_ref.shape[1] // HEAD_SIZE):
            cols = slice(h * HEAD_SIZE, (h + 1) * HEAD_SIZE)
            both = part[:unit, at + h * LANES : at + (h + 1) * LANES].astype(f32)
            key_ref[rows, cols] = both[:, :HEAD_SIZE]
            value_ref[rows, cols] = both[:, HEAD_SIZE:]
        rows = pl.ds(pl.multiple_of(r * thin, thin), thin)
        out_ref[rows] = part[unit:].astype(f32)


def place_qkv(ring, pieces, width, cols):
    slots, parts = [x for xs, _ in pieces for x in xs], [x for _, x in pieces]
    thin = parts[0].shape[-2] - width // (2 * ring.n)
    return whole_call(
        functools.partial(place_qkv_kernel, ring, slots),
        "place_qkv",
        [shape(width, c) for c in cols] + [shape(thin * 2 * ring.n, width)],
        parts,
        0,
    )


def whole_call(kernel, name, outs, args, flops, scratch=(), scalars=(0, 0), vmem=VMEM_BYTES):
    moved = sum(x.size * x.dtype.itemsize for x in (*outs, *args))
    return pl.pallas_call(
        kernel,
        out_shape=list(outs),
        in_specs=[in_smem()] * scalars[0] + [in_vmem()] * (len(args) - scalars[0]),
        out_specs=[in_smem()] * scalars[1] + [in_vmem()] * (len(outs) - scalars[1]),
        scratch_shapes=list(scratch),
        compiler_params=pltpu.CompilerParams(vmem_limit_bytes=vmem),
        cost_estimate=pl.CostEstimate(
            flops=flops // COST_SCALE, bytes_accessed=moved // COST_SCALE, transcendentals=0
        ),
        name=name,
    )(*args)


def shape(*dims, dtype=f32):
    return jax.ShapeDtypeStruct(dims, dtype)


def first_lanes(rows):
    return lax.broadcasted_iota(jnp.int32, (rows, LANES), 1) < HEAD_SIZE


def head_mean(x):
    i = lax.broadcasted_iota(jnp.int32, (LANES, LANES), 0) // HEAD_SIZE
    j = lax.broadcasted_iota(jnp.int32, (LANES, LANES), 1) // HEAD_SIZE
    mean = jnp.where(i == j, 1.0 / HEAD_SIZE, 0.0).astype(bf16)
    high = x.astype(bf16)
    low = (x - high.astype(f32)).astype(bf16)
    return jnp.dot(high, mean, preferred_element_type=f32) + jnp.dot(
        low, mean, preferred_element_type=f32
    )


def turn(x, cosine, sines):
    lane = lax.broadcasted_iota(jnp.int32, x.shape, 1) % HEAD_SIZE
    half = HEAD_SIZE // 2
    other = jnp.where(
        lane < half, pltpu.roll(x, LANES - half, axis=1), pltpu.roll(x, half, axis=1)
    )
    return x * cosine + other * sines


def row_scale(x):
    return lax.rsqrt(jnp.mean(x * x, axis=-1, keepdims=True) + EPSILON)


def norm_back(upstream, x, scale, gain):
    inner = upstream * gain
    return scale * (inner - x * (scale * scale * jnp.mean(inner * x, axis=-1, keepdims=True)))


def head_norm_back(upstream, x, gain):
    scale = lax.rsqrt(head_mean(x * x) + EPSILON)
    inner = upstream * gain
    back = scale * (inner - x * (scale * scale * head_mean(inner * x)))
    return back, jnp.sum(upstream * x * scale, axis=0, keepdims=True)


def gain_of(ref):
    return ref[...].astype(f32)


def head_gain(ref):
    return jnp.concatenate([gain_of(ref)] * 2, axis=1)


def lanes(tile):
    return slice(tile * LANES, (tile + 1) * LANES)


def project_kv_kernel(
    tiles, last, order, segments, tokens, gain, w_key, w_value, key_gain, inverse, *refs
):
    starts, hidden, kv_raw, kv, w_kv, cosine, sines = refs
    x = tokens[...].astype(f32)
    hidden[...] = (x * row_scale(x) * gain_of(gain)).astype(bf16)
    rows = x.shape[0]
    blk = rows // tiles
    mine = order[lax.axis_index("ctx")]
    lane = lax.broadcasted_iota(jnp.int32, (blk, LANES), 1) % HEAD_SIZE
    for t in range(tiles):
        block = last - mine if t % 2 else mine
        place = block * blk + lax.broadcasted_iota(jnp.int32, (blk, LANES), 0)
        angles = place.astype(f32) * inverse[...]
        at = slice(t * blk, (t + 1) * blk)
        cosine[at] = jnp.cos(angles)
        sine = jnp.sin(angles)
        sines[at] = jnp.where(lane < HEAD_SIZE // 2, -sine, sine)
    first = first_lanes(rows)
    for h in range(kv.shape[1] // LANES):
        cols = slice(h * HEAD_SIZE, (h + 1) * HEAD_SIZE)
        w_kv[:, lanes(h)] = jnp.concatenate([w_key[:, cols], w_value[:, cols]], axis=1)
        raw = jnp.dot(hidden[...], w_kv[:, lanes(h)], preferred_element_type=f32)
        kv_raw[:, lanes(h)] = raw
        normed = raw * lax.rsqrt(head_mean(raw * raw) + EPSILON) * head_gain(key_gain)
        kv[:, lanes(h)] = jnp.where(first, turn(normed, cosine[...], sines[...]), raw).astype(bf16)
    for seq in range(segments.shape[0]):
        for d in range(3):
            before = jnp.where(segments[seq : seq + 1] <= d, 1.0, 0.0)
            starts[seq, d] = jnp.sum(before).astype(jnp.int32)


def project_q_kernel(tiles, hidden, w_query, query_gain, cosine, sines, query_raw, q_tiles):
    rows = hidden.shape[0]
    blk = rows // tiles
    first = first_lanes(rows)
    for h in range(q_tiles.shape[0]):
        raw = jnp.dot(hidden[...], w_query[:, lanes(h)], preferred_element_type=f32)
        query_raw[:, lanes(h)] = raw
        normed = raw * lax.rsqrt(head_mean(raw * raw) + EPSILON) * head_gain(query_gain)
        turned = turn(normed, cosine[...], sines[...]).astype(bf16).astype(f32) * 0.125
        pair = [
            jnp.where(first, turned, 0.0),
            jnp.where(first, pltpu.roll(turned, HEAD_SIZE, axis=1), 0.0),
        ]
        for g, one in enumerate(pair):
            for t in range(tiles):
                q_tiles[h, t, g * blk : (g + 1) * blk] = one[t * blk : (t + 1) * blk].astype(bf16)


def half_rows(pair, rows, which):
    first = (lax.axis_index("tp") + which) % 2 if pair else which
    return pl.ds(pl.multiple_of(first * (rows // 2), rows // 2), rows // 2)


def mix_kernel(pair, acc, w_out, attended, o, lse, *halves):
    heads, tiles, rows, _ = acc.shape
    blk = rows // 2
    first = first_lanes(rows)
    for h in range(heads):
        for t in range(tiles):
            x = acc[h, t]
            value = jnp.where(first, 0.0, x * pltpu.roll(1.0 / x, HEAD_SIZE, axis=1))
            o[h, t] = value
            lse[h, t] = jnp.log2(x.T[:8])
            low = pltpu.roll(value[:blk], HEAD_SIZE, axis=1) + value[blk:]
            attended[t * blk : (t + 1) * blk, lanes(h)] = low.astype(bf16)
    for which, half in enumerate(halves):
        rows = half_rows(pair, attended.shape[0], which)
        half[...] = jnp.dot(attended[rows], w_out[...], preferred_element_type=f32).astype(bf16)


def ffn_kernel(tokens, attn, gain, hidden_back, w_gate, w_up, *refs):
    mixed, hidden_two, hidden_ffn, back_gate, back_up, gain_grad, low, sums = refs
    step, last = pl.program_id(0), pl.num_programs(0) - 1

    @pl.when(step == 0)
    def _():
        x = tokens[...].astype(f32) + attn[...].astype(f32)
        mixed[...] = x
        hidden_two[...] = (x * row_scale(x) * gain_of(gain)).astype(bf16)
        sums[...] = jnp.zeros_like(sums)

    gating = jnp.dot(hidden_two[...], w_gate[...], preferred_element_type=f32)
    lifted = jnp.dot(hidden_two[...], w_up[...], preferred_element_type=f32)
    upstream = hidden_back[...]
    logistic = jax.nn.sigmoid(gating)
    silu = gating * logistic
    gate = (upstream * lifted * logistic * (1.0 + gating * (1.0 - logistic))).astype(bf16)
    up = (upstream * silu).astype(bf16)
    ffn = (silu * lifted).astype(bf16)
    for ref, value in ((hidden_ffn, ffn), (back_gate, gate), (back_up, up)):
        cols = ref.shape[2]
        for k in range(ref.shape[0]):
            ref[k] = value[:, k * cols : (k + 1) * cols]
    sums[...] += lax.dot_general(gate, w_gate[...], NT, preferred_element_type=f32)
    sums[...] += lax.dot_general(up, w_up[...], NT, preferred_element_type=f32)

    @pl.when(step == last)
    def _():
        x = mixed[...]
        gain_grad[...] = jnp.sum(sums[...] * x * row_scale(x), axis=0, keepdims=True)
        low[...] = sums[...].astype(bf16)


def block_cols(units):
    return 256 if units % 256 == 0 else units


def feed_forward(tokens, attn, gain, hidden_back, w_gate, w_up):
    rows, width = tokens.shape
    units = w_gate.shape[1]
    cols = FFN_COLS if units % FFN_COLS == 0 else units
    thin = block_cols(units)
    whole = pl.BlockSpec((rows, width), lambda j: (0, 0))
    line = pl.BlockSpec((1, width), lambda j: (0, 0))
    weight = pl.BlockSpec((width, cols), lambda j: (0, j))
    block = pl.BlockSpec((cols // thin, rows, thin), lambda j: (j, 0, 0))
    low = shape(units // thin, rows, thin, dtype=bf16)
    return pl.pallas_call(
        ffn_kernel,
        grid=(units // cols,),
        out_shape=[shape(rows, width), shape(rows, width, dtype=bf16), low, low, low]
        + [shape(1, width), shape(rows, width, dtype=bf16)],
        in_specs=[whole, whole, line, pl.BlockSpec((rows, cols), lambda j: (0, j)), weight, weight],
        out_specs=[whole, whole, block, block, block, line, whole],
        scratch_shapes=[pltpu.VMEM((rows, width), f32)],
        compiler_params=pltpu.CompilerParams(vmem_limit_bytes=VMEM_BYTES),
        cost_estimate=pl.CostEstimate(
            flops=8 * rows * width * units // COST_SCALE, bytes_accessed=2**20, transcendentals=0
        ),
        name="feed_forward",
    )(tokens, attn, gain, hidden_back, w_gate, w_up)


def down_kernel(pair, *refs):
    ffn, w_down, out = refs[:2], refs[2], refs[3]
    cols = ffn[0].shape[2]
    for which, x in enumerate(ffn):
        part = jnp.zeros((x.shape[1], out.shape[1]), f32)
        for k in range(x.shape[0]):
            part += jnp.dot(
                x[k], w_down[k * cols : (k + 1) * cols], preferred_element_type=f32
            )
        out[half_rows(pair, out.shape[0], which)] = part.astype(bf16)


def back_kernel(pair, cotangent, gain, w_out, o, lse, *refs):
    mixed, mine, theirs, (back_mixed, back_proj, do_tiles, stats) = (
        refs[:2],
        refs[2:4],
        refs[4:6],
        refs[6:],
    )
    for which in (0, 1):
        rows = half_rows(pair, cotangent.shape[0], which)
        x = mixed[which][...]
        upstream = mine[which][...].astype(f32) + theirs[which][...].astype(f32)
        back = cotangent[rows].astype(f32) + norm_back(upstream, x, row_scale(x), gain_of(gain))
        back_mixed[rows] = back
        back_proj[rows] = back.astype(bf16)
    heads, tiles, rows, _ = o.shape
    blk = rows // 2
    first = first_lanes(blk)
    row = lax.broadcasted_iota(jnp.int32, (8, rows), 0)
    for h in range(heads):
        attn = lax.dot_general(back_proj[...], w_out[lanes(h)], NT, preferred_element_type=f32)
        for t in range(tiles):
            here = attn[t * blk : (t + 1) * blk]
            do = jnp.concatenate(
                [
                    jnp.where(first, 0.0, pltpu.roll(here, HEAD_SIZE, axis=1)),
                    jnp.where(first, 0.0, here),
                ],
                axis=0,
            ).astype(bf16)
            do_tiles[h, t] = do
            delta = jnp.sum((do.astype(f32) * o[h, t]).T, axis=0, keepdims=True)
            stats[h, t] = jnp.where(row == 0, lse[h, t], delta)


def back_query_kernel(dq, query_raw, query_gain, cosine, sines, query_delta, gain_grad):
    heads, tiles, _, rows = dq.shape
    blk = rows // 2
    gain_grad[...] = jnp.zeros_like(gain_grad)
    for t in range(tiles):
        at = slice(t * blk, (t + 1) * blk)
        for h in range(heads):
            both = jnp.concatenate([dq[h, t, :, :blk], dq[h, t, :, blk:]], axis=0) * 0.125
            turned = turn(both.T, cosine[at], -sines[at])
            back, gain_terms = head_norm_back(turned, query_raw[at, lanes(h)], head_gain(query_gain))
            query_delta[at, lanes(h)] = back.astype(bf16)
            gain_grad[...] += gain_terms


def back_project_kernel(
    ring,
    tokens,
    hidden,
    query_delta,
    own_dkv,
    kv_raw,
    key_gain,
    cosine,
    sines,
    w_query,
    w_kv,
    attended,
    back_proj,
    *refs,
):
    low, norm_grad, gain_grad, kv_delta = refs[:4]
    outs, all_ref = refs[4:-1], refs[-1]
    rows, width = tokens.shape
    first = first_lanes(rows)
    gain_grad[...] = jnp.zeros_like(gain_grad)
    for h in range(own_dkv.shape[1] // LANES):
        dkv = own_dkv[:, lanes(h)].astype(f32)
        turned = turn(dkv, cosine[...], -sines[...])
        back, gain_terms = head_norm_back(turned, kv_raw[:, lanes(h)], head_gain(key_gain))
        kv_delta[:, lanes(h)] = jnp.where(first, back, dkv).astype(bf16)
        gain_grad[...] += gain_terms
    part = lax.dot_general(
        query_delta[...], w_query[...], NT, preferred_element_type=f32
    ) + lax.dot_general(kv_delta[...], w_kv[...], NT, preferred_element_type=f32)
    low[...] = part.astype(bf16)
    x = tokens[...].astype(f32)
    norm_grad[...] = jnp.sum(part * x * row_scale(x), axis=0, keepdims=True)
    if not outs:
        return
    lhs = hidden[...].T
    n = ring.n
    unit = width // (2 * n)
    q_cols = query_delta.shape[1]
    for cols, right in (
        (slice(0, q_cols), query_delta),
        (slice(q_cols, q_cols + kv_delta.shape[1]), kv_delta),
    ):
        grad = jnp.dot(lhs, right[...], preferred_element_type=f32).astype(bf16)
        all_ref[:, :unit, cols] = grad.reshape(2 * n, unit, grad.shape[1])
    grad = jnp.dot(attended[...].T, back_proj[...], preferred_element_type=f32).astype(bf16)
    all_ref[:, unit:] = grad.reshape(2 * n, -1, width)
    deal(ring, lambda at: all_ref[at], lambda ref, x: ref.__setitem__(..., x), outs)


def dot(a, b, dims):
    return lax.dot_general(a, b, ((dims[:1], dims[1:]), ((), ())), preferred_element_type=f32)


def on_device(
    tokens,
    cotangent,
    block_order,
    segment_ids,
    norm_gain,
    w_query,
    key_weight,
    value_weight,
    query_gain,
    key_gain,
    w_out,
    ffn_gain,
    w_gate,
    w_up,
    w_down,
):
    devices = lax.axis_size("ctx")
    ring = Ring(devices)
    other_ring = Ring(devices, -1)
    far = ring.n // 2
    rows, width = tokens.shape
    seq_count = segment_ids.shape[0]
    blk = rows // seq_count // 2
    tiles = 2 * seq_count
    kv_heads = key_weight.shape[1] // HEAD_SIZE
    q_cols, k_cols = w_query.shape[1], key_weight.shape[1]
    units = w_gate.shape[1]
    packed = units % 256 == 0 and width % (32 * ring.n) == 0 and w_out.shape[0] % (32 * ring.n) == 0
    pair = lax.axis_size("tp") == 2

    def line(x):
        return x.reshape(1, -1)

    inverse = ROPE_BASE ** (-np.arange(0, HEAD_SIZE, 2) / HEAD_SIZE)
    inverse = np.tile(inverse, 4)[None, :].astype(np.float32)
    starts, hidden_input, kv_raw, own_kv, w_kv, cosine, sines = whole_call(
        functools.partial(project_kv_kernel, tiles, 2 * devices - 1),
        "project_kv",
        [
            shape(seq_count, 3, dtype=jnp.int32),
            shape(rows, width, dtype=bf16),
            shape(rows, 2 * k_cols),
            shape(rows, 2 * k_cols, dtype=bf16),
            shape(width, 2 * k_cols, dtype=bf16),
            shape(rows, LANES),
            shape(rows, LANES),
        ],
        [
            block_order,
            segment_ids,
            tokens,
            line(norm_gain),
            key_weight,
            value_weight,
            line(key_gain),
            jnp.asarray(inverse),
        ],
        4 * rows * width * k_cols,
        scalars=(1, 1),
        vmem=ALL_VMEM,
    )
    gather = RingGather(ring, own_kv)
    flying = gather.send(gather.sends())
    query_raw, q_tiles = whole_call(
        functools.partial(project_q_kernel, tiles),
        "project_q",
        [shape(rows, q_cols), shape(kv_heads, tiles, 2 * blk, LANES, dtype=bf16)],
        [hidden_input, w_query, line(query_gain), cosine, sines],
        2 * rows * width * q_cols,
    )

    attention = Attention(ring, block_order, starts, blk)
    acc = attention.forward(gather.pieces[:1], q_tiles, None)
    late = gather.pieces[1]
    while True:
        *came, acc = lax.optimization_barrier((*flying, acc))
        now = gather.arrive(came)
        if gather.done():
            break
        flying = gather.send(gather.sends())
        acc = attention.forward([late, *now], q_tiles, acc)
        late = gather.pieces[-1]
    acc = attention.forward([late, *gather.pieces[-2:]], q_tiles, acc)
    kv_pieces = {
        max(abs(d) for d, _ in slots): gather.pieces[i - 1 : i + 1]
        for i, (slots, _) in enumerate(gather.pieces)
        if i % 2
    }
    attended, o, lse, attn_mine, attn_send = whole_call(
        functools.partial(mix_kernel, pair),
        "mix",
        [
            shape(rows, q_cols, dtype=bf16),
            shape(*acc.shape),
            shape(kv_heads, tiles, 8, 2 * blk),
            shape(rows // 2, width, dtype=bf16),
            shape(rows // 2, width, dtype=bf16),
        ],
        [acc, w_out],
        2 * rows * width * q_cols,
    )

    def halves_of(x):
        at = lax.axis_index("tp") if pair else 0
        return [
            lax.dynamic_slice_in_dim(x, (at + k) % 2 * (rows // 2), rows // 2, 0) for k in (0, 1)
        ]

    def from_first(xs):
        at = lax.axis_index("tp") if pair else 0
        return jnp.concatenate([jnp.where(at == k, xs[0], xs[1]) for k in (0, 1)])

    cots, toks = halves_of(cotangent), halves_of(tokens)
    if pair:
        (attn_theirs,) = from_other([attn_send])
        upstream = [dot(x, w_down, (1, 1)) for x in cots]
        attn_theirs, *upstream = lax.optimization_barrier((attn_theirs, *upstream))
        attn = total(attn_mine, attn_theirs)
    else:
        attn, attn_next = lax.psum((attn_mine, attn_send), "tp")
        upstream = [dot(x, w_down, (1, 1)) for x in cots]

    def feed(k, attn):
        return feed_forward(toks[k], attn, line(ffn_gain), upstream[k], w_gate, w_up)

    if pair:
        (attn_next,) = from_other([attn])
        fed = [feed(0, attn)]
        attn_next, *fed[0] = lax.optimization_barrier((attn_next, *fed[0]))
        (last,) = from_other([fed[0][-1]])
        fed.append(feed(1, attn_next))
        last, *fed[1] = lax.optimization_barrier((last, *fed[1]))
        (first,) = from_other([fed[1][-1]])
    else:
        fed = [feed(0, attn), feed(1, attn_next)]
        first, last = lax.psum((fed[0][-1], fed[1][-1]), "tp")
    mixed, hidden_two, hidden_ffn, back_gate, back_up, ffn_gain_grads, mine = zip(*fed)
    if not pair:
        mine = [jnp.zeros_like(x) for x in mine]
    grad_ffn_gain = ffn_gain_grads[0] + ffn_gain_grads[1]
    if packed:
        dealt_out = ffn_grads(ring, hidden_two, back_gate, back_up, hidden_ffn, cots)
        first, *dealt_out = lax.optimization_barrier((first, *dealt_out))
        dealt_out, _ = exchanged(ring, dealt_out)
        ffn_box = []
        ffn_sum = Steps(sum_steps(ring, dealt_terms(ring, dealt_out), ffn_box))
        first, last = advance([ffn_sum], first, last)
    else:

        def by_units(xs):
            return jnp.concatenate(xs, axis=1).transpose(1, 0, 2).reshape(rows, units)

        two, cot = jnp.concatenate(hidden_two), jnp.concatenate(cots)
        grad_w_gate, grad_w_up, grad_w_down = sum_over_ctx(
            ring,
            [
                dot(two, by_units(back_gate), (0, 0)).astype(bf16),
                dot(two, by_units(back_up), (0, 0)).astype(bf16),
                dot(by_units(hidden_ffn), cot, (0, 0)).astype(bf16),
            ],
        )
        ffn_sum = None

    back_mixed, back_proj, do_tiles, stats = whole_call(
        functools.partial(back_kernel, pair),
        "back",
        [
            shape(rows, width),
            shape(rows, width, dtype=bf16),
            shape(*q_tiles.shape, dtype=bf16),
            shape(*lse.shape),
        ],
        [cotangent, line(ffn_gain), w_out, o, lse, *mixed, *mine, first, last],
        2 * rows * width * q_cols,
    )
    output_swap, more = None, hidden_ffn
    dq = None
    terms = {}

    dkv_sum = Steps(sum_steps(ring, lambda d: terms[d]))
    for d in range(far, -1, -1):
        if d < far:
            chains = [ffn_sum, dkv_sum if d < far - 1 else None]
            if d == far - 2 and pair:
                output_swap = Steps(exchange_steps(output_part))
            if d in (far - 2, far - 3):
                chains.append(output_swap)
            do_tiles, dq, *more = advance(chains, do_tiles, dq, *more)
            if d == far - 1:
                (output_part,) = whole_call(
                    functools.partial(down_kernel, pair),
                    "down",
                    [shape(rows, width, dtype=bf16)],
                    [*more, w_down],
                    2 * rows * width * units,
                )
                more = [output_part]
        dq, keep, give = attention.backward(kv_pieces[d], q_tiles, do_tiles, stats, dq)
        terms[d] = [keep, ring.sibling(give)]
    placed, done = [], 0
    (dq,) = advance([None if LATE else ffn_sum, dkv_sum], dq)
    query_delta, grad_query_gain = whole_call(
        back_query_kernel,
        "back_query",
        [shape(rows, q_cols, dtype=bf16), shape(1, LANES)],
        [dq, query_raw, line(query_gain), cosine, sines],
        2 * rows * width,
    )
    if packed:
        done = len(ffn_box[0].pieces)
        placed = place_ffn(ring, ffn_box[0].pieces, width, [])
    query_delta, *placed = advance([dkv_sum], query_delta, *placed)
    own_dkv = dkv_sum.result
    wide = width // (2 * ring.n) + w_out.shape[0] // (2 * ring.n)
    one_low, grad_norm_gain, grad_key_gain, kv_delta, *cuts = whole_call(
        functools.partial(back_project_kernel, other_ring),
        "back_project",
        [
            shape(rows, width, dtype=bf16),
            shape(1, width),
            shape(1, LANES),
            shape(rows, 2 * k_cols, dtype=bf16),
        ]
        + (dealt(ring, shape(wide, width, dtype=bf16)) if packed else []),
        [
            tokens,
            hidden_input,
            query_delta,
            own_dkv,
            kv_raw,
            line(key_gain),
            cosine,
            sines,
            w_query,
            w_kv,
            attended,
            back_proj,
        ],
        4 * rows * width * (q_cols + 2 * k_cols),
        [pltpu.VMEM((2 * ring.n, wide, width), bf16)],
    )

    gains = jnp.concatenate(
        [
            grad_norm_gain[0],
            grad_ffn_gain[0],
            grad_query_gain[0, :HEAD_SIZE] + grad_query_gain[0, HEAD_SIZE:],
            grad_key_gain[0, :HEAD_SIZE],
        ]
    )
    exchanges = [("ctx", devices, k) for k in bits(devices)[2:] + bits(devices)[1::-1]]
    exchanges += [("tp", lax.axis_size("tp"), k) for k in bits(lax.axis_size("tp"))]
    gain_sum = Steps(pair_steps(gains, exchanges))
    one_swap = Steps(exchange_steps(one_low)) if pair else None
    if packed:
        qkv_box = []
        cuts, _ = exchanged(other_ring, cuts)
        qkv_sum = Steps(sum_steps(other_ring, dealt_terms(other_ring, cuts), qkv_box))
        gather = ffn_box[0]
        round_at = 0
        while qkv_sum.generator is not None:
            came = len(gather.pieces)
            chains = [qkv_sum]
            if round_at in (1, 4):
                chains.append(one_swap)
            if round_at > 5:
                chains.append(gain_sum)
            placed = advance(chains, *placed)
            if round_at % 2 == 0:
                placed = advance([ffn_sum, gain_sum if round_at < 5 else None], *placed)
            if came > done:
                placed = place_ffn(ring, gather.pieces[done:came], width, placed)
                done = came
            round_at += 1
        if done < len(gather.pieces):
            placed = place_ffn(ring, gather.pieces[done:], width, placed)
        grad_w_gate, grad_w_up, grad_w_down = placed
        grad_w_query, grad_w_key, grad_w_value, grad_w_out = place_qkv(
            other_ring, qkv_box[0].pieces, width, (q_cols, k_cols, k_cols)
        )
    else:
        grad_w_query, grad_kv, grad_w_out = sum_over_ctx(
            ring,
            [
                dot(hidden_input, query_delta, (0, 0)).astype(bf16),
                dot(hidden_input, kv_delta, (0, 0)).astype(bf16),
                dot(attended, back_proj, (0, 0)).astype(bf16),
            ],
        )
        grad_kv = grad_kv.reshape(width, kv_heads, 2, HEAD_SIZE)
        grad_w_key = grad_kv[:, :, 0].reshape(width, k_cols)
        grad_w_value = grad_kv[:, :, 1].reshape(width, k_cols)
    while gain_sum.generator is not None:
        advance([gain_sum])
    gains = gain_sum.result
    if pair:
        for swap in (output_swap, one_swap):
            while swap.generator is not None:
                advance([swap])
        output = output_part.astype(f32) + output_swap.result.astype(f32)
        back_one = one_low.astype(f32) + one_swap.result.astype(f32)
    else:
        output = lax.psum(output_part, "tp").astype(f32)
        back_one = lax.psum(one_low, "tp").astype(f32)
    output = (from_first(mixed) + output).astype(bf16)
    inputs = tokens.astype(f32)
    input_grad = back_mixed + norm_back(back_one, inputs, row_scale(inputs), norm_gain)

    return (
        output,
        input_grad,
        gains[:width],
        grad_w_query,
        grad_w_key,
        grad_w_value,
        gains[2 * width : 2 * width + HEAD_SIZE],
        gains[2 * width + HEAD_SIZE :],
        grad_w_out,
        gains[width : 2 * width],
        grad_w_gate,
        grad_w_up,
        grad_w_down,
    )


def solution(mesh):
    return jax.shard_map(
        on_device,
        mesh=mesh,
        in_specs=(
            P("ctx", None),
            P("ctx", None),
            P(),
            P(),
            P(),
            P(None, "tp"),
            P(None, "tp"),
            P(None, "tp"),
            P(),
            P(),
            P("tp", None),
            P(),
            P(None, "tp"),
            P(None, "tp"),
            P("tp", None),
        ),
        out_specs=(
            P("ctx", None),
            P("ctx", None),
            P(),
            P(None, "tp"),
            P(None, "tp"),
            P(None, "tp"),
            P(),
            P(),
            P("tp", None),
            P(),
            P(None, "tp"),
            P(None, "tp"),
            P("tp", None),
        ),
        check_vma=False,
    )
```
